32 devices in a mesh: frm: 16 (over z, y, x), sp: 2 (over core).
Axes of the slice: x: 2, y: 2, z: 4, core: 2. Of those that a mesh axis runs over, the one named last changes fastest.
Arguments:
- tokens: bfloat16 [64, 256, 1024], P('frm', 'sp'), may hold values from -6 to 6
- out_cotangent: bfloat16 [64, 256, 1024], P('frm', 'sp'), may hold values from -6 to 6
- level_embed: bfloat16 [64, 1024], P(('frm', 'sp')), may hold values from -6 to 6
- ada_weight: bfloat16 [1024, 6144], replicated, may hold values from -0.1875 to 0.1875
- ada_bias: bfloat16 [6144], replicated, may hold values from -2 to 2
- qkv_weight: bfloat16 [1024, 3072], replicated, may hold values from -0.1875 to 0.1875
- qkv_bias: bfloat16 [3072], replicated, may hold values from -2 to 2
- proj_weight: bfloat16 [1024, 1024], replicated, may hold values from -1.5 to 1.5
- proj_bias: bfloat16 [1024], replicated, may hold values from -2 to 2
- up_weight: bfloat16 [1024, 4096], replicated, may hold values from -0.1875 to 0.1875
- up_bias: bfloat16 [4096], replicated, may hold values from -2 to 2
- down_weight: bfloat16 [4096, 1024], replicated, may hold values from -0.09375 to 0.09375
- down_bias: bfloat16 [1024], replicated, may hold values from -2 to 2
- context_count: int32 [4], replicated, may hold values from 1 to 15, as said below
- frame_level: int32 [4, 16], replicated, may hold values from 0 to 63, as said below
- slot_time: int32 [64], replicated, may hold values from 0 to 15, as said below
Outputs:
- block_out: bfloat16 [64, 256, 1024], P('frm', 'sp')
- tokens_grad: bfloat16 [64, 256, 1024], P('frm', 'sp')
- ada_weight_grad: float32 [1024, 6144], P(('frm', 'sp'))
- ada_bias_grad: float32 [6144], P(('frm', 'sp'))
- qkv_weight_grad: float32 [1024, 3072], P(('frm', 'sp'))
- qkv_bias_grad: float32 [3072], P(('frm', 'sp'))
- proj_weight_grad: float32 [1024, 1024], P(('frm', 'sp'))
- proj_bias_grad: float32 [1024], P(('frm', 'sp'))
- up_weight_grad: float32 [1024, 4096], P(('frm', 'sp'))
- up_bias_grad: float32 [4096], P(('frm', 'sp'))
- down_weight_grad: float32 [4096, 1024], P(('frm', 'sp'))
- down_bias_grad: float32 [1024], P(('frm', 'sp'))
The draws below stay inside these ranges and needn't reach their ends.
Inputs may be any that keep to these rules, and one draw needn't show every extreme that they name: `context_count`: every clip has at least one context frame and at least one noisy frame. frame_level[c, t] is 0 exactly for t < context_count[c] and at least 1 otherwise. `slot_time`: slots c * 16 to (c + 1) * 16 - 1 hold the frames of clip c, each time 0 to 15 once.
All inputs are finite; a program needn't handle non-finite values.
Results may differ from the reference program's by a relative error of at most 0.014.
The reference program's roundings to bfloat16 on the way count: a program that leaves them out, or rounds other values in their place, can miss the bound.
Values may be sent and summed in bfloat16 or wider, within the bound.
No kernel may reach another device: no remote copies, remote signals or barrier semaphores. Data moves between devices by JAX's collectives and lax.ppermute only.
A program may use at most 512 MiB of HBM per device.

```python
import math
import jax
import jax.numpy as jnp
from jax import lax

D = 1024
HEADS = 16
HDIM = 64
FF = 4096
FRAMES = 16
GRID = 16
PATCH = 256
SLOTS = 64
CLIPS = 4
LEVELS = 64


def clip_layout(key):
    folded = jax.random.fold_in(key, 11)
    key_ctx, key_level, key_rank = jax.random.split(folded, 3)
    contexts = jax.random.randint(key_ctx, (CLIPS,), 1, FRAMES).astype(jnp.int32)
    contexts = contexts.at[0].set(1).at[CLIPS - 1].set(FRAMES - 1)
    time_grid = jnp.arange(FRAMES, dtype=jnp.int32)[None, :]
    levels = jax.random.randint(key_level, (CLIPS, FRAMES), 1, LEVELS).astype(jnp.int32)
    levels = jnp.where(time_grid < contexts[:, None], 0, levels)
    levels = levels.at[0, FRAMES - 1].set(LEVELS - 1)
    rank_keys = jax.random.randint(key_rank, (CLIPS, FRAMES), 0, FRAMES).astype(jnp.int32) * FRAMES + time_grid
    sort_score = levels * (FRAMES * FRAMES) + rank_keys
    placed = jnp.argsort(sort_score, axis=1, stable=True).astype(jnp.int32)
    return (contexts, levels, placed.reshape(CLIPS * FRAMES))


def draw_context_count(key, part):
    return clip_layout(key)[0]


def draw_frame_level(key, part):
    return clip_layout(key)[1]


def draw_slot_time(key, part):
    return clip_layout(key)[2]


def block_levels(own_key, extent, cuts, smallest, largest):
    def one(dim, shards_of):
        heights = jax.random.uniform(jax.random.fold_in(jax.random.fold_in(own_key, 6), dim), (shards_of,), jnp.float32, smallest / len(cuts), largest / len(cuts))
        return jnp.repeat(jnp.exp(heights), extent[dim] // shards_of).reshape((-1,) + (1,) * (len(extent) - dim - 1))

    factor_of = one(*cuts[0])
    for cut in cuts[1:]:
        factor_of = factor_of * one(*cut)
    return factor_of


def gaussian(own_key, shape, scale, reach, shards=(), kind=jnp.bfloat16):
    factor_of = block_levels(own_key, shape, shards, -0.22, 0.18) if shards else 1.0
    result = jax.random.normal(own_key, shape, jnp.float32) * scale * factor_of
    return jnp.minimum(jnp.maximum(result, -reach), reach).astype(kind)


def setup_inputs(seed: int = 0) -> dict:
    key_list = jax.random.split(jax.random.key(seed), 17)
    return {
        "tokens": gaussian(key_list[0], (SLOTS, PATCH, D), 1.0, 6.0, ((0, 16), (1, 2))),
        "out_cotangent": gaussian(key_list[1], (SLOTS, PATCH, D), 1.0, 6.0, ((0, 16), (1, 2))),
        "level_embed": gaussian(key_list[2], (LEVELS, D), 1.0, 6.0, ((0, 32),)),
        "ada_weight": gaussian(key_list[3], (D, 6 * D), D ** -0.5, 0.1875),
        "ada_bias": gaussian(key_list[4], (6 * D,), 0.3, 2.0),
        "qkv_weight": gaussian(key_list[5], (D, 3 * D), D ** -0.5, 0.1875),
        "qkv_bias": gaussian(key_list[6], (3 * D,), 0.3, 2.0),
        "proj_weight": gaussian(key_list[7], (D, D), (D // 64) ** -0.5, 1.5),
        "proj_bias": gaussian(key_list[8], (D,), 0.3, 2.0),
        "up_weight": gaussian(key_list[9], (D, FF), D ** -0.5, 0.1875),
        "up_bias": gaussian(key_list[10], (FF,), 0.3, 2.0),
        "down_weight": gaussian(key_list[11], (FF, D), FF ** -0.5, 0.09375),
        "down_bias": gaussian(key_list[12], (D,), 0.3, 2.0),
        "context_count": draw_context_count(jax.random.fold_in(key_list[16], 71), 0),
        "frame_level": draw_frame_level(jax.random.fold_in(key_list[16], 71), 0),
        "slot_time": draw_slot_time(jax.random.fold_in(key_list[16], 71), 0),
    }


@jax.custom_vjp
def low(v):
    return lax.optimization_barrier(v.astype(jnp.bfloat16)).astype(jnp.float32)

@jax.custom_vjp
def low_back(v):
    return v

def low_keep(v):
    return (low(v), None)

def low_pass(kept, grad):
    return (grad,)

def back_keep(v):
    return (v, None)

def back_low(kept, grad):
    return (low(grad),)
low.defvjp(low_keep, low_pass)
low_back.defvjp(back_keep, back_low)
norm_eps = 1e-06
masked_out = -1e+30

def product(left_op, right_op):
    return jnp.dot(left_op, right_op, precision=lax.Precision.HIGHEST)

def layer_norm(values_in):
    centre = values_in - lax.optimization_barrier(jnp.mean(values_in, axis=-1, keepdims=True))
    return centre * lax.rsqrt(lax.optimization_barrier(jnp.mean(centre * centre, axis=-1, keepdims=True)) + norm_eps)

def frequencies(span_dims):
    pair_ids = jnp.arange(span_dims // 2, dtype=jnp.float32)
    return jnp.exp(pair_ids * (-2.0 * math.log(10000.0) / span_dims))

def rotary_angles(tok_times, tok_rows, tok_cols, head_dim):
    first_span = head_dim // 4
    second_span = 3 * head_dim // 8
    return (tok_times[:, None] * frequencies(first_span)[None, :], tok_rows[:, None] * frequencies(second_span)[None, :], tok_cols[:, None] * frequencies(second_span)[None, :])

def rotate(values_in, angle_set, direction):
    pieces = []
    offset = 0
    for angle_row in angle_set:
        half_span = angle_row.shape[1]
        lead_part = values_in[..., offset:offset + half_span]
        tail_part = values_in[..., offset + half_span:offset + 2 * half_span]
        cosine = jnp.cos(angle_row)[:, None, :]
        sine_term = direction * jnp.sin(angle_row)[:, None, :]
        pieces.append(lead_part * cosine - tail_part * sine_term)
        pieces.append(tail_part * cosine + lead_part * sine_term)
        offset = offset + 2 * half_span
    return jnp.concatenate(pieces, axis=-1)

def reference(tokens, out_cotangent, level_embed, ada_weight, ada_bias, qkv_weight, qkv_bias, proj_weight, proj_bias, up_weight, up_bias, down_weight, down_bias, context_count, frame_level, slot_time):
    clip_of_slot = jnp.arange(SLOTS, dtype=jnp.int32) // FRAMES
    slot_level = frame_level[clip_of_slot, slot_time]
    clip_times = slot_time.reshape(CLIPS, FRAMES)
    patch_ids = jnp.arange(PATCH, dtype=jnp.int32)
    score_scale = 1.0 / math.sqrt(HDIM)
    tok_rows = jnp.tile(patch_ids // GRID, FRAMES).astype(jnp.float32)
    tok_cols = jnp.tile(patch_ids % GRID, FRAMES).astype(jnp.float32)
    embed_act = low(jax.nn.silu(level_embed.astype(jnp.float32)))

    def forward(inputs, ada_w, ada_b, qkv_w, qkv_b, proj_w, proj_b, up_w, up_b, down_w, down_b):
        mod_table = low_back(low(product(embed_act, ada_w) + ada_b))
        slot_mod = mod_table[slot_level].reshape(CLIPS, FRAMES, 6 * D)
        clip_inputs = inputs.reshape(CLIPS, FRAMES, PATCH, D)

        def one_clip(operands):
            clip_in, clip_mod, times_here, context_here = operands
            mod_parts = [clip_mod[:, None, part_no * D:(part_no + 1) * D] for part_no in range(6)]
            shift_one, scale_one, gate_one, shift_two, scale_two, gate_two = mod_parts
            hidden_one = low(layer_norm(clip_in) * (1.0 + scale_one) + shift_one).reshape(FRAMES * PATCH, D)
            projected = low_back(product(hidden_one, qkv_w) + qkv_b)
            tok_times = jnp.repeat(times_here, PATCH).astype(jnp.float32)
            angle_set = rotary_angles(tok_times, tok_rows, tok_cols, HDIM)
            split_shape = (FRAMES * PATCH, HEADS, HDIM)
            queries = low(rotate(projected[:, :D].reshape(split_shape), angle_set, 1.0))
            key_rows = low(rotate(projected[:, D:2 * D].reshape(split_shape), angle_set, 1.0))
            values = low(projected[:, 2 * D:].reshape(split_shape))
            time_ok = (times_here[None, :] <= times_here[:, None]) | (times_here[None, :] < context_here)
            visible = jnp.broadcast_to(time_ok[:, None, :, None], (FRAMES, PATCH, FRAMES, PATCH)).reshape(FRAMES * PATCH, FRAMES * PATCH)

            def one_head(head_ops):
                query_one, key_one, value_one = head_ops
                scores = low_back(product(query_one, key_one.T) * score_scale)
                scores = jnp.where(visible, scores, masked_out)
                probs_low = low(jax.nn.softmax(scores, axis=-1))
                return product(probs_low, value_one)
            attended = lax.map(jax.checkpoint(one_head), (queries.transpose(1, 0, 2), key_rows.transpose(1, 0, 2), values.transpose(1, 0, 2)))
            attended = low_back(low(attended.transpose(1, 0, 2).reshape(FRAMES * PATCH, D)))
            attn_proj = low_back(product(attended, proj_w) + proj_b).reshape(FRAMES, PATCH, D)
            after_attn = clip_in + gate_one * attn_proj
            hidden_two = low(layer_norm(after_attn) * (1.0 + scale_two) + shift_two).reshape(FRAMES * PATCH, D)
            pre_act = low_back(product(hidden_two, up_w) + up_b)
            activated = low(jax.nn.gelu(pre_act, approximate=True))
            branch_out = low_back(product(activated, down_w) + down_b).reshape(FRAMES, PATCH, D)
            return after_attn + gate_two * branch_out
        outputs = lax.map(jax.checkpoint(one_clip), (clip_inputs, slot_mod, clip_times, context_count))
        return outputs.reshape(SLOTS, PATCH, D)
    block_out, pullback = jax.vjp(forward, tokens.astype(jnp.float32), ada_weight.astype(jnp.float32), ada_bias.astype(jnp.float32), qkv_weight.astype(jnp.float32), qkv_bias.astype(jnp.float32), proj_weight.astype(jnp.float32), proj_bias.astype(jnp.float32), up_weight.astype(jnp.float32), up_bias.astype(jnp.float32), down_weight.astype(jnp.float32), down_bias.astype(jnp.float32))
    gradients = pullback(out_cotangent.astype(jnp.float32))
    return (block_out.astype(jnp.bfloat16), gradients[0].astype(jnp.bfloat16), gradients[1], gradients[2], gradients[3], gradients[4], gradients[5], gradients[6], gradients[7], gradients[8], gradients[9], gradients[10])
```

```python
import functools
import math

import jax
import jax.numpy as jnp
import numpy as np
from jax import lax
from jax.experimental import pallas as pl
from jax.experimental.pallas import tpu as pltpu
from jax.sharding import PartitionSpec as P

HEADS = 16
HDIM = 64
FRAMES = 16
GRID = 16
LANES = 128
MIB = 2**20

norm_eps = 1e-06
masked_out = -1e30
score_scale = 0.125

f32 = jnp.float32
bf16 = jnp.bfloat16
NN = (((1,), (0,)), ((), ()))
NT = (((1,), (1,)), ((), ()))
TN = (((0,), (0,)), ((), ()))
AXES = ("frm", "sp")
VMEM = pltpu.VMEM


def dot(left_op, right_op, dims=NN):
    return lax.dot_general(left_op, right_op, dims, preferred_element_type=f32)


def exchange(value, groups):
    return lax.all_to_all(value, AXES, 0, 0, axis_index_groups=groups)


def to_everyone(value, devices):
    return exchange(
        jnp.broadcast_to(value[None], (devices,) + value.shape), [list(range(devices))]
    )


def rotary_lanes():
    lane = np.arange(LANES) % HDIM
    start = np.where(lane < 16, 0, np.where(lane < 40, 16, 40))
    half = np.where(lane < 16, 8, 12)
    offset = lane - start
    freq = np.exp((offset % half).astype(np.float32) * np.float32(-math.log(10000.0)) / half)
    sign = np.where(offset < half, -1.0, 1.0)
    return (
        freq.astype(np.float32),
        sign.astype(np.float32),
        (lane < 16),
        (lane >= 16) & (lane < 40),
    )


def rotate_lanes(value, cosine, sine):
    lane = lax.broadcasted_iota(jnp.int32, value.shape, 1) % HDIM
    near_first = pltpu.roll(value, LANES - 8, 1)
    near_second = pltpu.roll(value, 8, 1)
    far_first = pltpu.roll(value, LANES - 12, 1)
    far_second = pltpu.roll(value, 12, 1)
    in_first = (lane < 28) | ((lane >= 40) & (lane < 52))
    far = jnp.where(in_first, far_first, far_second)
    near = jnp.where(lane < 8, near_first, near_second)
    partner = jnp.where(lane < 16, near, far)
    return value * cosine + partner * sine


def keyval_kernel(tok_ref, shift_ref, scale_ref, wk_ref, wv_ref, bk_ref, bv_ref,
                  cos_ref, sin_ref, hid_ref, kv_ref):
    frames, patches, _ = tok_ref.shape
    cols = wk_ref.shape[1]

    @pl.when(pl.program_id(0) == 0)
    def _():
        for f in range(frames):
            x = tok_ref[f].astype(f32)
            centre = x - jnp.mean(x, axis=1, keepdims=True)
            inv = lax.rsqrt(jnp.mean(centre * centre, axis=1, keepdims=True) + norm_eps)
            hid = centre * inv * (1.0 + scale_ref[f : f + 1, :]) + shift_ref[f : f + 1, :]
            hid_ref[f * patches : (f + 1) * patches, :] = hid.astype(bf16)

    keys = dot(hid_ref[...], wk_ref[...]) + bk_ref[...]
    vals = (dot(hid_ref[...], wv_ref[...]) + bv_ref[...]).astype(bf16)
    for p in range(cols // LANES):
        lanes = slice(p * LANES, (p + 1) * LANES)
        kv_ref[p, 0] = rotate_lanes(keys[:, lanes], cos_ref[...], sin_ref[...]).astype(bf16)
        kv_ref[p, 1] = vals[:, lanes]


def query_kernel(hid_ref, wq_ref, bq_ref, cos_ref, sin_ref, q_ref):
    query = dot(hid_ref[...], wq_ref[...]) + bq_ref[...]
    for p in range(wq_ref.shape[1] // LANES):
        lanes = slice(p * LANES, (p + 1) * LANES)
        q_ref[p] = rotate_lanes(query[:, lanes], cos_ref[...], sin_ref[...]).astype(bf16)


def whole(shape):
    return pl.BlockSpec(shape, lambda *_: (0,) * len(shape))


def project(tokens, shift_one, scale_one, qkv_weight, qkv_bias, cosine, sine, cols=512):
    frames, patches, width = tokens.shape
    rows = frames * patches
    pairs = width // LANES
    steps, some = width // cols, cols // LANES

    def column(part):
        return lambda c: (0, part * steps + c)

    hidden, keyvals = pl.pallas_call(
        keyval_kernel,
        out_shape=[
            jax.ShapeDtypeStruct((rows, width), bf16),
            jax.ShapeDtypeStruct((pairs, 2, rows, LANES), bf16),
        ],
        grid=(steps,),
        in_specs=[
            whole(tokens.shape),
            whole(shift_one.shape),
            whole(scale_one.shape),
            pl.BlockSpec((width, cols), column(1)),
            pl.BlockSpec((width, cols), column(2)),
            pl.BlockSpec((1, cols), column(1)),
            pl.BlockSpec((1, cols), column(2)),
            whole((rows, LANES)),
            whole((rows, LANES)),
        ],
        out_specs=[
            whole((rows, width)),
            pl.BlockSpec((some, 2, rows, LANES), lambda c: (c, 0, 0, 0)),
        ],
        compiler_params=pltpu.CompilerParams(vmem_limit_bytes=40 * MIB),
        cost_estimate=pl.CostEstimate(
            flops=4 * rows * width * width, bytes_accessed=8 * MIB, transcendentals=0
        ),
        name="project_keyval",
    )(tokens, shift_one, scale_one, qkv_weight, qkv_weight, qkv_bias, qkv_bias, cosine, sine)
    queries = pl.pallas_call(
        query_kernel,
        out_shape=jax.ShapeDtypeStruct((pairs, rows, LANES), bf16),
        grid=(steps,),
        in_specs=[
            whole((rows, width)),
            pl.BlockSpec((width, cols), column(0)),
            pl.BlockSpec((1, cols), column(0)),
            whole((rows, LANES)),
            whole((rows, LANES)),
        ],
        out_specs=pl.BlockSpec((some, rows, LANES), lambda c: (c, 0, 0)),
        compiler_params=pltpu.CompilerParams(vmem_limit_bytes=40 * MIB),
        cost_estimate=pl.CostEstimate(
            flops=2 * rows * width * width, bytes_accessed=4 * MIB, transcendentals=0
        ),
        name="project_query",
    )(hidden, qkv_weight, qkv_bias, cosine, sine)
    return hidden, keyvals, queries


def key_extra(first_frame, rows, patches):
    row = lax.broadcasted_iota(jnp.int32, (rows, LANES), 0)
    lane = lax.broadcasted_iota(jnp.int32, (rows, LANES), 1)
    hit = (lane == first_frame + row // patches) | ((lane >= FRAMES) & (lane < FRAMES + 3))
    return jnp.where(hit, 1.0, 0.0).astype(bf16)


def split_three(column):
    high = column.astype(bf16).astype(f32)
    rest = column - high
    mid = rest.astype(bf16).astype(f32)
    return high, mid, rest - mid


def attend_kernel(part, rows_part, patches, joined, chunk, q_ref, vis_ref, kv_ref, o_ref, ext_ref,
                  key_all, val_all):
    blocks, rows, _ = q_ref.shape
    frames, frames_part = rows // patches, rows_part // patches
    for b in range(blocks):
        here = slice(b * rows, (b + 1) * rows)
        key_all[here, :LANES] = kv_ref[b, 0]
        key_all[here, LANES:] = key_extra((b // 2) * frames, rows, patches)
        val_all[here, :LANES] = kv_ref[b, 1]
        val_all[here, LANES:] = jnp.full((rows, LANES), 1.0, bf16)
    tile = joined * rows_part
    lane = lax.broadcasted_iota(jnp.int32, (tile, LANES), 1)
    mine_rows = slice(part * rows_part, (part + 1) * rows_part)

    def step(t, carry):
        query = jnp.concatenate([q_ref[t * joined + i, mine_rows, :] for i in range(joined)], axis=0)
        query = query * score_scale
        seen = jnp.concatenate(
            [
                jnp.broadcast_to(
                    vis_ref[pl.ds((t * joined + i) * frames + part * frames_part + f, 1), :],
                    (patches, LANES),
                )
                for i in range(joined)
                for f in range(frames_part)
            ],
            axis=0,
        )
        outs, ext_heads = [], []
        for h in range(2):
            mine = jnp.where((lane >= HDIM) == (h == 1), query, jnp.zeros_like(query))
            query_ext = jnp.concatenate([mine.astype(bf16), seen.astype(bf16)], axis=1)
            top = None
            for c in range(blocks * rows // chunk):
                keys_here = slice(c * chunk, (c + 1) * chunk)
                scores = dot(query_ext, key_all[keys_here, :], NT)
                chunk_top = jnp.max(scores, axis=1, keepdims=True)
                new_top = chunk_top if top is None else jnp.maximum(top, chunk_top)
                some = dot(jnp.exp(scores - new_top).astype(bf16), val_all[keys_here, :])
                total = some if top is None else total * jnp.exp(top - new_top) + some
                top = new_top
            weight_sum = total[:, LANES : LANES + 1]
            outs.append(total[:, :LANES] / weight_sum)
            high, mid, low = split_three(-(top + jnp.log(weight_sum)))
            ext = jnp.where(lane == FRAMES, high, seen)
            ext = jnp.where(lane == FRAMES + 1, mid, ext)
            ext_heads.append(jnp.where(lane == FRAMES + 2, low, ext).astype(bf16))
        out = jnp.where(lane < HDIM, outs[0], outs[1]).astype(bf16)
        for i in range(joined):
            here = slice(i * rows_part, (i + 1) * rows_part)
            o_ref[t * joined + i] = out[here, :]
            for h in range(2):
                ext_ref[h, t * joined + i] = ext_heads[h][here, :]
        return carry

    lax.fori_loop(0, blocks // joined, step, 0)


def attend(queries, visible, keyvals, patches, part, parts, tile=512, chunk=1024):
    blocks, rows, _ = queries.shape
    rows_part = rows // parts
    keys = blocks * rows
    return pl.pallas_call(
        functools.partial(attend_kernel, part, rows_part, patches, tile // rows_part, chunk),
        out_shape=[
            jax.ShapeDtypeStruct((blocks, rows_part, LANES), bf16),
            jax.ShapeDtypeStruct((2, blocks, rows_part, LANES), bf16),
        ],
        in_specs=[pl.BlockSpec(memory_space=VMEM)] * 3,
        out_specs=[pl.BlockSpec(memory_space=VMEM)] * 2,
        scratch_shapes=[VMEM((keys, 2 * LANES), bf16), VMEM((keys, 2 * LANES), bf16)],
        compiler_params=pltpu.CompilerParams(vmem_limit_bytes=48 * MIB),
        cost_estimate=pl.CostEstimate(
            flops=8 * blocks * rows_part * keys * 2 * LANES,
            bytes_accessed=4 * MIB,
            transcendentals=0,
        ),
        name="attend",
    )(queries, visible, keyvals)


def attend_back_kernel(parts, part, patches, chunk, carried, last, *refs):
    at = 0

    def take(count):
        nonlocal at
        found = refs[at : at + count]
        at += count
        return found

    (q_ref, kv_ref, do_ref) = take(3)
    ext_refs, o_refs = take(parts), take(parts)
    ctime_ref, stime_ref, cpatch_ref, spatch_ref = take(4)
    carry_ref = take(1)[0] if carried else None
    (dkv_ref, dq_ref) = take(2)
    q_all, do_all, key_all, val_all, key_turned, dq_turned = refs[at:]
    blocks, rows, _ = q_ref.shape
    rows_part = rows // parts
    frames, frames_part = rows // patches, rows_part // patches
    queries = blocks * rows
    lane = lax.broadcasted_iota(jnp.int32, (rows_part, LANES), 1)
    for b in range(blocks):
        for i in range(parts):
            here = slice(b * rows + i * rows_part, b * rows + (i + 1) * rows_part)
            there = slice(i * rows_part, (i + 1) * rows_part)
            query = q_ref[b, there, :] * score_scale
            grad = do_ref[b, there, :]
            mixed = grad.astype(f32) * o_refs[i][b].astype(f32)
            for h in range(2):
                mine = (lane >= HDIM) == (h == 1)
                q_all[h, here, :LANES] = jnp.where(mine, query, jnp.zeros_like(query)).astype(bf16)
                q_all[h, here, LANES:] = ext_refs[i][h, b]
                do_all[h, here, :LANES] = jnp.where(mine, grad, jnp.zeros_like(grad))
                row_mix = jnp.sum(jnp.where(mine, mixed, 0.0), axis=1, keepdims=True)
                high, mid, low = split_three(-row_mix)
                ext = jnp.where(lane == 1, mid, jnp.where(lane == 2, low, 0.0))
                do_all[h, here, LANES:] = jnp.where(lane == 0, high, ext).astype(bf16)
    if carried:
        dq_turned[...] = carry_ref[...]
    else:
        dq_turned[...] = jnp.zeros_like(dq_turned)
    key_rows = slice(part * rows_part, (part + 1) * rows_part)
    for b in range(blocks):
        here = slice(b * rows_part, (b + 1) * rows_part)
        keys = kv_ref[b, 0, key_rows, :]
        key_all[here, :LANES] = keys
        key_all[here, LANES:] = key_extra((b // 2) * frames + part * frames_part, rows_part, patches)
        val_all[here, :LANES] = kv_ref[b, 1, key_rows, :]
        val_all[here, LANES:] = jnp.where(lane < 3, 1.0, 0.0).astype(bf16)
        key_turned[b] = keys.astype(f32).T.astype(bf16)

    def back(value, row, half):
        cosine = ctime_ref[pl.ds(row, 1), :] + cpatch_ref[half]
        sine = stime_ref[pl.ds(row, 1), :] + spatch_ref[half]
        return rotate_lanes(value, cosine, -sine).astype(bf16)

    def step(t, carry):
        here = pl.ds(pl.multiple_of(t * rows_part, rows_part), rows_part)
        key_tile = key_all[here, :]
        val_tile = val_all[here, :]
        turned = key_turned[t]
        dk = jnp.zeros((rows_part, LANES), f32)
        dv = jnp.zeros((rows_part, LANES), f32)
        for c in range(queries // chunk):
            span = slice(c * chunk, (c + 1) * chunk)
            for h in range(2):
                query = q_all[h, span, :]
                grad = do_all[h, span, :]
                probs = jnp.exp(dot(key_tile, query, NT))
                dv = dv + dot(probs.astype(bf16), grad[:, :LANES])
                grad_scores = (probs * dot(val_tile, grad, NT)).astype(bf16)
                dk = dk + dot(grad_scores, query[:, :LANES])
                head = slice(HDIM * h, HDIM * (h + 1))
                dq_turned[head, span] += dot(turned[head, :], grad_scores)
        for f in range(frames_part):
            rows_here = slice(f * patches, (f + 1) * patches)
            row = t * frames + part * frames_part + f
            dkv_ref[t, 0, rows_here, :] = back(dk[rows_here, :], row, t % 2)
        dkv_ref[t, 1] = dv.astype(bf16)
        return carry

    lax.fori_loop(0, blocks, step, 0)

    if last:
        for b in range(blocks):
            for f in range(frames):
                there = slice(b * rows + f * patches, b * rows + (f + 1) * patches)
                turned_back = back(dq_turned[:, there].T * score_scale, b * frames + f, b % 2)
                dq_ref[b, f * patches : (f + 1) * patches, :] = turned_back
    else:
        dq_ref[...] = dq_turned[...]


def attend_back(queries, keyvals, grads, exts, outs, rotary, carry, part, last, patches, chunk=1024):
    parts = len(exts)
    blocks, rows, _ = queries.shape
    rows_part = rows // parts
    total = blocks * rows
    carried = carry is not None
    operands = [queries, keyvals, grads, *exts, *outs, *rotary] + ([carry] if carried else [])
    dq_shape = jax.ShapeDtypeStruct((LANES, total), f32)
    if last:
        dq_shape = jax.ShapeDtypeStruct((blocks, rows, LANES), bf16)
    return pl.pallas_call(
        functools.partial(attend_back_kernel, parts, part, patches, chunk, carried, last),
        out_shape=[jax.ShapeDtypeStruct((blocks, 2, rows_part, LANES), bf16), dq_shape],
        in_specs=[pl.BlockSpec(memory_space=VMEM)] * len(operands),
        out_specs=[pl.BlockSpec(memory_space=VMEM)] * 2,
        scratch_shapes=[
            VMEM((2, total, 2 * LANES), bf16),
            VMEM((2, total, 2 * LANES), bf16),
            VMEM((blocks * rows_part, 2 * LANES), bf16),
            VMEM((blocks * rows_part, 2 * LANES), bf16),
            VMEM((blocks, LANES, rows_part), bf16),
            VMEM((LANES, total), f32),
        ],
        compiler_params=pltpu.CompilerParams(vmem_limit_bytes=56 * MIB),
        cost_estimate=pl.CostEstimate(
            flops=20 * total * blocks * rows_part * 2 * LANES,
            bytes_accessed=8 * MIB,
            transcendentals=0,
        ),
        name="attend_back",
    )(*operands)


def feed_kernel(hid_ref, grad_ref, up_ref, bias_ref, down_ref,
                branch_ref, back_ref, biasgrad_ref, joined_ref,
                hid_turned, up_slots, down_slots, up_sems, down_sems):
    step, steps = pl.program_id(0), pl.num_programs(0)
    width, cols = up_ref.shape
    devices, _, share, _ = joined_ref.shape
    quarters = down_slots.shape[2]
    dests = down_slots.shape[1]
    up_parts = width // cols
    slot = step % 2

    def copies(at):
        across = pl.ds(pl.multiple_of((at % up_parts) * cols, cols), cols)
        up_copy = pltpu.make_async_copy(
            up_slots.at[at % 2], joined_ref.at[:, at // up_parts, :, across], up_sems.at[at % 2]
        )
        down_copy = pltpu.make_async_copy(
            down_slots.at[at % 2],
            joined_ref.at[pl.ds(at * dests, dests), quarters : 2 * quarters],
            down_sems.at[at % 2],
        )
        return up_copy, down_copy

    @pl.when(step == 0)
    def _():
        hid_turned[...] = hid_ref[...].T

    pre = dot(hid_ref[...], up_ref[...]) + bias_ref[...]
    square = pre * pre
    bend = jnp.tanh(0.7978845608 * (pre + 0.044715 * pre * square))
    act = (0.5 * pre * (1.0 + bend)).astype(bf16)
    slope = 0.5 * (1.0 + bend) + 0.5 * pre * (1.0 - bend * bend) * (
        0.7978845608 * (1.0 + 3.0 * 0.044715 * square)
    )
    branch = dot(act, down_ref[...])
    pre_grad = (slope * dot(grad_ref[...], down_ref[...], NT)).astype(bf16)
    biasgrad_ref[...] = jnp.sum(pre_grad.astype(f32), axis=0, keepdims=True)
    back = dot(pre_grad, up_ref[...], NT)

    @pl.when(step == 0)
    def _():
        branch_ref[...] = branch
        back_ref[...] = back

    @pl.when(step > 0)
    def _():
        branch_ref[...] += branch
        back_ref[...] += back

    @pl.when(step >= 2)
    def _():
        for copy in copies(step - 2):
            copy.wait()

    up_grad = dot(hid_turned[...], pre_grad).astype(bf16)
    up_slots[slot] = up_grad.reshape(devices, share, cols)
    down_grad = dot(act.T, grad_ref[...]).astype(bf16)
    down_slots[slot] = down_grad.reshape(dests, quarters, share, width)
    for copy in copies(step):
        copy.start()

    @pl.when(step == steps - 1)
    def _():
        for at in (steps - 2, steps - 1):
            for copy in copies(at):
                copy.wait()


def feed_forward(hidden, grad, up_weight, up_bias, down_weight, devices, cols=512):
    rows, width = hidden.shape
    inner = up_weight.shape[1]
    share, quarters = width // devices, inner // width
    dests = cols * devices // inner
    return pl.pallas_call(
        feed_kernel,
        out_shape=[
            jax.ShapeDtypeStruct((rows, width), f32),
            jax.ShapeDtypeStruct((rows, width), f32),
            jax.ShapeDtypeStruct((1, inner), f32),
            jax.ShapeDtypeStruct((devices, 2 * quarters + 1, share, width), bf16),
        ],
        grid=(inner // cols,),
        in_specs=[
            whole((rows, width)),
            whole((rows, width)),
            pl.BlockSpec((width, cols), lambda c: (0, c)),
            pl.BlockSpec((1, cols), lambda c: (0, c)),
            pl.BlockSpec((cols, width), lambda c: (c, 0)),
        ],
        out_specs=[
            whole((rows, width)),
            whole((rows, width)),
            pl.BlockSpec((1, cols), lambda c: (0, c)),
            pl.BlockSpec(memory_space=pl.ANY),
        ],
        scratch_shapes=[
            VMEM((width, rows), bf16),
            VMEM((2, devices, share, cols), bf16),
            VMEM((2, dests, quarters, share, width), bf16),
            pltpu.SemaphoreType.DMA((2,)),
            pltpu.SemaphoreType.DMA((2,)),
        ],
        compiler_params=pltpu.CompilerParams(vmem_limit_bytes=56 * MIB),
        cost_estimate=pl.CostEstimate(
            flops=12 * rows * width * inner, bytes_accessed=36 * MIB, transcendentals=0
        ),
        name="feed_forward",
    )(hidden, grad, up_weight, up_bias, down_weight)


def proj_grad_kernel(attn_ref, grad_ref, _, joined_ref):
    devices, _, share, width = joined_ref.shape
    joined_ref[...] = dot(attn_ref[...].T, grad_ref[...]).astype(bf16).reshape(
        devices, 1, share, width
    )


def proj_weight_grad(attn_low, grad_proj, joined, steps=2):
    rows, width = attn_low.shape
    devices, entries, share, _ = joined.shape
    return pl.pallas_call(
        proj_grad_kernel,
        out_shape=jax.ShapeDtypeStruct(joined.shape, joined.dtype),
        grid=(steps,),
        in_specs=[
            pl.BlockSpec((rows, width // steps), lambda c: (0, c)),
            whole((rows, width)),
            pl.BlockSpec(memory_space=pl.ANY),
        ],
        out_specs=pl.BlockSpec(
            (devices // steps, 1, share, width), lambda c: (c, entries - 1, 0, 0)
        ),
        input_output_aliases={2: 0},
        compiler_params=pltpu.CompilerParams(vmem_limit_bytes=40 * MIB),
        cost_estimate=pl.CostEstimate(
            flops=2 * rows * width * width, bytes_accessed=4 * MIB, transcendentals=0
        ),
        name="proj_weight_grad",
    )(attn_low, grad_proj, joined)


def layer_norm(values_in):
    centre = values_in - jnp.mean(values_in, axis=-1, keepdims=True)
    inv_scale = lax.rsqrt(jnp.mean(centre * centre, axis=-1, keepdims=True) + norm_eps)
    return (centre * inv_scale, inv_scale)


def norm_back(grad_in, normed, inv_scale):
    mean_grad = jnp.mean(grad_in, axis=-1, keepdims=True)
    mean_mix = jnp.mean(grad_in * normed, axis=-1, keepdims=True)
    return inv_scale * (grad_in - mean_grad - normed * mean_mix)


def body(
    tokens,
    out_cotangent,
    level_embed,
    ada_weight,
    ada_bias,
    qkv_weight,
    qkv_bias,
    proj_weight,
    proj_bias,
    up_weight,
    up_bias,
    down_weight,
    down_bias,
    context_count,
    frame_level,
    slot_time,
):
    frames, patches, width = tokens.shape
    rows = frames * patches
    inner = up_weight.shape[1]
    frm_count, sp_count = lax.axis_size("frm"), lax.axis_size("sp")
    devices = frm_count * sp_count
    group = FRAMES // frames * sp_count
    clips = devices // group
    frm, sp = lax.axis_index("frm"), lax.axis_index("sp")
    me = frm * sp_count + sp
    clip = me // group
    clip_groups = [list(range(first, first + group)) for first in range(0, devices, group)]
    everyone = [list(range(devices))]
    halves = 2
    share = width // devices
    per_dest = inner // devices

    levels_here = level_embed.shape[0]
    embed_all = to_everyone(level_embed, devices).reshape(devices * levels_here, width)

    clip_times = lax.dynamic_slice_in_dim(slot_time, clip * FRAMES, FRAMES)
    clip_levels = lax.dynamic_index_in_dim(frame_level, clip, 0, keepdims=False)
    context = lax.dynamic_index_in_dim(context_count, clip, 0, keepdims=False)
    seen = (clip_times[None, :] <= clip_times[:, None]) | (clip_times[None, :] < context)
    visible = jnp.pad(
        jnp.where(seen, 0.0, masked_out).astype(f32), ((0, 0), (0, LANES - FRAMES))
    )

    def by_blocks(table):
        table = table.reshape(FRAMES // frames, 1, frames, LANES)
        return jnp.broadcast_to(table, (FRAMES // frames, sp_count, frames, LANES)).reshape(
            group * frames, LANES
        )

    visible = by_blocks(visible)
    freq, sign, time_lane, row_lane = rotary_lanes()
    angle_time = clip_times.astype(f32)[:, None] * freq[None, :]
    ctime = by_blocks(jnp.where(time_lane[None, :], jnp.cos(angle_time), 0.0))
    stime = by_blocks(jnp.where(time_lane[None, :], jnp.sin(angle_time) * sign[None, :], 0.0))
    patch_ids = jnp.arange(sp_count * patches, dtype=jnp.int32).reshape(sp_count, patches)
    place = jnp.where(
        row_lane[None, None, :], (patch_ids // GRID)[..., None], (patch_ids % GRID)[..., None]
    )
    angle_patch = place.astype(f32) * freq[None, None, :]
    cpatch = jnp.where(time_lane, 0.0, jnp.cos(angle_patch))
    spatch = jnp.where(time_lane, 0.0, jnp.sin(angle_patch) * sign)
    rotary = [ctime, stime, cpatch, spatch]

    def my_table(time_part, patch_part):
        mine = lax.dynamic_slice_in_dim(time_part, me % group * frames, frames)
        half = lax.dynamic_index_in_dim(patch_part, sp, 0, keepdims=False)
        return (mine[:, None, :] + half[None]).reshape(rows, LANES)

    cosine, sine = my_table(ctime, cpatch), my_table(stime, spatch)

    my_times = lax.dynamic_slice_in_dim(slot_time, frm * frames, frames)
    my_levels = jnp.take(clip_levels, my_times)
    embed_act = jax.nn.silu(embed_all.astype(f32)).astype(bf16)
    level_ids = jnp.arange(devices * levels_here, dtype=jnp.int32)
    pick = (my_levels[:, None] == level_ids[None, :]).astype(bf16)
    my_embed = dot(pick, embed_act).astype(bf16)
    frame_mod = dot(my_embed, ada_weight) + ada_bias.astype(f32)
    frame_mod = lax.reduce_precision(frame_mod, 8, 7)
    mod_parts = [frame_mod[:, i * width : (i + 1) * width] for i in range(6)]
    shift_one, scale_one = mod_parts[0], mod_parts[1]
    gate_one, shift_two, scale_two, gate_two = [part[:, None, :] for part in mod_parts[2:]]

    hidden_one, keyval_parts, query_parts = project(
        tokens, shift_one, scale_one, qkv_weight, qkv_bias.astype(f32)[None, :], cosine, sine
    )
    keyvals = exchange(keyval_parts, clip_groups)
    queries = exchange(query_parts, clip_groups)
    outs, exts, attended = [], [], []
    for part in range(halves):
        out, ext = attend(queries, visible, keyvals, patches, part, halves)
        outs.append(out)
        exts.append(ext)
        attended.append(exchange(out, clip_groups))

    hidden_own, _ = lax.optimization_barrier((hidden_one, queries))
    hidden_clip = lax.all_gather(hidden_own, AXES, axis_index_groups=clip_groups).reshape(
        group * rows, width
    )

    attn_low = jnp.concatenate(
        [part.transpose(1, 0, 2).reshape(rows // halves, width) for part in attended], axis=0
    )
    attn_proj = (dot(attn_low, proj_weight) + proj_bias.astype(f32)).reshape(
        frames, patches, width
    )
    inputs = tokens.astype(f32)
    after_attn = inputs + gate_one * attn_proj
    normed_two, rscale_two = layer_norm(after_attn)
    hidden_two = (
        (normed_two * (1.0 + scale_two) + shift_two).astype(bf16).reshape(rows, width)
    )
    grad_out = out_cotangent.astype(f32)
    grad_branch = (gate_two * grad_out).astype(bf16).reshape(rows, width)
    branch, grad_hidden_two, up_b_grad, joined = feed_forward(
        hidden_two, grad_branch, up_weight, up_bias.astype(f32)[None, :], down_weight, devices
    )

    grad_hidden_two = grad_hidden_two.reshape(frames, patches, width)
    grad_after = grad_out + norm_back(grad_hidden_two * (1.0 + scale_two), normed_two, rscale_two)
    grad_proj = (gate_one * grad_after).astype(bf16).reshape(rows, width)
    grad_parts = dot(grad_proj, proj_weight, NT).astype(bf16)
    grad_parts = grad_parts.reshape(rows, group, LANES).transpose(1, 0, 2)
    grads = exchange(grad_parts, clip_groups)

    joined = proj_weight_grad(attn_low, grad_proj, joined)
    summed = lax.psum_scatter(joined, AXES, scatter_dimension=0, tiled=True)[0].astype(f32)
    quarters = inner // width
    up_w_out = jnp.concatenate([summed[i] for i in range(quarters)], axis=1)
    down_w_out = summed[quarters : 2 * quarters].reshape(per_dest, width)
    proj_w_out = summed[2 * quarters]

    branch_out = (branch + down_bias.astype(f32)).reshape(frames, patches, width)
    block_out = (after_attn + gate_two * branch_out).astype(bf16)
    early_sums = jnp.concatenate(
        [
            jnp.sum(grad_after * attn_proj, axis=1),
            jnp.sum(grad_hidden_two, axis=1),
            jnp.sum(grad_hidden_two * normed_two, axis=1),
            jnp.sum(grad_out * branch_out, axis=1),
        ],
        axis=1,
    )

    def share_out(slot_sums, biases):
        high = biases.astype(bf16)
        low = (biases - high.astype(f32)).astype(bf16)
        sums = slot_sums.astype(bf16).reshape(1, -1)
        sums = jnp.broadcast_to(sums, (devices, sums.shape[1]))
        got = exchange(jnp.concatenate([sums, high, low], axis=1), everyone).astype(f32)
        count = slot_sums.size
        extra = jnp.sum(got[:, count:], axis=0)
        size = biases.shape[1]
        return (
            got[:, :count].reshape(devices * frames, -1).astype(bf16),
            extra[:size] + extra[size:],
        )

    early_biases = jnp.concatenate(
        [
            up_b_grad.reshape(devices, per_dest),
            jnp.sum(grad_proj.astype(f32), axis=0).reshape(devices, share),
            jnp.sum(grad_branch.astype(f32), axis=0).reshape(devices, share),
        ],
        axis=1,
    )
    early_slots, early_bias_out = share_out(early_sums, early_biases)
    up_b_out = early_bias_out[:per_dest]
    proj_b_out = early_bias_out[per_dest : per_dest + share]
    down_b_out = early_bias_out[per_dest + share :]
    slot_ids = (jnp.arange(devices * frames, dtype=jnp.int32) // (sp_count * frames)) * frames
    slot_ids = slot_ids + jnp.arange(devices * frames, dtype=jnp.int32) % frames
    slot_levels = frame_level[slot_ids // FRAMES, slot_time[slot_ids]]
    member_of = (level_ids[:, None] == slot_levels[None, :]).astype(bf16)
    my_columns = lax.dynamic_slice_in_dim(embed_act, me * share, share, axis=1)

    def level_out(slots):
        level_grad = dot(member_of, slots).astype(bf16)
        return dot(my_columns, level_grad, TN), jnp.sum(level_grad.astype(f32), axis=0)

    early_w, early_b = level_out(early_slots)

    carry = None
    own_keyvals, grad_keyvals = [], []
    for part in range(halves):
        some, carry = attend_back(
            queries, keyvals, grads, exts, outs, rotary, carry, part, part == halves - 1, patches
        )
        grad_keyvals.append(some)
        own_keyvals.append(exchange(some, clip_groups))
    grad_queries = carry
    own_queries = exchange(grad_queries, clip_groups)

    grad_keyval = jnp.concatenate(grad_keyvals, axis=2)
    grad_heads = jnp.concatenate(
        [grad_queries, grad_keyval[:, 0], grad_keyval[:, 1]], axis=2
    ).reshape(group * rows, 3 * LANES)
    qkv_part = dot(hidden_clip, grad_heads, TN).astype(bf16)
    qkv_got = exchange(qkv_part.reshape(devices, share, 3 * LANES), everyone)
    qkv_w_out = (
        jnp.sum(qkv_got.reshape(clips, group, share, 3 * LANES).astype(f32), axis=0)
        .reshape(group, share, 3, LANES)
        .transpose(1, 2, 0, 3)
        .reshape(share, 3 * width)
    )

    def to_rows(value):
        return value.transpose(1, 0, 2).reshape(value.shape[1], width)

    grad_rows = jnp.concatenate(
        [
            to_rows(own_queries),
            jnp.concatenate([to_rows(part[:, 0]) for part in own_keyvals], axis=0),
            jnp.concatenate([to_rows(part[:, 1]) for part in own_keyvals], axis=0),
        ],
        axis=1,
    )
    grad_hidden_one = dot(grad_rows, qkv_weight, NT).reshape(frames, patches, width)
    normed_one, rscale_one = layer_norm(inputs)
    late_sums = jnp.concatenate(
        [jnp.sum(grad_hidden_one, axis=1), jnp.sum(grad_hidden_one * normed_one, axis=1)], axis=1
    )
    tokens_grad = (
        grad_after
        + norm_back(grad_hidden_one * (1.0 + scale_one[:, None, :]), normed_one, rscale_one)
    ).astype(bf16)
    late_slots, qkv_b_out = share_out(
        late_sums, jnp.sum(grad_rows.astype(f32), axis=0).reshape(devices, 3 * share)
    )
    late_w, late_b = level_out(late_slots)
    ada_w_out = jnp.concatenate([late_w, early_w], axis=1)
    ada_b_all = jnp.concatenate([late_b, early_b])
    ada_share = ada_b_all.shape[0] // devices
    ada_b_out = lax.dynamic_slice_in_dim(ada_b_all, me * ada_share, ada_share)
    return (
        block_out,
        tokens_grad,
        ada_w_out,
        ada_b_out,
        qkv_w_out,
        qkv_b_out,
        proj_w_out,
        proj_b_out,
        up_w_out,
        up_b_out,
        down_w_out,
        down_b_out,
    )


def solution(mesh):
    tokens_spec = P("frm", "sp", None)
    rows_spec = P(AXES, None)
    vector_spec = P(AXES)
    return jax.shard_map(
        body,
        mesh=mesh,
        in_specs=(tokens_spec, tokens_spec, rows_spec) + (P(),) * 13,
        out_specs=(tokens_spec, tokens_spec) + (rows_spec, vector_spec) * 5,
        check_vma=False,
    )
```

```python
import functools
import math

import jax
import jax.numpy as jnp
import numpy as np
from jax import lax
from jax.experimental import pallas as pl
from jax.experimental.pallas import tpu as pltpu
from jax.sharding import PartitionSpec as P

HEADS = 16
HDIM = 64
FRAMES = 16
GRID = 16
LANES = 128
MIB = 2**20

norm_eps = 1e-06
masked_out = -1e30
score_scale = 0.125

f32 = jnp.float32
bf16 = jnp.bfloat16
NN = (((1,), (0,)), ((), ()))
NT = (((1,), (1,)), ((), ()))
TN = (((0,), (0,)), ((), ()))
AXES = ("frm", "sp")
VMEM = pltpu.VMEM


def dot(left_op, right_op, dims=NN):
    return lax.dot_general(left_op, right_op, dims, preferred_element_type=f32)


def exchange(value, groups):
    return lax.all_to_all(value, AXES, 0, 0, axis_index_groups=groups)


def to_everyone(value, devices):
    return exchange(
        jnp.broadcast_to(value[None], (devices,) + value.shape), [list(range(devices))]
    )


def rotary_lanes():
    lane = np.arange(LANES) % HDIM
    start = np.where(lane < 16, 0, np.where(lane < 40, 16, 40))
    half = np.where(lane < 16, 8, 12)
    offset = lane - start
    freq = np.exp((offset % half).astype(np.float32) * np.float32(-math.log(10000.0)) / half)
    sign = np.where(offset < half, -1.0, 1.0)
    return (
        freq.astype(np.float32),
        sign.astype(np.float32),
        (lane < 16),
        (lane >= 16) & (lane < 40),
    )


def rotate_lanes(value, cosine, sine):
    lane = lax.broadcasted_iota(jnp.int32, value.shape, 1) % HDIM
    near_first = pltpu.roll(value, LANES - 8, 1)
    near_second = pltpu.roll(value, 8, 1)
    far_first = pltpu.roll(value, LANES - 12, 1)
    far_second = pltpu.roll(value, 12, 1)
    in_first = (lane < 28) | ((lane >= 40) & (lane < 52))
    far = jnp.where(in_first, far_first, far_second)
    near = jnp.where(lane < 8, near_first, near_second)
    partner = jnp.where(lane < 16, near, far)
    return value * cosine + partner * sine


def project_kernel(tok_ref, shift_ref, scale_ref, wq_ref, wk_ref, wv_ref, bq_ref, bk_ref, bv_ref,
                   cos_ref, sin_ref, turned_ref, out_ref, hid_all):
    frames, patches, _ = tok_ref.shape

    @pl.when(pl.program_id(0) == 0)
    def _():
        for f in range(frames):
            here = slice(f * patches, (f + 1) * patches)
            x = tok_ref[f].astype(f32)
            centre = x - jnp.mean(x, axis=1, keepdims=True)
            inv = lax.rsqrt(jnp.mean(centre * centre, axis=1, keepdims=True) + norm_eps)
            hid = centre * inv * (1.0 + scale_ref[f : f + 1, :]) + shift_ref[f : f + 1, :]
            hid = hid.astype(bf16)
            hid_all[here, :] = hid
            turned_ref[:, here] = hid.T

    hid = hid_all[...]
    query = dot(hid, wq_ref[...]) + bq_ref[...]
    keys = dot(hid, wk_ref[...]) + bk_ref[...]
    vals = (dot(hid, wv_ref[...]) + bv_ref[...]).astype(bf16)
    for p in range(wq_ref.shape[1] // LANES):
        lanes = slice(p * LANES, (p + 1) * LANES)
        out_ref[p, 0] = rotate_lanes(query[:, lanes], cos_ref[...], sin_ref[...]).astype(bf16)
        out_ref[p, 1] = rotate_lanes(keys[:, lanes], cos_ref[...], sin_ref[...]).astype(bf16)
        out_ref[p, 2] = vals[:, lanes]


def whole(shape):
    return pl.BlockSpec(shape, lambda *_: (0,) * len(shape))


def project(tokens, shift_one, scale_one, qkv_weight, qkv_bias, cosine, sine, cols=256):
    frames, patches, width = tokens.shape
    rows = frames * patches
    pairs = width // LANES
    steps, some = width // cols, cols // LANES

    def column(part):
        return lambda c: (0, part * steps + c)

    return pl.pallas_call(
        project_kernel,
        out_shape=[
            jax.ShapeDtypeStruct((width, rows), bf16),
            jax.ShapeDtypeStruct((pairs, 3, rows, LANES), bf16),
        ],
        grid=(steps,),
        in_specs=[whole(tokens.shape), whole(shift_one.shape), whole(scale_one.shape)]
        + [pl.BlockSpec((width, cols), column(part)) for part in range(3)]
        + [pl.BlockSpec((1, cols), column(part)) for part in range(3)]
        + [whole((rows, LANES)), whole((rows, LANES))],
        out_specs=[
            whole((width, rows)),
            pl.BlockSpec((some, 3, rows, LANES), lambda c: (c, 0, 0, 0)),
        ],
        scratch_shapes=[VMEM((rows, width), bf16)],
        compiler_params=pltpu.CompilerParams(vmem_limit_bytes=40 * MIB),
        cost_estimate=pl.CostEstimate(
            flops=6 * rows * width * width, bytes_accessed=10 * MIB, transcendentals=0
        ),
        name="project",
    )(tokens, shift_one, scale_one, *[qkv_weight] * 3, *[qkv_bias] * 3, cosine, sine)


def key_extra(first_frame, rows, patches):
    row = lax.broadcasted_iota(jnp.int32, (rows, LANES), 0)
    lane = lax.broadcasted_iota(jnp.int32, (rows, LANES), 1)
    hit = (lane == first_frame + row // patches) | ((lane >= FRAMES) & (lane < FRAMES + 3))
    return jnp.where(hit, 1.0, 0.0).astype(bf16)


def split_three(column):
    high = column.astype(bf16).astype(f32)
    rest = column - high
    mid = rest.astype(bf16).astype(f32)
    return high, mid, rest - mid


def attend_kernel(part, rows_part, patches, joined, chunk, qkv_ref, vis_ref, o_ref, ext_ref,
                  key_all, val_all):
    blocks, _, rows, _ = qkv_ref.shape
    frames, frames_part = rows // patches, rows_part // patches
    for b in range(blocks):
        here = slice(b * rows, (b + 1) * rows)
        key_all[here, :LANES] = qkv_ref[b, 1]
        key_all[here, LANES:] = key_extra((b // 2) * frames, rows, patches)
        val_all[here, :LANES] = qkv_ref[b, 2]
        val_all[here, LANES:] = jnp.full((rows, LANES), 1.0, bf16)
    tile = joined * rows_part
    lane = lax.broadcasted_iota(jnp.int32, (tile, LANES), 1)
    mine_rows = slice(part * rows_part, (part + 1) * rows_part)

    def step(t, carry):
        query = jnp.concatenate(
            [qkv_ref[t * joined + i, 0, mine_rows, :] for i in range(joined)], axis=0
        )
        query = query * score_scale
        seen = jnp.concatenate(
            [
                jnp.broadcast_to(
                    vis_ref[pl.ds((t * joined + i) * frames + part * frames_part + f, 1), :],
                    (patches, LANES),
                )
                for i in range(joined)
                for f in range(frames_part)
            ],
            axis=0,
        )
        outs, ext_heads = [], []
        for h in range(2):
            mine = jnp.where((lane >= HDIM) == (h == 1), query, jnp.zeros_like(query))
            query_ext = jnp.concatenate([mine.astype(bf16), seen.astype(bf16)], axis=1)
            top = None
            for c in range(blocks * rows // chunk):
                keys_here = slice(c * chunk, (c + 1) * chunk)
                scores = dot(query_ext, key_all[keys_here, :], NT)
                chunk_top = jnp.max(scores, axis=1, keepdims=True)
                new_top = chunk_top if top is None else jnp.maximum(top, chunk_top)
                some = dot(jnp.exp(scores - new_top).astype(bf16), val_all[keys_here, :])
                total = some if top is None else total * jnp.exp(top - new_top) + some
                top = new_top
            weight_sum = total[:, LANES : LANES + 1]
            outs.append(total[:, :LANES] / weight_sum)
            high, mid, low = split_three(-(top + jnp.log(weight_sum)))
            ext = jnp.where(lane == FRAMES, high, seen)
            ext = jnp.where(lane == FRAMES + 1, mid, ext)
            ext_heads.append(jnp.where(lane == FRAMES + 2, low, ext).astype(bf16))
        out = jnp.where(lane < HDIM, outs[0], outs[1]).astype(bf16)
        for i in range(joined):
            here = slice(i * rows_part, (i + 1) * rows_part)
            o_ref[t * joined + i] = out[here, :]
            for h in range(2):
                ext_ref[h, t * joined + i] = ext_heads[h][here, :]
        return carry

    lax.fori_loop(0, blocks // joined, step, 0)


def attend(heads, visible, patches, part, parts, tile=512, chunk=1024):
    blocks, _, rows, _ = heads.shape
    rows_part = rows // parts
    keys = blocks * rows
    return pl.pallas_call(
        functools.partial(attend_kernel, part, rows_part, patches, tile // rows_part, chunk),
        out_shape=[
            jax.ShapeDtypeStruct((blocks, rows_part, LANES), bf16),
            jax.ShapeDtypeStruct((2, blocks, rows_part, LANES), bf16),
        ],
        in_specs=[pl.BlockSpec(memory_space=VMEM)] * 2,
        out_specs=[pl.BlockSpec(memory_space=VMEM)] * 2,
        scratch_shapes=[VMEM((keys, 2 * LANES), bf16), VMEM((keys, 2 * LANES), bf16)],
        compiler_params=pltpu.CompilerParams(vmem_limit_bytes=48 * MIB),
        cost_estimate=pl.CostEstimate(
            flops=8 * blocks * rows_part * keys * 2 * LANES,
            bytes_accessed=4 * MIB,
            transcendentals=0,
        ),
        name="attend",
    )(heads, visible)


def attend_back_kernel(parts, part, patches, chunk, carried, last, *refs):
    at = 0

    def take(count):
        nonlocal at
        found = refs[at : at + count]
        at += count
        return found

    (qkv_ref, do_ref) = take(2)
    ext_refs, o_refs = take(parts), take(parts)
    ctime_ref, stime_ref, cpatch_ref, spatch_ref = take(4)
    carry_ref = take(1)[0] if carried else None
    if last:
        (grads_ref,) = take(1)
    else:
        grads_ref, carry_out = take(2)
    q_all, do_all, key_all, val_all, key_turned, dq_turned = refs[at:]
    blocks, _, rows, _ = qkv_ref.shape
    rows_part = rows // parts
    frames, frames_part = rows // patches, rows_part // patches
    queries = blocks * rows
    lane = lax.broadcasted_iota(jnp.int32, (rows_part, LANES), 1)
    for b in range(blocks):
        for i in range(parts):
            here = slice(b * rows + i * rows_part, b * rows + (i + 1) * rows_part)
            there = slice(i * rows_part, (i + 1) * rows_part)
            query = qkv_ref[b, 0, there, :] * score_scale
            grad = do_ref[b, there, :]
            mixed = grad.astype(f32) * o_refs[i][b].astype(f32)
            for h in range(2):
                mine = (lane >= HDIM) == (h == 1)
                q_all[h, here, :LANES] = jnp.where(mine, query, jnp.zeros_like(query)).astype(bf16)
                q_all[h, here, LANES:] = ext_refs[i][h, b]
                do_all[h, here, :LANES] = jnp.where(mine, grad, jnp.zeros_like(grad))
                row_mix = jnp.sum(jnp.where(mine, mixed, 0.0), axis=1, keepdims=True)
                high, mid, low = split_three(-row_mix)
                ext = jnp.where(lane == 1, mid, jnp.where(lane == 2, low, 0.0))
                do_all[h, here, LANES:] = jnp.where(lane == 0, high, ext).astype(bf16)
    if carried:
        dq_turned[...] = carry_ref[...]
    else:
        dq_turned[...] = jnp.zeros_like(dq_turned)
    key_rows = slice(part * rows_part, (part + 1) * rows_part)
    for b in range(blocks):
        here = slice(b * rows_part, (b + 1) * rows_part)
        keys = qkv_ref[b, 1, key_rows, :]
        key_all[here, :LANES] = keys
        key_all[here, LANES:] = key_extra((b // 2) * frames + part * frames_part, rows_part, patches)
        val_all[here, :LANES] = qkv_ref[b, 2, key_rows, :]
        val_all[here, LANES:] = jnp.where(lane < 3, 1.0, 0.0).astype(bf16)
        key_turned[b] = keys.astype(f32).T.astype(bf16)

    first = rows if last else 0

    def back(value, row, half):
        cosine = ctime_ref[pl.ds(row, 1), :] + cpatch_ref[half]
        sine = stime_ref[pl.ds(row, 1), :] + spatch_ref[half]
        return rotate_lanes(value, cosine, -sine).astype(bf16)

    def step(t, carry):
        here = pl.ds(pl.multiple_of(t * rows_part, rows_part), rows_part)
        key_tile = key_all[here, :]
        val_tile = val_all[here, :]
        turned = key_turned[t]
        dk = jnp.zeros((rows_part, LANES), f32)
        dv = jnp.zeros((rows_part, LANES), f32)
        for c in range(queries // chunk):
            span = slice(c * chunk, (c + 1) * chunk)
            for h in range(2):
                query = q_all[h, span, :]
                grad = do_all[h, span, :]
                probs = jnp.exp(dot(key_tile, query, NT))
                dv = dv + dot(probs.astype(bf16), grad[:, :LANES])
                grad_scores = (probs * dot(val_tile, grad, NT)).astype(bf16)
                dk = dk + dot(grad_scores, query[:, :LANES])
                head = slice(HDIM * h, HDIM * (h + 1))
                dq_turned[head, span] += dot(turned[head, :], grad_scores)
        for f in range(frames_part):
            rows_here = slice(f * patches, (f + 1) * patches)
            row = t * frames + part * frames_part + f
            keys_here = slice(first + f * patches, first + (f + 1) * patches)
            grads_ref[t, keys_here, :] = back(dk[rows_here, :], row, t % 2)
        grads_ref[t, first + rows_part : first + 2 * rows_part, :] = dv.astype(bf16)
        return carry

    lax.fori_loop(0, blocks, step, 0)

    if last:
        for b in range(blocks):
            for f in range(frames):
                there = slice(b * rows + f * patches, b * rows + (f + 1) * patches)
                turned_back = back(dq_turned[:, there].T * score_scale, b * frames + f, b % 2)
                grads_ref[b, f * patches : (f + 1) * patches, :] = turned_back
    else:
        carry_out[...] = dq_turned[...]


def attend_back(heads, grads, exts, outs, rotary, carry, part, last, patches, chunk=1024):
    parts = len(exts)
    blocks, _, rows, _ = heads.shape
    rows_part = rows // parts
    total = blocks * rows
    carried = carry is not None
    operands = [heads, grads, *exts, *outs, *rotary] + ([carry] if carried else [])
    kept = 2 * rows_part + (rows if last else 0)
    out_shape = [jax.ShapeDtypeStruct((blocks, kept, LANES), bf16)]
    if not last:
        out_shape.append(jax.ShapeDtypeStruct((LANES, total), f32))
    return pl.pallas_call(
        functools.partial(attend_back_kernel, parts, part, patches, chunk, carried, last),
        out_shape=out_shape,
        in_specs=[pl.BlockSpec(memory_space=VMEM)] * len(operands),
        out_specs=[pl.BlockSpec(memory_space=VMEM)] * len(out_shape),
        scratch_shapes=[
            VMEM((2, total, 2 * LANES), bf16),
            VMEM((2, total, 2 * LANES), bf16),
            VMEM((blocks * rows_part, 2 * LANES), bf16),
            VMEM((blocks * rows_part, 2 * LANES), bf16),
            VMEM((blocks, LANES, rows_part), bf16),
            VMEM((LANES, total), f32),
        ],
        compiler_params=pltpu.CompilerParams(vmem_limit_bytes=56 * MIB),
        cost_estimate=pl.CostEstimate(
            flops=20 * total * blocks * rows_part * 2 * LANES,
            bytes_accessed=8 * MIB,
            transcendentals=0,
        ),
        name="attend_back",
    )(*operands)


def feed_kernel(hid_ref, grad_ref, up_ref, bias_ref, down_ref,
                branch_ref, back_ref, biasgrad_ref, joined_ref,
                hid_turned, up_slots, down_slots, up_sems, down_sems):
    step, steps = pl.program_id(0), pl.num_programs(0)
    width, cols = up_ref.shape
    devices, _, share, _ = joined_ref.shape
    quarters = down_slots.shape[2]
    dests = down_slots.shape[1]
    up_parts = width // cols
    slot = step % 2

    def copies(at):
        across = pl.ds(pl.multiple_of((at % up_parts) * cols, cols), cols)
        up_copy = pltpu.make_async_copy(
            up_slots.at[at % 2], joined_ref.at[:, at // up_parts, :, across], up_sems.at[at % 2]
        )
        down_copy = pltpu.make_async_copy(
            down_slots.at[at % 2],
            joined_ref.at[pl.ds(at * dests, dests), quarters : 2 * quarters],
            down_sems.at[at % 2],
        )
        return up_copy, down_copy

    @pl.when(step == 0)
    def _():
        hid_turned[...] = hid_ref[...].T

    pre = dot(hid_ref[...], up_ref[...]) + bias_ref[...]
    square = pre * pre
    bend = jnp.tanh(0.7978845608 * (pre + 0.044715 * pre * square))
    act = (0.5 * pre * (1.0 + bend)).astype(bf16)
    slope = 0.5 * (1.0 + bend) + 0.5 * pre * (1.0 - bend * bend) * (
        0.7978845608 * (1.0 + 3.0 * 0.044715 * square)
    )
    branch = dot(act, down_ref[...])
    pre_grad = (slope * dot(grad_ref[...], down_ref[...], NT)).astype(bf16)
    biasgrad_ref[...] = jnp.sum(pre_grad.astype(f32), axis=0, keepdims=True)
    back = dot(pre_grad, up_ref[...], NT)

    @pl.when(step == 0)
    def _():
        branch_ref[...] = branch
        back_ref[...] = back

    @pl.when(step > 0)
    def _():
        branch_ref[...] += branch
        back_ref[...] += back

    @pl.when(step >= 2)
    def _():
        for copy in copies(step - 2):
            copy.wait()

    up_grad = dot(hid_turned[...], pre_grad).astype(bf16)
    up_slots[slot] = up_grad.reshape(devices, share, cols)
    down_grad = dot(act.T, grad_ref[...]).astype(bf16)
    down_slots[slot] = down_grad.reshape(dests, quarters, share, width)
    for copy in copies(step):
        copy.start()

    @pl.when(step == steps - 1)
    def _():
        for at in (steps - 2, steps - 1):
            for copy in copies(at):
                copy.wait()


def feed_forward(hidden, grad, up_weight, up_bias, down_weight, devices, cols=512):
    rows, width = hidden.shape
    inner = up_weight.shape[1]
    share, quarters = width // devices, inner // width
    dests = cols * devices // inner
    return pl.pallas_call(
        feed_kernel,
        out_shape=[
            jax.ShapeDtypeStruct((rows, width), f32),
            jax.ShapeDtypeStruct((rows, width), f32),
            jax.ShapeDtypeStruct((1, inner), f32),
            jax.ShapeDtypeStruct((devices, 2 * quarters + 1, share, width), bf16),
        ],
        grid=(inner // cols,),
        in_specs=[
            whole((rows, width)),
            whole((rows, width)),
            pl.BlockSpec((width, cols), lambda c: (0, c)),
            pl.BlockSpec((1, cols), lambda c: (0, c)),
            pl.BlockSpec((cols, width), lambda c: (c, 0)),
        ],
        out_specs=[
            whole((rows, width)),
            whole((rows, width)),
            pl.BlockSpec((1, cols), lambda c: (0, c)),
            pl.BlockSpec(memory_space=pl.ANY),
        ],
        scratch_shapes=[
            VMEM((width, rows), bf16),
            VMEM((2, devices, share, cols), bf16),
            VMEM((2, dests, quarters, share, width), bf16),
            pltpu.SemaphoreType.DMA((2,)),
            pltpu.SemaphoreType.DMA((2,)),
        ],
        compiler_params=pltpu.CompilerParams(vmem_limit_bytes=56 * MIB),
        cost_estimate=pl.CostEstimate(
            flops=12 * rows * width * inner, bytes_accessed=36 * MIB, transcendentals=0
        ),
        name="feed_forward",
    )(hidden, grad, up_weight, up_bias, down_weight)


def proj_grad_kernel(attn_ref, grad_ref, _, joined_ref):
    devices, _, share, width = joined_ref.shape
    joined_ref[...] = dot(attn_ref[...].T, grad_ref[...]).astype(bf16).reshape(
        devices, 1, share, width
    )


def proj_weight_grad(attn_low, grad_proj, joined, steps=2):
    rows, width = attn_low.shape
    devices, entries, share, _ = joined.shape
    return pl.pallas_call(
        proj_grad_kernel,
        out_shape=jax.ShapeDtypeStruct(joined.shape, joined.dtype),
        grid=(steps,),
        in_specs=[
            pl.BlockSpec((rows, width // steps), lambda c: (0, c)),
            whole((rows, width)),
            pl.BlockSpec(memory_space=pl.ANY),
        ],
        out_specs=pl.BlockSpec(
            (devices // steps, 1, share, width), lambda c: (c, entries - 1, 0, 0)
        ),
        input_output_aliases={2: 0},
        compiler_params=pltpu.CompilerParams(vmem_limit_bytes=40 * MIB),
        cost_estimate=pl.CostEstimate(
            flops=2 * rows * width * width, bytes_accessed=4 * MIB, transcendentals=0
        ),
        name="proj_weight_grad",
    )(attn_low, grad_proj, joined)


def merge_kernel(*refs):
    parts = len(refs) - 13
    att_refs = refs[:parts]
    (weight_ref, bias_ref, tok_ref, cot_ref, gate_one_ref, shift_ref, scale_ref, gate_two_ref,
     low_ref, proj_ref, after_ref, hid_ref, grad_ref) = refs[parts:]
    frames, patches, width = tok_ref.shape
    pairs, rows_part, _ = att_refs[0].shape
    for i, att_ref in enumerate(att_refs):
        low = jnp.concatenate([att_ref[p] for p in range(pairs)], axis=1)
        there = slice(i * rows_part, (i + 1) * rows_part)
        low_ref[there, :] = low
        proj = dot(low, weight_ref[...]) + bias_ref[...]
        proj_ref[there, :] = proj
        for j in range(rows_part // patches):
            f = i * (rows_part // patches) + j
            here = slice(f * patches, (f + 1) * patches)
            row = slice(f, f + 1)
            after = tok_ref[f].astype(f32) + gate_one_ref[row, :] * proj[
                j * patches : (j + 1) * patches, :
            ]
            after_ref[here, :] = after
            centre = after - jnp.mean(after, axis=1, keepdims=True)
            inv = lax.rsqrt(jnp.mean(centre * centre, axis=1, keepdims=True) + norm_eps)
            hid = centre * inv * (1.0 + scale_ref[row, :]) + shift_ref[row, :]
            hid_ref[here, :] = hid.astype(bf16)
            grad_ref[here, :] = (gate_two_ref[row, :] * cot_ref[f].astype(f32)).astype(bf16)


def merge_heads(attended, proj_weight, proj_bias, tokens, cotangent, mods):
    frames, patches, width = tokens.shape
    rows = frames * patches
    operands = [*attended, proj_weight, proj_bias, tokens, cotangent, *mods]
    return pl.pallas_call(
        merge_kernel,
        out_shape=[
            jax.ShapeDtypeStruct((rows, width), bf16),
            jax.ShapeDtypeStruct((rows, width), f32),
            jax.ShapeDtypeStruct((rows, width), f32),
            jax.ShapeDtypeStruct((rows, width), bf16),
            jax.ShapeDtypeStruct((rows, width), bf16),
        ],
        in_specs=[pl.BlockSpec(memory_space=VMEM)] * len(operands),
        out_specs=[pl.BlockSpec(memory_space=VMEM)] * 5,
        compiler_params=pltpu.CompilerParams(vmem_limit_bytes=48 * MIB),
        cost_estimate=pl.CostEstimate(
            flops=2 * rows * width * width, bytes_accessed=16 * MIB, transcendentals=0
        ),
        name="merge_heads",
    )(*operands)


def unmerge_kernel(branch_ref, back_ref, after_ref, proj_ref, cot_ref, gate_one_ref, scale_ref,
                   gate_two_ref, weight_ref, bias_ref,
                   out_ref, grad_ref, gproj_ref, parts_ref, sums_ref, biases_ref):
    frames, patches, width = cot_ref.shape
    pairs = parts_ref.shape[0]
    proj_sum = jnp.zeros((1, width), f32)
    down_sum = jnp.zeros((1, width), f32)

    def column_sum(value):
        return jnp.sum(value, axis=0, keepdims=True)

    for f in range(frames):
        here = slice(f * patches, (f + 1) * patches)
        row = slice(f, f + 1)
        cot = cot_ref[f].astype(f32)
        after = after_ref[here, :]
        branch = branch_ref[here, :] + bias_ref[...]
        out_ref[f] = (after + gate_two_ref[row, :] * branch).astype(bf16)
        sums_ref[3 * frames + f : 3 * frames + f + 1, :] = column_sum(cot * branch)
        down_sum += column_sum((gate_two_ref[row, :] * cot).astype(bf16).astype(f32))
        centre = after - jnp.mean(after, axis=1, keepdims=True)
        inv = lax.rsqrt(jnp.mean(centre * centre, axis=1, keepdims=True) + norm_eps)
        normed = centre * inv
        back = back_ref[here, :]
        sums_ref[frames + f : frames + f + 1, :] = column_sum(back)
        sums_ref[2 * frames + f : 2 * frames + f + 1, :] = column_sum(back * normed)
        scaled = back * (1.0 + scale_ref[row, :])
        mean_grad = jnp.mean(scaled, axis=1, keepdims=True)
        mean_mix = jnp.mean(scaled * normed, axis=1, keepdims=True)
        grad = cot + inv * (scaled - mean_grad - normed * mean_mix)
        grad_ref[here, :] = grad
        sums_ref[f : f + 1, :] = column_sum(grad * proj_ref[here, :])
        gproj = (gate_one_ref[row, :] * grad).astype(bf16)
        gproj_ref[here, :] = gproj
        proj_sum += column_sum(gproj.astype(f32))
    biases_ref[0:1, :] = proj_sum
    biases_ref[1:2, :] = down_sum
    step = 2 * patches
    for i in range(frames * patches // step):
        here = slice(i * step, (i + 1) * step)
        part = dot(gproj_ref[here, :], weight_ref[...], NT).astype(bf16)
        for p in range(pairs):
            parts_ref[p, here, :] = part[:, p * LANES : (p + 1) * LANES]


def unmerge_heads(branch, back, after, proj, cotangent, gate_one, scale_two, gate_two,
                  proj_weight, down_bias):
    frames, patches, width = cotangent.shape
    rows = frames * patches
    operands = [branch, back, after, proj, cotangent, gate_one, scale_two, gate_two, proj_weight,
                down_bias]
    return pl.pallas_call(
        unmerge_kernel,
        out_shape=[
            jax.ShapeDtypeStruct((frames, patches, width), bf16),
            jax.ShapeDtypeStruct((rows, width), f32),
            jax.ShapeDtypeStruct((rows, width), bf16),
            jax.ShapeDtypeStruct((width // LANES, rows, LANES), bf16),
            jax.ShapeDtypeStruct((4 * frames, width), f32),
            jax.ShapeDtypeStruct((2, width), f32),
        ],
        in_specs=[pl.BlockSpec(memory_space=VMEM)] * len(operands),
        out_specs=[pl.BlockSpec(memory_space=VMEM)] * 6,
        compiler_params=pltpu.CompilerParams(vmem_limit_bytes=56 * MIB),
        cost_estimate=pl.CostEstimate(
            flops=2 * rows * width * width, bytes_accessed=20 * MIB, transcendentals=0
        ),
        name="unmerge_heads",
    )(*operands)


def heads_grad_kernel(hid_ref, first_ref, last_ref, out_ref, total):
    rows = hid_ref.shape[2]
    rows_part = first_ref.shape[1] // 2
    grad = jnp.concatenate(
        [
            last_ref[0, :rows, :],
            jnp.concatenate(
                [first_ref[0, :rows_part, :], last_ref[0, rows : rows + rows_part, :]], axis=0
            ),
            jnp.concatenate([first_ref[0, rows_part:, :], last_ref[0, rows + rows_part :, :]], axis=0),
        ],
        axis=1,
    )
    some = dot(hid_ref[0], grad)

    @pl.when(pl.program_id(0) == 0)
    def _():
        total[...] = some

    @pl.when(pl.program_id(0) > 0)
    def _():
        total[...] += some

    @pl.when(pl.program_id(0) == pl.num_programs(0) - 1)
    def _():
        out_ref[...] = total[...].astype(bf16)


def heads_grad(hidden_clip, first, last):
    blocks, width, rows = hidden_clip.shape
    return pl.pallas_call(
        heads_grad_kernel,
        out_shape=jax.ShapeDtypeStruct((width, 3 * LANES), bf16),
        grid=(blocks,),
        in_specs=[
            pl.BlockSpec((1, width, rows), lambda b: (b, 0, 0)),
            pl.BlockSpec((1,) + first.shape[1:], lambda b: (b, 0, 0)),
            pl.BlockSpec((1,) + last.shape[1:], lambda b: (b, 0, 0)),
        ],
        out_specs=whole((width, 3 * LANES)),
        scratch_shapes=[VMEM((width, 3 * LANES), f32)],
        compiler_params=pltpu.CompilerParams(vmem_limit_bytes=40 * MIB),
        cost_estimate=pl.CostEstimate(
            flops=6 * blocks * rows * width * LANES, bytes_accessed=12 * MIB, transcendentals=0
        ),
        name="heads_grad",
    )(hidden_clip, first, last)


def finish_kernel(first_ref, last_ref, wq_ref, wk_ref, wv_ref, tok_ref, scale_ref, after_ref,
                  out_ref, sums_ref, bq_ref, bk_ref, bv_ref, total):
    frames, patches, width = tok_ref.shape
    rows = frames * patches
    rows_part = first_ref.shape[1] // 2
    step = pl.program_id(0)
    query, keys, vals = [], [], []
    for p in range(first_ref.shape[0]):
        query.append(last_ref[p, :rows, :])
        keys.append(
            jnp.concatenate(
                [first_ref[p, :rows_part, :], last_ref[p, rows : rows + rows_part, :]], axis=0
            )
        )
        vals.append(
            jnp.concatenate([first_ref[p, rows_part:, :], last_ref[p, rows + rows_part :, :]], axis=0)
        )
    some = None
    for grads, weight_ref, bias_ref in (
        (query, wq_ref, bq_ref), (keys, wk_ref, bk_ref), (vals, wv_ref, bv_ref)
    ):
        grads = jnp.concatenate(grads, axis=1)
        bias_ref[...] = jnp.sum(grads.astype(f32), axis=0, keepdims=True)
        term = dot(grads, weight_ref[...], NT)
        some = term if some is None else some + term

    @pl.when(step == 0)
    def _():
        total[...] = some

    @pl.when(step > 0)
    def _():
        total[...] += some

    @pl.when(step == pl.num_programs(0) - 1)
    def _():
        for f in range(frames):
            here = slice(f * patches, (f + 1) * patches)
            x = tok_ref[f].astype(f32)
            centre = x - jnp.mean(x, axis=1, keepdims=True)
            inv = lax.rsqrt(jnp.mean(centre * centre, axis=1, keepdims=True) + norm_eps)
            normed = centre * inv
            back = total[here, :]
            sums_ref[f : f + 1, :] = jnp.sum(back, axis=0, keepdims=True)
            sums_ref[frames + f : frames + f + 1, :] = jnp.sum(back * normed, axis=0, keepdims=True)
            scaled = back * (1.0 + scale_ref[f : f + 1, :])
            mean_grad = jnp.mean(scaled, axis=1, keepdims=True)
            mean_mix = jnp.mean(scaled * normed, axis=1, keepdims=True)
            grad = after_ref[here, :] + inv * (scaled - mean_grad - normed * mean_mix)
            out_ref[f] = grad.astype(bf16)


def finish(first, last, qkv_weight, tokens, scale_one, grad_after, cols=256):
    frames, patches, width = tokens.shape
    rows = frames * patches
    steps, some = width // cols, cols // LANES

    def column(part):
        return lambda c: (0, part * steps + c)

    return pl.pallas_call(
        finish_kernel,
        out_shape=[
            jax.ShapeDtypeStruct((frames, patches, width), bf16),
            jax.ShapeDtypeStruct((2 * frames, width), f32),
        ]
        + [jax.ShapeDtypeStruct((1, width), f32)] * 3,
        grid=(steps,),
        in_specs=[
            pl.BlockSpec((some,) + first.shape[1:], lambda c: (c, 0, 0)),
            pl.BlockSpec((some,) + last.shape[1:], lambda c: (c, 0, 0)),
        ]
        + [pl.BlockSpec((width, cols), column(part)) for part in range(3)]
        + [whole(tokens.shape), whole(scale_one.shape), whole((rows, width))],
        out_specs=[whole((frames, patches, width)), whole((2 * frames, width))]
        + [pl.BlockSpec((1, cols), lambda c: (0, c))] * 3,
        scratch_shapes=[VMEM((rows, width), f32)],
        compiler_params=pltpu.CompilerParams(vmem_limit_bytes=48 * MIB),
        cost_estimate=pl.CostEstimate(
            flops=6 * rows * width * width, bytes_accessed=16 * MIB, transcendentals=0
        ),
        name="finish",
    )(first, last, *[qkv_weight] * 3, tokens, scale_one, grad_after)


def lay_rows_kernel(group, got_ref, out_ref):
    clips = got_ref.shape[0] // group
    width = out_ref.shape[1] // 3
    for p in range(group):
        total = got_ref[p].astype(f32)
        for c in range(1, clips):
            total = total + got_ref[c * group + p].astype(f32)
        for part in range(3):
            at = part * width + p * LANES
            out_ref[:, at : at + LANES] = total[:, part * LANES : (part + 1) * LANES]


def lay_rows(got, group):
    share, triple = got.shape[1:]
    return pl.pallas_call(
        functools.partial(lay_rows_kernel, group),
        out_shape=jax.ShapeDtypeStruct((share, group * triple), f32),
        in_specs=[pl.BlockSpec(memory_space=VMEM)],
        out_specs=pl.BlockSpec(memory_space=VMEM),
        name="lay_rows",
    )(got)


def body(
    tokens,
    out_cotangent,
    level_embed,
    ada_weight,
    ada_bias,
    qkv_weight,
    qkv_bias,
    proj_weight,
    proj_bias,
    up_weight,
    up_bias,
    down_weight,
    down_bias,
    context_count,
    frame_level,
    slot_time,
):
    frames, patches, width = tokens.shape
    rows = frames * patches
    inner = up_weight.shape[1]
    frm_count, sp_count = lax.axis_size("frm"), lax.axis_size("sp")
    devices = frm_count * sp_count
    group = FRAMES // frames * sp_count
    clips = devices // group
    frm, sp = lax.axis_index("frm"), lax.axis_index("sp")
    me = frm * sp_count + sp
    clip = me // group
    clip_groups = [list(range(first, first + group)) for first in range(0, devices, group)]
    everyone = [list(range(devices))]
    halves = 2
    share = width // devices
    per_dest = inner // devices

    levels_here = level_embed.shape[0]
    embed_all = to_everyone(level_embed, devices).reshape(devices * levels_here, width)

    clip_times = lax.dynamic_slice_in_dim(slot_time, clip * FRAMES, FRAMES)
    clip_levels = lax.dynamic_index_in_dim(frame_level, clip, 0, keepdims=False)
    context = lax.dynamic_index_in_dim(context_count, clip, 0, keepdims=False)
    seen = (clip_times[None, :] <= clip_times[:, None]) | (clip_times[None, :] < context)
    visible = jnp.pad(
        jnp.where(seen, 0.0, masked_out).astype(f32), ((0, 0), (0, LANES - FRAMES))
    )

    def by_blocks(table):
        table = table.reshape(FRAMES // frames, 1, frames, LANES)
        return jnp.broadcast_to(table, (FRAMES // frames, sp_count, frames, LANES)).reshape(
            group * frames, LANES
        )

    visible = by_blocks(visible)
    freq, sign, time_lane, row_lane = rotary_lanes()
    angle_time = clip_times.astype(f32)[:, None] * freq[None, :]
    ctime = by_blocks(jnp.where(time_lane[None, :], jnp.cos(angle_time), 0.0))
    stime = by_blocks(jnp.where(time_lane[None, :], jnp.sin(angle_time) * sign[None, :], 0.0))
    patch_ids = jnp.arange(sp_count * patches, dtype=jnp.int32).reshape(sp_count, patches)
    place = jnp.where(
        row_lane[None, None, :], (patch_ids // GRID)[..., None], (patch_ids % GRID)[..., None]
    )
    angle_patch = place.astype(f32) * freq[None, None, :]
    cpatch = jnp.where(time_lane, 0.0, jnp.cos(angle_patch))
    spatch = jnp.where(time_lane, 0.0, jnp.sin(angle_patch) * sign)
    rotary = [ctime, stime, cpatch, spatch]

    def my_table(time_part, patch_part):
        mine = lax.dynamic_slice_in_dim(time_part, me % group * frames, frames)
        half = lax.dynamic_index_in_dim(patch_part, sp, 0, keepdims=False)
        return (mine[:, None, :] + half[None]).reshape(rows, LANES)

    cosine, sine = my_table(ctime, cpatch), my_table(stime, spatch)

    my_times = lax.dynamic_slice_in_dim(slot_time, frm * frames, frames)
    my_levels = jnp.take(clip_levels, my_times)
    embed_act = jax.nn.silu(embed_all.astype(f32)).astype(bf16)
    level_ids = jnp.arange(devices * levels_here, dtype=jnp.int32)
    pick = (my_levels[:, None] == level_ids[None, :]).astype(bf16)
    my_embed = dot(pick, embed_act).astype(bf16)
    frame_mod = dot(my_embed, ada_weight) + ada_bias.astype(f32)
    frame_mod = lax.reduce_precision(frame_mod, 8, 7)
    shift_one, scale_one, gate_one, shift_two, scale_two, gate_two = [
        frame_mod[:, i * width : (i + 1) * width] for i in range(6)
    ]

    hidden_turned, head_parts = project(
        tokens, shift_one, scale_one, qkv_weight, qkv_bias.astype(f32)[None, :], cosine, sine
    )
    heads = exchange(head_parts, clip_groups)
    outs, exts, attended = [], [], []
    for part in range(halves):
        out, ext = attend(heads, visible, patches, part, halves)
        outs.append(out)
        exts.append(ext)
        attended.append(exchange(out, clip_groups))

    hidden_turned, _ = lax.optimization_barrier((hidden_turned, heads))
    hidden_clip = lax.all_gather(hidden_turned, AXES, axis_index_groups=clip_groups)

    attn_low, attn_proj, after_attn, hidden_two, grad_branch = merge_heads(
        attended,
        proj_weight,
        proj_bias.astype(f32)[None, :],
        tokens,
        out_cotangent,
        (gate_one, shift_two, scale_two, gate_two),
    )
    branch, grad_hidden_two, up_b_grad, joined = feed_forward(
        hidden_two, grad_branch, up_weight, up_bias.astype(f32)[None, :], down_weight, devices
    )
    block_out, grad_after, grad_proj, grad_parts, early_sums, early_biases = unmerge_heads(
        branch,
        grad_hidden_two,
        after_attn,
        attn_proj,
        out_cotangent,
        gate_one,
        scale_two,
        gate_two,
        proj_weight,
        down_bias.astype(f32)[None, :],
    )
    grads = exchange(grad_parts, clip_groups)

    joined = proj_weight_grad(attn_low, grad_proj, joined)
    summed = lax.psum_scatter(joined, AXES, scatter_dimension=0, tiled=True)[0].astype(f32)
    quarters = inner // width
    up_w_out = jnp.concatenate([summed[i] for i in range(quarters)], axis=1)
    down_w_out = summed[quarters : 2 * quarters].reshape(per_dest, width)
    proj_w_out = summed[2 * quarters]

    def slot_parts(slot_sums, biases):
        kinds = slot_sums.shape[0] // frames
        sums = slot_sums.reshape(kinds, frames, width).transpose(1, 0, 2).reshape(frames, -1)
        sums = jnp.broadcast_to(sums.astype(bf16)[None], (devices, frames, kinds * width))
        high = biases.astype(bf16)
        low = (biases - high.astype(f32)).astype(bf16)
        both = jnp.concatenate([high, low], axis=1).reshape(devices, frames, -1)
        lanes = -(-both.shape[2] // LANES) * LANES
        both = jnp.pad(both, ((0, 0), (0, 0), (0, lanes - both.shape[2])))
        return jnp.concatenate([sums, both], axis=2)

    def bias_share(got, count, size):
        extra = jnp.sum(got[:, :, count:].astype(f32), axis=0)
        extra = extra[:, : 2 * size // frames].reshape(-1)
        return extra[:size] + extra[size:]

    slot_ids = (jnp.arange(devices * frames, dtype=jnp.int32) // (sp_count * frames)) * frames
    slot_ids = slot_ids + jnp.arange(devices * frames, dtype=jnp.int32) % frames
    slot_levels = frame_level[slot_ids // FRAMES, slot_time[slot_ids]]
    member_of = (level_ids[:, None] == slot_levels[None, :]).astype(bf16)
    my_columns = lax.dynamic_slice_in_dim(embed_act, me * share, share, axis=1)

    def level_out(got, count):
        slots = got[:, :, :count].reshape(devices * frames, count)
        level_grad = dot(member_of, slots).astype(bf16)
        return dot(my_columns, level_grad, TN), jnp.sum(level_grad.astype(f32), axis=0)

    early_parts = slot_parts(
        early_sums,
        jnp.concatenate(
            [
                up_b_grad.reshape(devices, per_dest),
                early_biases[0].reshape(devices, share),
                early_biases[1].reshape(devices, share),
            ],
            axis=1,
        ),
    )
    early_parts, _ = lax.optimization_barrier((early_parts, grads))
    early_got = exchange(early_parts, everyone)

    first_grads, carry = attend_back(
        heads, grads, exts, outs, rotary, None, 0, False, patches
    )
    carry, early_got = lax.optimization_barrier((carry, early_got))
    own_first = exchange(first_grads, clip_groups)
    (last_grads,) = attend_back(heads, grads, exts, outs, rotary, carry, 1, True, patches)
    last_parts, own_first = lax.optimization_barrier((last_grads, own_first))
    own_last = exchange(last_parts, clip_groups)

    early_w, early_b = level_out(early_got, 4 * width)
    early_bias_out = bias_share(early_got, 4 * width, per_dest + 2 * share)
    up_b_out = early_bias_out[:per_dest]
    proj_b_out = early_bias_out[per_dest : per_dest + share]
    down_b_out = early_bias_out[per_dest + share :]

    qkv_part = heads_grad(hidden_clip, first_grads, last_grads)
    qkv_part, own_last = lax.optimization_barrier((qkv_part, own_last))
    qkv_got = exchange(qkv_part.reshape(devices, share, 3 * LANES), everyone)
    qkv_w_out = lay_rows(qkv_got, group)

    tokens_grad, late_sums, *late_biases = finish(
        own_first, own_last, qkv_weight, tokens, scale_one, grad_after
    )
    late_parts = slot_parts(
        late_sums, jnp.concatenate(late_biases, axis=1).reshape(devices, 3 * share)
    )
    late_got = exchange(late_parts, everyone)
    late_w, late_b = level_out(late_got, 2 * width)
    qkv_b_out = bias_share(late_got, 2 * width, 3 * share)
    ada_w_out = jnp.concatenate([late_w, early_w], axis=1)
    ada_b_all = jnp.concatenate([late_b, early_b])
    ada_share = ada_b_all.shape[0] // devices
    ada_b_out = lax.dynamic_slice_in_dim(ada_b_all, me * ada_share, ada_share)
    return (
        block_out,
        tokens_grad,
        ada_w_out,
        ada_b_out,
        qkv_w_out,
        qkv_b_out,
        proj_w_out,
        proj_b_out,
        up_w_out,
        up_b_out,
        down_w_out,
        down_b_out,
    )


def solution(mesh):
    tokens_spec = P("frm", "sp", None)
    rows_spec = P(AXES, None)
    vector_spec = P(AXES)
    return jax.shard_map(
        body,
        mesh=mesh,
        in_specs=(tokens_spec, tokens_spec, rows_spec) + (P(),) * 13,
        out_specs=(tokens_spec, tokens_spec) + (rows_spec, vector_spec) * 5,
        check_vma=False,
    )
```

```python
import functools
import math

import jax
import jax.numpy as jnp
import numpy as np
from jax import lax
from jax.experimental import pallas as pl
from jax.experimental.pallas import tpu as pltpu
from jax.sharding import PartitionSpec as P

HEADS = 16
HDIM = 64
FRAMES = 16
GRID = 16
LANES = 128
MIB = 2**20

norm_eps = 1e-06
masked_out = -1e30
score_scale = 0.125

f32 = jnp.float32
bf16 = jnp.bfloat16
NN = (((1,), (0,)), ((), ()))
NT = (((1,), (1,)), ((), ()))
TN = (((0,), (0,)), ((), ()))
AXES = ("frm", "sp")
VMEM = pltpu.VMEM


def dot(left_op, right_op, dims=NN):
    return lax.dot_general(left_op, right_op, dims, preferred_element_type=f32)


def exchange(value, groups):
    return lax.all_to_all(value, AXES, 0, 0, axis_index_groups=groups)


def to_everyone(value, devices):
    return exchange(
        jnp.broadcast_to(value[None], (devices,) + value.shape), [list(range(devices))]
    )


def rotary_lanes():
    lane = np.arange(LANES) % HDIM
    start = np.where(lane < 16, 0, np.where(lane < 40, 16, 40))
    half = np.where(lane < 16, 8, 12)
    offset = lane - start
    freq = np.exp((offset % half).astype(np.float32) * np.float32(-math.log(10000.0)) / half)
    sign = np.where(offset < half, -1.0, 1.0)
    return (
        freq.astype(np.float32),
        sign.astype(np.float32),
        (lane < 16),
        (lane >= 16) & (lane < 40),
    )


def rotate_lanes(value, cosine, sine):
    lane = lax.broadcasted_iota(jnp.int32, value.shape, 1) % HDIM
    near_first = pltpu.roll(value, LANES - 8, 1)
    near_second = pltpu.roll(value, 8, 1)
    far_first = pltpu.roll(value, LANES - 12, 1)
    far_second = pltpu.roll(value, 12, 1)
    in_first = (lane < 28) | ((lane >= 40) & (lane < 52))
    far = jnp.where(in_first, far_first, far_second)
    near = jnp.where(lane < 8, near_first, near_second)
    partner = jnp.where(lane < 16, near, far)
    return value * cosine + partner * sine


def project_kernel(tok_ref, shift_ref, scale_ref, wq_ref, wk_ref, wv_ref, bq_ref, bk_ref, bv_ref,
                   cos_ref, sin_ref, turned_ref, out_ref, hid_all):
    frames, patches, _ = tok_ref.shape

    @pl.when(pl.program_id(0) == 0)
    def _():
        for f in range(frames):
            here = slice(f * patches, (f + 1) * patches)
            x = tok_ref[f].astype(f32)
            centre = x - jnp.mean(x, axis=1, keepdims=True)
            inv = lax.rsqrt(jnp.mean(centre * centre, axis=1, keepdims=True) + norm_eps)
            hid = centre * inv * (1.0 + scale_ref[f : f + 1, :]) + shift_ref[f : f + 1, :]
            hid = hid.astype(bf16)
            hid_all[here, :] = hid
            turned_ref[:, here] = hid.T

    hid = hid_all[...]
    query = dot(hid, wq_ref[...]) + bq_ref[...]
    keys = dot(hid, wk_ref[...]) + bk_ref[...]
    vals = (dot(hid, wv_ref[...]) + bv_ref[...]).astype(bf16)
    for p in range(wq_ref.shape[1] // LANES):
        lanes = slice(p * LANES, (p + 1) * LANES)
        out_ref[p, 0] = rotate_lanes(query[:, lanes], cos_ref[...], sin_ref[...]).astype(bf16)
        out_ref[p, 1] = rotate_lanes(keys[:, lanes], cos_ref[...], sin_ref[...]).astype(bf16)
        out_ref[p, 2] = vals[:, lanes]


def whole(shape):
    return pl.BlockSpec(shape, lambda *_: (0,) * len(shape))


def project(tokens, shift_one, scale_one, qkv_weight, qkv_bias, cosine, sine, cols=256):
    frames, patches, width = tokens.shape
    rows = frames * patches
    pairs = width // LANES
    steps, some = width // cols, cols // LANES

    def column(part):
        return lambda c: (0, part * steps + c)

    return pl.pallas_call(
        project_kernel,
        out_shape=[
            jax.ShapeDtypeStruct((width, rows), bf16),
            jax.ShapeDtypeStruct((pairs, 3, rows, LANES), bf16),
        ],
        grid=(steps,),
        in_specs=[whole(tokens.shape), whole(shift_one.shape), whole(scale_one.shape)]
        + [pl.BlockSpec((width, cols), column(part)) for part in range(3)]
        + [pl.BlockSpec((1, cols), column(part)) for part in range(3)]
        + [whole((rows, LANES)), whole((rows, LANES))],
        out_specs=[
            whole((width, rows)),
            pl.BlockSpec((some, 3, rows, LANES), lambda c: (c, 0, 0, 0)),
        ],
        scratch_shapes=[VMEM((rows, width), bf16)],
        compiler_params=pltpu.CompilerParams(vmem_limit_bytes=40 * MIB),
        cost_estimate=pl.CostEstimate(
            flops=6 * rows * width * width, bytes_accessed=10 * MIB, transcendentals=0
        ),
        name="project",
    )(tokens, shift_one, scale_one, *[qkv_weight] * 3, *[qkv_bias] * 3, cosine, sine)


def key_extra(first_frame, rows, patches):
    row = lax.broadcasted_iota(jnp.int32, (rows, LANES), 0)
    lane = lax.broadcasted_iota(jnp.int32, (rows, LANES), 1)
    hit = (lane == first_frame + row // patches) | ((lane >= FRAMES) & (lane < FRAMES + 3))
    return jnp.where(hit, 1.0, 0.0).astype(bf16)


def split_three(column):
    high = column.astype(bf16).astype(f32)
    rest = column - high
    mid = rest.astype(bf16).astype(f32)
    return high, mid, rest - mid


def attend_kernel(part, rows_part, patches, joined, joined_keys, qkv_ref, vis_ref, o_ref, ext_ref):
    blocks, _, rows, _ = qkv_ref.shape
    frames, frames_part = rows // patches, rows_part // patches
    tile, chunk = joined * rows_part, joined_keys * rows
    lane = lax.broadcasted_iota(jnp.int32, (tile, LANES), 1)
    mine_rows = slice(part * rows_part, (part + 1) * rows_part)
    ones = jnp.full((chunk, LANES), 1.0, bf16)

    def step(t, carry):
        query = jnp.concatenate(
            [qkv_ref[t * joined + i, 0, mine_rows, :] for i in range(joined)], axis=0
        )
        query = query * score_scale
        seen = jnp.concatenate(
            [
                jnp.broadcast_to(
                    vis_ref[pl.ds((t * joined + i) * frames + part * frames_part + f, 1), :],
                    (patches, LANES),
                )
                for i in range(joined)
                for f in range(frames_part)
            ],
            axis=0,
        )
        outs, ext_heads = [], []
        for h in range(2):
            mine = jnp.where((lane >= HDIM) == (h == 1), query, jnp.zeros_like(query))
            query_ext = jnp.concatenate([mine.astype(bf16), seen.astype(bf16)], axis=1)
            top = None
            for c in range(0, blocks, joined_keys):
                some_blocks = range(c, c + joined_keys)
                keys = jnp.concatenate(
                    [
                        jnp.concatenate(
                            [qkv_ref[b, 1], key_extra((b // 2) * frames, rows, patches)], axis=1
                        )
                        for b in some_blocks
                    ],
                    axis=0,
                )
                vals = jnp.concatenate([qkv_ref[b, 2] for b in some_blocks], axis=0)
                vals = jnp.concatenate([vals, ones], axis=1)
                scores = dot(query_ext, keys, NT)
                chunk_top = jnp.max(scores, axis=1, keepdims=True)
                new_top = chunk_top if top is None else jnp.maximum(top, chunk_top)
                some = dot(jnp.exp(scores - new_top).astype(bf16), vals)
                total = some if top is None else total * jnp.exp(top - new_top) + some
                top = new_top
            weight_sum = total[:, LANES : LANES + 1]
            outs.append(total[:, :LANES] / weight_sum)
            high, mid, low = split_three(-(top + jnp.log(weight_sum)))
            ext = jnp.where(lane == FRAMES, high, seen)
            ext = jnp.where(lane == FRAMES + 1, mid, ext)
            ext_heads.append(jnp.where(lane == FRAMES + 2, low, ext).astype(bf16))
        out = jnp.where(lane < HDIM, outs[0], outs[1]).astype(bf16)
        for i in range(joined):
            here = slice(i * rows_part, (i + 1) * rows_part)
            o_ref[t * joined + i] = out[here, :]
            for h in range(2):
                ext_ref[h, t * joined + i] = ext_heads[h][here, :]
        return carry

    lax.fori_loop(0, blocks // joined, step, 0)


def attend(heads, visible, patches, part, parts, tile=1024, chunk=1024):
    blocks, _, rows, _ = heads.shape
    rows_part = rows // parts
    keys = blocks * rows
    return pl.pallas_call(
        functools.partial(
            attend_kernel, part, rows_part, patches, tile // rows_part, chunk // rows
        ),
        out_shape=[
            jax.ShapeDtypeStruct((blocks, rows_part, LANES), bf16),
            jax.ShapeDtypeStruct((2, blocks, rows_part, LANES), bf16),
        ],
        in_specs=[pl.BlockSpec(memory_space=VMEM)] * 2,
        out_specs=[pl.BlockSpec(memory_space=VMEM)] * 2,
        compiler_params=pltpu.CompilerParams(vmem_limit_bytes=48 * MIB),
        cost_estimate=pl.CostEstimate(
            flops=8 * blocks * rows_part * keys * 2 * LANES,
            bytes_accessed=4 * MIB,
            transcendentals=0,
        ),
        name="attend",
    )(heads, visible)


def attend_back_kernel(parts, part, patches, joined, together, carried, last, *refs):
    at = 0

    def take(count):
        nonlocal at
        found = refs[at : at + count]
        at += count
        return found

    (qkv_ref, do_ref) = take(2)
    ext_refs, o_refs = take(parts), take(parts)
    ctime_ref, stime_ref, cpatch_ref, spatch_ref = take(4)
    if carried:
        carry_ref, mix_ref = take(2)
    if last:
        (grads_ref,) = take(1)
    else:
        grads_ref, carry_out, mix_ref = take(3)
    (dq_turned,) = refs[at:]
    blocks, _, rows, _ = qkv_ref.shape
    rows_part = rows // parts
    frames, frames_part = rows // patches, rows_part // patches
    lane = lax.broadcasted_iota(jnp.int32, (rows_part, LANES), 1)
    if carried:
        dq_turned[...] = carry_ref[...]
    else:
        dq_turned[...] = jnp.zeros_like(dq_turned)
        for b in range(blocks):
            for i in range(parts):
                there = slice(i * rows_part, (i + 1) * rows_part)
                mixed = do_ref[b, there, :].astype(f32) * o_refs[i][b].astype(f32)
                for h in range(2):
                    mine = jnp.where((lane >= HDIM) == (h == 1), mixed, 0.0)
                    high, mid, low = split_three(-jnp.sum(mine, axis=1, keepdims=True))
                    ext = jnp.where(lane == 1, mid, jnp.where(lane == 2, low, 0.0))
                    mix_ref[h, b, there, :] = jnp.where(lane == 0, high, ext).astype(bf16)
    key_rows = slice(part * rows_part, (part + 1) * rows_part)
    key_lane = lax.broadcasted_iota(jnp.int32, (together * rows_part, LANES), 1)
    mix_keys = jnp.where(key_lane < 3, 1.0, 0.0).astype(bf16)

    def back(value, row, half):
        cosine = ctime_ref[pl.ds(row, 1), :] + cpatch_ref[half]
        sine = stime_ref[pl.ds(row, 1), :] + spatch_ref[half]
        return rotate_lanes(value, cosine, -sine).astype(bf16)

    first = rows if last else 0

    def step(t, carry):
        key_blocks = [t * together + i for i in range(together)]
        keys = jnp.concatenate([qkv_ref[b, 1, key_rows, :] for b in key_blocks], axis=0)
        keys = keys * score_scale
        vals = jnp.concatenate([qkv_ref[b, 2, key_rows, :] for b in key_blocks], axis=0)
        turned = keys.astype(f32).T.astype(bf16)
        extra = jnp.concatenate(
            [
                key_extra((b // 2) * frames + part * frames_part, rows_part, patches)
                for b in key_blocks
            ],
            axis=0,
        )
        key_tiles, val_tiles = [], []
        for h in range(2):
            mine = (key_lane >= HDIM) == (h == 1)
            none = jnp.zeros_like(keys)
            key_tiles.append(
                jnp.concatenate([jnp.where(mine, keys, none).astype(bf16), extra], axis=1)
            )
            val_tiles.append(jnp.concatenate([jnp.where(mine, vals, none), mix_keys], axis=1))
        dk = [jnp.zeros((together * rows_part, LANES), f32)] * 2
        dv = [jnp.zeros((together * rows_part, LANES), f32)] * 2
        for c in range(0, blocks, joined):
            some = range(c, c + joined)
            span = slice(c * rows, (c + joined) * rows)
            query = jnp.concatenate([qkv_ref[b, 0] for b in some], axis=0)
            grad = jnp.concatenate([do_ref[b] for b in some], axis=0)
            for h in range(2):
                ext = jnp.concatenate([ext_refs[i][h, b] for b in some for i in range(parts)], axis=0)
                mix = jnp.concatenate([mix_ref[h, b] for b in some], axis=0)
                probs = jnp.exp(dot(key_tiles[h], jnp.concatenate([query, ext], axis=1), NT))
                dv[h] = dv[h] + dot(probs.astype(bf16), grad)
                moved = dot(val_tiles[h], jnp.concatenate([grad, mix], axis=1), NT)
                grad_scores = (probs * moved).astype(bf16)
                dk[h] = dk[h] + dot(grad_scores, query)
                head = slice(HDIM * h, HDIM * (h + 1))
                dq_turned[head, span] += dot(turned[head, :], grad_scores)
        dk = jnp.where(key_lane < HDIM, dk[0], dk[1]) * score_scale
        dv = jnp.where(key_lane < HDIM, dv[0], dv[1]).astype(bf16)
        for i, b in enumerate(key_blocks):
            for f in range(frames_part):
                rows_here = slice(i * rows_part + f * patches, i * rows_part + (f + 1) * patches)
                row = b * frames + part * frames_part + f
                keys_here = slice(first + f * patches, first + (f + 1) * patches)
                grads_ref[b, keys_here, :] = back(dk[rows_here, :], row, b % 2)
            grads_ref[b, first + rows_part : first + 2 * rows_part, :] = dv[
                i * rows_part : (i + 1) * rows_part, :
            ]
        return carry

    lax.fori_loop(0, blocks // together, step, 0)

    if last:
        for b in range(blocks):
            for f in range(frames):
                there = slice(b * rows + f * patches, b * rows + (f + 1) * patches)
                turned_back = back(dq_turned[:, there].T, b * frames + f, b % 2)
                grads_ref[b, f * patches : (f + 1) * patches, :] = turned_back
    else:
        carry_out[...] = dq_turned[...]


def attend_back(heads, grads, exts, outs, rotary, carry, part, last, patches, chunk=2048, together=2):
    parts = len(exts)
    blocks, _, rows, _ = heads.shape
    rows_part = rows // parts
    total = blocks * rows
    operands = [heads, grads, *exts, *outs, *rotary, *(carry or ())]
    kept = 2 * rows_part + (rows if last else 0)
    out_shape = [jax.ShapeDtypeStruct((blocks, kept, LANES), bf16)]
    if not last:
        out_shape.append(jax.ShapeDtypeStruct((LANES, total), f32))
        out_shape.append(jax.ShapeDtypeStruct((2, blocks, rows, LANES), bf16))
    return pl.pallas_call(
        functools.partial(
            attend_back_kernel, parts, part, patches, chunk // rows, together, carry is not None, last
        ),
        out_shape=out_shape,
        in_specs=[pl.BlockSpec(memory_space=VMEM)] * len(operands),
        out_specs=[pl.BlockSpec(memory_space=VMEM)] * len(out_shape),
        scratch_shapes=[VMEM((LANES, total), f32)],
        compiler_params=pltpu.CompilerParams(vmem_limit_bytes=56 * MIB),
        cost_estimate=pl.CostEstimate(
            flops=20 * total * blocks * rows_part * 2 * LANES,
            bytes_accessed=8 * MIB,
            transcendentals=0,
        ),
        name="attend_back",
    )(*operands)


def act_grad_kernel(cot_ref, gate_ref, down_ref, grad_ref, out_ref):
    frames, patches, _ = cot_ref.shape

    @pl.when(pl.program_id(0) == 0)
    def _():
        for f in range(frames):
            grad = gate_ref[f : f + 1, :] * cot_ref[f].astype(f32)
            grad_ref[f * patches : (f + 1) * patches, :] = grad.astype(bf16)

    out_ref[...] = dot(grad_ref[...], down_ref[...], NT)


def act_grad(cotangent, gate_two, down_weight, cols=512):
    frames, patches, width = cotangent.shape
    rows, inner = frames * patches, down_weight.shape[0]
    return pl.pallas_call(
        act_grad_kernel,
        out_shape=[
            jax.ShapeDtypeStruct((rows, width), bf16),
            jax.ShapeDtypeStruct((rows, inner), f32),
        ],
        grid=(inner // cols,),
        in_specs=[
            whole(cotangent.shape),
            whole(gate_two.shape),
            pl.BlockSpec((cols, width), lambda c: (c, 0)),
        ],
        out_specs=[whole((rows, width)), pl.BlockSpec((rows, cols), lambda c: (0, c))],
        compiler_params=pltpu.CompilerParams(vmem_limit_bytes=40 * MIB),
        cost_estimate=pl.CostEstimate(
            flops=2 * rows * width * inner, bytes_accessed=18 * MIB, transcendentals=0
        ),
        name="act_grad",
    )(cotangent, gate_two, down_weight)


def feed_kernel(hid_ref, grad_ref, actgrad_ref, up_ref, bias_ref, down_ref,
                branch_ref, back_ref, biasgrad_ref, joined_ref,
                hid_turned, up_slots, down_slots, up_sems, down_sems):
    step, steps = pl.program_id(0), pl.num_programs(0)
    width, cols = up_ref.shape
    group, clips, _, share, _ = joined_ref.shape
    some_clips, quarters = down_slots.shape[2:4]
    up_parts = width // cols
    slot = step % 2

    def copies(at):
        across = pl.ds(pl.multiple_of((at % up_parts) * cols, cols), cols)
        up_copy = pltpu.make_async_copy(
            up_slots.at[at % 2], joined_ref.at[:, :, at // up_parts, :, across], up_sems.at[at % 2]
        )
        down_copy = pltpu.make_async_copy(
            down_slots.at[at % 2],
            joined_ref.at[:, pl.ds(at * some_clips, some_clips), quarters : 2 * quarters],
            down_sems.at[at % 2],
        )
        return up_copy, down_copy

    @pl.when(step == 0)
    def _():
        hid_turned[...] = hid_ref[...].T

    @pl.when(step >= 2)
    def _():
        for copy in copies(step - 2):
            copy.wait()

    pre = dot(hid_ref[...], up_ref[...]) + bias_ref[...]
    square = pre * pre
    bend = jnp.tanh(pre * (0.7978845608 + (0.7978845608 * 0.044715) * square))
    half = 0.5 * (1.0 + bend)
    act = (pre * half).astype(bf16)
    slope = half + (0.5 * pre) * (1.0 - bend * bend) * (
        0.7978845608 + (0.7978845608 * 3.0 * 0.044715) * square
    )
    pre_grad = (slope * actgrad_ref[...]).astype(bf16)
    biasgrad_ref[...] = jnp.sum(pre_grad.astype(f32), axis=0, keepdims=True)
    branch = dot(act, down_ref[...])
    back = dot(pre_grad, up_ref[...], NT)
    up_grad = dot(hid_turned[...], pre_grad).astype(bf16)
    up_grad = up_grad.reshape(clips, group, share, cols)
    for c in range(clips):
        up_slots[slot, :, c] = up_grad[c]
    down_grad = dot(act.T, grad_ref[...]).astype(bf16)
    down_grad = down_grad.reshape(some_clips, group, quarters, share, width)
    for c in range(some_clips):
        down_slots[slot, :, c] = down_grad[c]

    @pl.when(step == 0)
    def _():
        branch_ref[...] = branch
        back_ref[...] = back

    @pl.when(step > 0)
    def _():
        branch_ref[...] += branch
        back_ref[...] += back

    for copy in copies(step):
        copy.start()

    @pl.when(step == steps - 1)
    def _():
        for at in (steps - 2, steps - 1):
            for copy in copies(at):
                copy.wait()


def feed_forward(hidden, grad, grad_act, up_weight, up_bias, down_weight, group, clips, cols=1024):
    rows, width = hidden.shape
    inner = up_weight.shape[1]
    share, quarters = width // (group * clips), inner // width
    some_clips = cols * clips // inner
    return pl.pallas_call(
        feed_kernel,
        out_shape=[
            jax.ShapeDtypeStruct((rows, width), f32),
            jax.ShapeDtypeStruct((rows, width), f32),
            jax.ShapeDtypeStruct((1, inner), f32),
            jax.ShapeDtypeStruct((group, clips, 2 * quarters + 1, share, width), bf16),
        ],
        grid=(inner // cols,),
        in_specs=[
            whole((rows, width)),
            whole((rows, width)),
            pl.BlockSpec((rows, cols), lambda c: (0, c)),
            pl.BlockSpec((width, cols), lambda c: (0, c)),
            pl.BlockSpec((1, cols), lambda c: (0, c)),
            pl.BlockSpec((cols, width), lambda c: (c, 0)),
        ],
        out_specs=[
            whole((rows, width)),
            whole((rows, width)),
            pl.BlockSpec((1, cols), lambda c: (0, c)),
            pl.BlockSpec(memory_space=pl.ANY),
        ],
        scratch_shapes=[
            VMEM((width, rows), bf16),
            VMEM((2, group, clips, share, cols), bf16),
            VMEM((2, group, some_clips, quarters, share, width), bf16),
            pltpu.SemaphoreType.DMA((2,)),
            pltpu.SemaphoreType.DMA((2,)),
        ],
        compiler_params=pltpu.CompilerParams(vmem_limit_bytes=58 * MIB),
        cost_estimate=pl.CostEstimate(
            flops=10 * rows * width * inner, bytes_accessed=44 * MIB, transcendentals=0
        ),
        name="feed_forward",
    )(hidden, grad, grad_act, up_weight, up_bias, down_weight)


def proj_grad_kernel(attn_ref, grad_ref, _, joined_ref):
    group, clips, _, share, width = joined_ref.shape
    grad = dot(attn_ref[...].T, grad_ref[...]).astype(bf16).reshape(clips, group, share, width)
    for c in range(clips):
        joined_ref[:, c, 0] = grad[c]


def proj_weight_grad(attn_low, grad_proj, joined):
    rows, width = attn_low.shape
    group, clips, entries, share, _ = joined.shape
    return pl.pallas_call(
        proj_grad_kernel,
        out_shape=jax.ShapeDtypeStruct(joined.shape, joined.dtype),
        grid=(1,),
        in_specs=[
            whole((rows, width)),
            whole((rows, width)),
            pl.BlockSpec(memory_space=pl.ANY),
        ],
        out_specs=pl.BlockSpec((group, clips, 1, share, width), lambda c: (0, 0, entries - 1, 0, 0)),
        input_output_aliases={2: 0},
        compiler_params=pltpu.CompilerParams(vmem_limit_bytes=40 * MIB),
        cost_estimate=pl.CostEstimate(
            flops=2 * rows * width * width, bytes_accessed=4 * MIB, transcendentals=0
        ),
        name="proj_weight_grad",
    )(attn_low, grad_proj, joined)


def merge_kernel(*refs):
    parts = len(refs) - 10
    att_refs = refs[:parts]
    (weight_ref, bias_ref, tok_ref, gate_one_ref, shift_ref, scale_ref,
     low_ref, proj_ref, after_ref, hid_ref) = refs[parts:]
    frames, patches, width = tok_ref.shape
    pairs, rows_part, _ = att_refs[0].shape
    for i, att_ref in enumerate(att_refs):
        low = jnp.concatenate([att_ref[p] for p in range(pairs)], axis=1)
        there = slice(i * rows_part, (i + 1) * rows_part)
        low_ref[there, :] = low
        proj = dot(low, weight_ref[...]) + bias_ref[...]
        proj_ref[there, :] = proj
        for j in range(rows_part // patches):
            f = i * (rows_part // patches) + j
            here = slice(f * patches, (f + 1) * patches)
            row = slice(f, f + 1)
            after = tok_ref[f].astype(f32) + gate_one_ref[row, :] * proj[
                j * patches : (j + 1) * patches, :
            ]
            after_ref[here, :] = after
            centre = after - jnp.mean(after, axis=1, keepdims=True)
            inv = lax.rsqrt(jnp.mean(centre * centre, axis=1, keepdims=True) + norm_eps)
            hid = centre * inv * (1.0 + scale_ref[row, :]) + shift_ref[row, :]
            hid_ref[here, :] = hid.astype(bf16)


def merge_heads(attended, proj_weight, proj_bias, tokens, mods):
    frames, patches, width = tokens.shape
    rows = frames * patches
    operands = [*attended, proj_weight, proj_bias, tokens, *mods]
    return pl.pallas_call(
        merge_kernel,
        out_shape=[
            jax.ShapeDtypeStruct((rows, width), bf16),
            jax.ShapeDtypeStruct((rows, width), f32),
            jax.ShapeDtypeStruct((rows, width), f32),
            jax.ShapeDtypeStruct((rows, width), bf16),
        ],
        in_specs=[pl.BlockSpec(memory_space=VMEM)] * len(operands),
        out_specs=[pl.BlockSpec(memory_space=VMEM)] * 4,
        compiler_params=pltpu.CompilerParams(vmem_limit_bytes=48 * MIB),
        cost_estimate=pl.CostEstimate(
            flops=2 * rows * width * width, bytes_accessed=16 * MIB, transcendentals=0
        ),
        name="merge_heads",
    )(*operands)


def column_sum(value):
    return jnp.sum(value, axis=0, keepdims=True)


def unmerge_kernel(back_ref, after_ref, cot_ref, gate_one_ref, scale_ref, weight_ref,
                   grad_ref, gproj_ref, parts_ref):
    frames, patches, width = cot_ref.shape
    for f in range(frames):
        here = slice(f * patches, (f + 1) * patches)
        row = slice(f, f + 1)
        after = after_ref[here, :]
        centre = after - jnp.mean(after, axis=1, keepdims=True)
        inv = lax.rsqrt(jnp.mean(centre * centre, axis=1, keepdims=True) + norm_eps)
        normed = centre * inv
        scaled = back_ref[here, :] * (1.0 + scale_ref[row, :])
        mean_grad = jnp.mean(scaled, axis=1, keepdims=True)
        mean_mix = jnp.mean(scaled * normed, axis=1, keepdims=True)
        grad = cot_ref[f].astype(f32) + inv * (scaled - mean_grad - normed * mean_mix)
        grad_ref[here, :] = grad
        gproj_ref[here, :] = (gate_one_ref[row, :] * grad).astype(bf16)
    step = 2 * patches
    for i in range(frames * patches // step):
        here = slice(i * step, (i + 1) * step)
        part = dot(gproj_ref[here, :], weight_ref[...], NT).astype(bf16)
        for p in range(parts_ref.shape[0]):
            parts_ref[p, here, :] = part[:, p * LANES : (p + 1) * LANES]


def unmerge_heads(back, after, cotangent, gate_one, scale_two, proj_weight):
    frames, patches, width = cotangent.shape
    rows = frames * patches
    operands = [back, after, cotangent, gate_one, scale_two, proj_weight]
    return pl.pallas_call(
        unmerge_kernel,
        out_shape=[
            jax.ShapeDtypeStruct((rows, width), f32),
            jax.ShapeDtypeStruct((rows, width), bf16),
            jax.ShapeDtypeStruct((width // LANES, rows, LANES), bf16),
        ],
        in_specs=[pl.BlockSpec(memory_space=VMEM)] * len(operands),
        out_specs=[pl.BlockSpec(memory_space=VMEM)] * 3,
        compiler_params=pltpu.CompilerParams(vmem_limit_bytes=48 * MIB),
        cost_estimate=pl.CostEstimate(
            flops=2 * rows * width * width, bytes_accessed=12 * MIB, transcendentals=0
        ),
        name="unmerge_heads",
    )(*operands)


def side_kernel(branch_ref, back_ref, after_ref, proj_ref, cot_ref, gate_two_ref, bias_ref,
                grad_ref, gproj_ref, gbranch_ref, out_ref, sums_ref, biases_ref):
    frames, patches, width = cot_ref.shape
    proj_sum = jnp.zeros((1, width), f32)
    down_sum = jnp.zeros((1, width), f32)
    for f in range(frames):
        here = slice(f * patches, (f + 1) * patches)
        cot = cot_ref[f].astype(f32)
        after = after_ref[here, :]
        branch = branch_ref[here, :] + bias_ref[...]
        out_ref[f] = (after + gate_two_ref[f : f + 1, :] * branch).astype(bf16)
        centre = after - jnp.mean(after, axis=1, keepdims=True)
        inv = lax.rsqrt(jnp.mean(centre * centre, axis=1, keepdims=True) + norm_eps)
        back = back_ref[here, :]
        for kind, term in enumerate(
            (grad_ref[here, :] * proj_ref[here, :], back, back * (centre * inv), cot * branch)
        ):
            sums_ref[kind * frames + f : kind * frames + f + 1, :] = column_sum(term)
        down_sum += column_sum(gbranch_ref[here, :].astype(f32))
        proj_sum += column_sum(gproj_ref[here, :].astype(f32))
    biases_ref[0:1, :] = proj_sum
    biases_ref[1:2, :] = down_sum


def side_sums(branch, back, after, proj, cotangent, gate_two, down_bias, grad_after, grad_proj,
              grad_branch):
    frames, patches, width = cotangent.shape
    operands = [branch, back, after, proj, cotangent, gate_two, down_bias, grad_after, grad_proj,
                grad_branch]
    return pl.pallas_call(
        side_kernel,
        out_shape=[
            jax.ShapeDtypeStruct((frames, patches, width), bf16),
            jax.ShapeDtypeStruct((4 * frames, width), f32),
            jax.ShapeDtypeStruct((2, width), f32),
        ],
        in_specs=[pl.BlockSpec(memory_space=VMEM)] * len(operands),
        out_specs=[pl.BlockSpec(memory_space=VMEM)] * 3,
        compiler_params=pltpu.CompilerParams(vmem_limit_bytes=48 * MIB),
        cost_estimate=pl.CostEstimate(flops=0, bytes_accessed=16 * MIB, transcendentals=0),
        name="side_sums",
    )(*operands)


def heads_grad_kernel(hid_ref, first_ref, last_ref, out_ref, bias_ref, total):
    rows = hid_ref.shape[2]
    rows_part = first_ref.shape[1] // 2
    grad = jnp.concatenate(
        [
            last_ref[0, :rows, :],
            jnp.concatenate(
                [first_ref[0, :rows_part, :], last_ref[0, rows : rows + rows_part, :]], axis=0
            ),
            jnp.concatenate([first_ref[0, rows_part:, :], last_ref[0, rows + rows_part :, :]], axis=0),
        ],
        axis=1,
    )
    some = dot(hid_ref[0], grad)
    some_bias = column_sum(grad.astype(f32))

    @pl.when(pl.program_id(0) == 0)
    def _():
        total[...] = some
        bias_ref[...] = some_bias

    @pl.when(pl.program_id(0) > 0)
    def _():
        total[...] += some
        bias_ref[...] += some_bias

    @pl.when(pl.program_id(0) == pl.num_programs(0) - 1)
    def _():
        devices, triple, _ = out_ref.shape
        share = triple // 3
        for k in range(3):
            part = total[:, k * LANES : (k + 1) * LANES].astype(bf16)
            out_ref[:, k * share : (k + 1) * share, :] = part.reshape(devices, share, LANES)


def heads_grad(hidden_clip, first, last, devices):
    blocks, width, rows = hidden_clip.shape
    shape = (devices, 3 * width // devices, LANES)
    return pl.pallas_call(
        heads_grad_kernel,
        out_shape=[
            jax.ShapeDtypeStruct(shape, bf16),
            jax.ShapeDtypeStruct((1, 3 * LANES), f32),
        ],
        grid=(blocks,),
        in_specs=[
            pl.BlockSpec((1, width, rows), lambda b: (b, 0, 0)),
            pl.BlockSpec((1,) + first.shape[1:], lambda b: (b, 0, 0)),
            pl.BlockSpec((1,) + last.shape[1:], lambda b: (b, 0, 0)),
        ],
        out_specs=[whole(shape), whole((1, 3 * LANES))],
        scratch_shapes=[VMEM((width, 3 * LANES), f32)],
        compiler_params=pltpu.CompilerParams(vmem_limit_bytes=40 * MIB),
        cost_estimate=pl.CostEstimate(
            flops=6 * blocks * rows * width * LANES, bytes_accessed=12 * MIB, transcendentals=0
        ),
        name="heads_grad",
    )(hidden_clip, first, last)


def finish_kernel(first_ref, last_ref, wq_ref, wk_ref, wv_ref, tok_ref, scale_ref, after_ref,
                  part_ref, partbias_ref, out_ref, send_ref, total):
    frames, patches, width = tok_ref.shape
    rows = frames * patches
    rows_part = first_ref.shape[1] // 2
    step = pl.program_id(0)
    query, keys, vals = [], [], []
    for p in range(first_ref.shape[0]):
        query.append(last_ref[p, :rows, :])
        keys.append(
            jnp.concatenate(
                [first_ref[p, :rows_part, :], last_ref[p, rows : rows + rows_part, :]], axis=0
            )
        )
        vals.append(
            jnp.concatenate([first_ref[p, rows_part:, :], last_ref[p, rows + rows_part :, :]], axis=0)
        )
    some = None
    for grads, weight_ref in ((query, wq_ref), (keys, wk_ref), (vals, wv_ref)):
        term = dot(jnp.concatenate(grads, axis=1), weight_ref[...], NT)
        some = term if some is None else some + term

    @pl.when(step == 0)
    def _():
        total[...] = some

    @pl.when(step > 0)
    def _():
        total[...] += some

    @pl.when(step == pl.num_programs(0) - 1)
    def _():
        shift_sums, scale_sums = [], []
        for f in range(frames):
            here = slice(f * patches, (f + 1) * patches)
            x = tok_ref[f].astype(f32)
            centre = x - jnp.mean(x, axis=1, keepdims=True)
            inv = lax.rsqrt(jnp.mean(centre * centre, axis=1, keepdims=True) + norm_eps)
            normed = centre * inv
            back = total[here, :]
            shift_sums.append(column_sum(back))
            scale_sums.append(column_sum(back * normed))
            scaled = back * (1.0 + scale_ref[f : f + 1, :])
            mean_grad = jnp.mean(scaled, axis=1, keepdims=True)
            mean_mix = jnp.mean(scaled * normed, axis=1, keepdims=True)
            grad = after_ref[here, :] + inv * (scaled - mean_grad - normed * mean_mix)
            out_ref[f] = grad.astype(bf16)
        sums = jnp.concatenate(shift_sums + scale_sums, axis=0)
        sums = jnp.concatenate(
            [sums[:, i : i + LANES] for i in range(0, width, LANES)], axis=0
        ).astype(bf16)
        bias = [partbias_ref[:, k * LANES : (k + 1) * LANES] for k in range(3)]
        high = [value.astype(bf16).astype(f32) for value in bias]
        low = [value - upper for value, upper in zip(bias, high)]
        bias = jnp.concatenate(high + low + [jnp.zeros((10, LANES), f32)], axis=0).astype(bf16)
        devices, triple, _ = part_ref.shape
        count = sums.shape[0]
        send_ref[:, count : count + triple, :] = part_ref[...]
        for d in range(devices):
            send_ref[d, :count, :] = sums
            send_ref[d, count + triple :, :] = bias


def finish(first, last, qkv_weight, tokens, scale_one, grad_after, part, part_bias, cols=256):
    frames, patches, width = tokens.shape
    rows = frames * patches
    steps, some = width // cols, cols // LANES

    devices, triple, _ = part.shape
    send_shape = (devices, 2 * frames * (width // LANES) + triple + 16, LANES)

    def column(third):
        return lambda c: (0, third * steps + c)

    return pl.pallas_call(
        finish_kernel,
        out_shape=[
            jax.ShapeDtypeStruct((frames, patches, width), bf16),
            jax.ShapeDtypeStruct(send_shape, bf16),
        ],
        grid=(steps,),
        in_specs=[
            pl.BlockSpec((some,) + first.shape[1:], lambda c: (c, 0, 0)),
            pl.BlockSpec((some,) + last.shape[1:], lambda c: (c, 0, 0)),
        ]
        + [pl.BlockSpec((width, cols), column(part)) for part in range(3)]
        + [whole(tokens.shape), whole(scale_one.shape), whole((rows, width))]
        + [whole(part.shape), whole(part_bias.shape)],
        out_specs=[whole((frames, patches, width)), whole(send_shape)],
        scratch_shapes=[VMEM((rows, width), f32)],
        compiler_params=pltpu.CompilerParams(vmem_limit_bytes=48 * MIB),
        cost_estimate=pl.CostEstimate(
            flops=6 * rows * width * width, bytes_accessed=16 * MIB, transcendentals=0
        ),
        name="finish",
    )(first, last, *[qkv_weight] * 3, tokens, scale_one, grad_after, part, part_bias)


def last_kernel(group, frames, got_ref, member_ref, cols_ref, rows_ref, bias_ref, ada_ref, adasum_ref):
    devices = got_ref.shape[0]
    clips = devices // group
    width = rows_ref.shape[1] // 3
    tiles = width // LANES
    count = 2 * frames * tiles
    share = (got_ref.shape[1] - count - 16) // 3
    for i in range(tiles // 2):
        sums = got_ref[:, i * 4 * frames : (i + 1) * 4 * frames, :]
        sums = sums.reshape(devices * 4 * frames, LANES)
        for j in range(2):
            for kind in range(2):
                level = dot(member_ref[2 * j + kind], sums).astype(bf16)
                at = kind * width + (2 * i + j) * LANES
                ada_ref[:, at : at + LANES] = dot(cols_ref[...], level)
                adasum_ref[:, at : at + LANES] = column_sum(level.astype(f32))
    for p in range(group):
        bias = got_ref[p, count + 3 * share :, :].astype(f32)
        for c in range(1, clips):
            bias = bias + got_ref[c * group + p, count + 3 * share :, :].astype(f32)
        for third in range(3):
            at = third * width + p * LANES
            here = slice(count + third * share, count + (third + 1) * share)
            total = got_ref[p, here, :].astype(f32)
            for c in range(1, clips):
                total = total + got_ref[c * group + p, here, :].astype(f32)
            rows_ref[:, at : at + LANES] = total
            bias_ref[:, at : at + LANES] = bias[third : third + 1, :] + bias[third + 3 : third + 4, :]


def last_sums(got, member, columns, group, frames, width):
    devices = got.shape[0]
    share = width // devices
    return pl.pallas_call(
        functools.partial(last_kernel, group, frames),
        out_shape=[
            jax.ShapeDtypeStruct((share, 3 * width), f32),
            jax.ShapeDtypeStruct((1, 3 * width), f32),
            jax.ShapeDtypeStruct((share, 2 * width), f32),
            jax.ShapeDtypeStruct((1, 2 * width), f32),
        ],
        in_specs=[pl.BlockSpec(memory_space=VMEM)] * 3,
        out_specs=[pl.BlockSpec(memory_space=VMEM)] * 4,
        compiler_params=pltpu.CompilerParams(vmem_limit_bytes=48 * MIB),
        cost_estimate=pl.CostEstimate(flops=0, bytes_accessed=4 * MIB, transcendentals=0),
        name="last_sums",
    )(got, member, columns)


def body(
    tokens,
    out_cotangent,
    level_embed,
    ada_weight,
    ada_bias,
    qkv_weight,
    qkv_bias,
    proj_weight,
    proj_bias,
    up_weight,
    up_bias,
    down_weight,
    down_bias,
    context_count,
    frame_level,
    slot_time,
):
    frames, patches, width = tokens.shape
    rows = frames * patches
    inner = up_weight.shape[1]
    frm_count, sp_count = lax.axis_size("frm"), lax.axis_size("sp")
    devices = frm_count * sp_count
    group = FRAMES // frames * sp_count
    clips = devices // group
    frm, sp = lax.axis_index("frm"), lax.axis_index("sp")
    me = frm * sp_count + sp
    clip = me // group
    clip_groups = [list(range(first, first + group)) for first in range(0, devices, group)]
    across_clips = [list(range(first, devices, group)) for first in range(group)]
    everyone = [list(range(devices))]
    halves = 2
    share = width // devices
    per_dest = inner // devices

    levels_here = level_embed.shape[0]
    embed_all = to_everyone(level_embed, devices).reshape(devices * levels_here, width)

    clip_times = lax.dynamic_slice_in_dim(slot_time, clip * FRAMES, FRAMES)
    clip_levels = lax.dynamic_index_in_dim(frame_level, clip, 0, keepdims=False)
    context = lax.dynamic_index_in_dim(context_count, clip, 0, keepdims=False)
    seen = (clip_times[None, :] <= clip_times[:, None]) | (clip_times[None, :] < context)
    visible = jnp.pad(
        jnp.where(seen, 0.0, masked_out).astype(f32), ((0, 0), (0, LANES - FRAMES))
    )

    def by_blocks(table):
        table = table.reshape(FRAMES // frames, 1, frames, LANES)
        return jnp.broadcast_to(table, (FRAMES // frames, sp_count, frames, LANES)).reshape(
            group * frames, LANES
        )

    visible = by_blocks(visible)
    freq, sign, time_lane, row_lane = rotary_lanes()
    angle_time = clip_times.astype(f32)[:, None] * freq[None, :]
    ctime = by_blocks(jnp.where(time_lane[None, :], jnp.cos(angle_time), 0.0))
    stime = by_blocks(jnp.where(time_lane[None, :], jnp.sin(angle_time) * sign[None, :], 0.0))
    patch_ids = jnp.arange(sp_count * patches, dtype=jnp.int32).reshape(sp_count, patches)
    place = jnp.where(
        row_lane[None, None, :], (patch_ids // GRID)[..., None], (patch_ids % GRID)[..., None]
    )
    angle_patch = place.astype(f32) * freq[None, None, :]
    cpatch = jnp.where(time_lane, 0.0, jnp.cos(angle_patch))
    spatch = jnp.where(time_lane, 0.0, jnp.sin(angle_patch) * sign)
    rotary = [ctime, stime, cpatch, spatch]

    def my_table(time_part, patch_part):
        mine = lax.dynamic_slice_in_dim(time_part, me % group * frames, frames)
        half = lax.dynamic_index_in_dim(patch_part, sp, 0, keepdims=False)
        return (mine[:, None, :] + half[None]).reshape(rows, LANES)

    cosine, sine = my_table(ctime, cpatch), my_table(stime, spatch)

    my_times = lax.dynamic_slice_in_dim(slot_time, frm * frames, frames)
    my_levels = jnp.take(clip_levels, my_times)
    embed_act = jax.nn.silu(embed_all.astype(f32)).astype(bf16)
    level_ids = jnp.arange(devices * levels_here, dtype=jnp.int32)
    pick = (my_levels[:, None] == level_ids[None, :]).astype(bf16)
    my_embed = dot(pick, embed_act).astype(bf16)
    frame_mod = dot(my_embed, ada_weight) + ada_bias.astype(f32)
    frame_mod = lax.reduce_precision(frame_mod, 8, 7)
    shift_one, scale_one, gate_one, shift_two, scale_two, gate_two = [
        frame_mod[:, i * width : (i + 1) * width] for i in range(6)
    ]

    hidden_turned, head_parts = project(
        tokens, shift_one, scale_one, qkv_weight, qkv_bias.astype(f32)[None, :], cosine, sine
    )
    heads = exchange(head_parts, clip_groups)

    grad_branch, grad_act = act_grad(out_cotangent, gate_two, down_weight)
    slot_ids = (jnp.arange(devices * frames, dtype=jnp.int32) // (sp_count * frames)) * frames
    slot_ids = slot_ids + jnp.arange(devices * frames, dtype=jnp.int32) % frames
    slot_levels = frame_level[slot_ids // FRAMES, slot_time[slot_ids]]
    member_of = (level_ids[:, None] == slot_levels[None, :]).astype(bf16)
    my_columns = lax.dynamic_slice_in_dim(embed_act, me * share, share, axis=1)
    which = jnp.arange(4, dtype=jnp.int32)
    member_last = jnp.where(
        (which[:, None] == which[None, :])[:, None, None, :, None],
        member_of.reshape(1, -1, devices, 1, frames),
        jnp.zeros((), bf16),
    ).reshape(4, -1, devices * 4 * frames)
    columns_turned = my_columns.T
    heads, grad_branch, grad_act, member_of, my_columns, member_last, columns_turned = (
        lax.optimization_barrier(
            (heads, grad_branch, grad_act, member_of, my_columns, member_last, columns_turned)
        )
    )
    outs, exts, attended = [], [], []
    for part in range(halves):
        out, ext = attend(heads, visible, patches, part, halves)
        outs.append(out)
        exts.append(ext)
        attended.append(exchange(out, clip_groups))

    hidden_turned, _ = lax.optimization_barrier((hidden_turned, heads))
    hidden_clip = lax.all_gather(hidden_turned, AXES, axis_index_groups=clip_groups)

    attn_low, attn_proj, after_attn, hidden_two = merge_heads(
        attended,
        proj_weight,
        proj_bias.astype(f32)[None, :],
        tokens,
        (gate_one, shift_two, scale_two),
    )
    branch, grad_hidden_two, up_b_grad, joined = feed_forward(
        hidden_two,
        grad_branch,
        grad_act,
        up_weight,
        up_bias.astype(f32)[None, :],
        down_weight,
        group,
        clips,
    )
    grad_after, grad_proj, grad_parts = unmerge_heads(
        grad_hidden_two, after_attn, out_cotangent, gate_one, scale_two, proj_weight
    )
    grads = exchange(grad_parts, clip_groups)
    block_out, early_sums, early_biases = side_sums(
        branch,
        grad_hidden_two,
        after_attn,
        attn_proj,
        out_cotangent,
        gate_two,
        down_bias.astype(f32)[None, :],
        grad_after,
        grad_proj,
        grad_branch,
    )

    joined = proj_weight_grad(attn_low, grad_proj, joined)
    joined, hidden_clip = lax.optimization_barrier((joined, hidden_clip))
    summed = joined
    for groups in (clip_groups, across_clips):
        summed = lax.psum_scatter(
            summed, AXES, scatter_dimension=0, axis_index_groups=groups, tiled=True
        )[0]
    summed = summed.astype(f32)
    quarters = inner // width
    up_w_out = jnp.concatenate([summed[i] for i in range(quarters)], axis=1)
    down_w_out = summed[quarters : 2 * quarters].reshape(per_dest, width)
    proj_w_out = summed[2 * quarters]

    def slot_parts(slot_sums, biases):
        kinds = slot_sums.shape[0] // frames
        sums = slot_sums.reshape(kinds, frames, width).transpose(1, 0, 2).reshape(frames, -1)
        sums = jnp.broadcast_to(sums.astype(bf16)[None], (devices, frames, kinds * width))
        high = biases.astype(bf16)
        low = (biases - high.astype(f32)).astype(bf16)
        both = jnp.concatenate([high, low], axis=1).reshape(devices, frames, -1)
        lanes = -(-both.shape[2] // LANES) * LANES
        both = jnp.pad(both, ((0, 0), (0, 0), (0, lanes - both.shape[2])))
        return jnp.concatenate([sums, both], axis=2)

    def bias_share(got, count, size):
        extra = jnp.sum(got[:, :, count:].astype(f32), axis=0)
        extra = extra[:, : 2 * size // frames].reshape(-1)
        return extra[:size] + extra[size:]

    def level_out(got, count):
        slots = got[:, :, :count].reshape(devices * frames, count)
        level_grad = dot(member_of, slots).astype(bf16)
        return dot(my_columns, level_grad, TN), jnp.sum(level_grad.astype(f32), axis=0)

    early_parts = slot_parts(
        early_sums,
        jnp.concatenate(
            [
                up_b_grad.reshape(devices, per_dest),
                early_biases[0].reshape(devices, share),
                early_biases[1].reshape(devices, share),
            ],
            axis=1,
        ),
    )
    early_parts, _ = lax.optimization_barrier((early_parts, grads))
    early_got = exchange(early_parts, everyone)

    first_grads, carry, mixes = attend_back(
        heads, grads, exts, outs, rotary, None, 0, False, patches
    )
    carry, early_got = lax.optimization_barrier((carry, early_got))
    own_first = exchange(first_grads, clip_groups)
    (last_grads,) = attend_back(
        heads, grads, exts, outs, rotary, (carry, mixes), 1, True, patches
    )
    last_parts, own_first = lax.optimization_barrier((last_grads, own_first))
    own_last = exchange(last_parts, clip_groups)

    early_w, early_b = level_out(early_got, 4 * width)
    early_bias_out = bias_share(early_got, 4 * width, per_dest + 2 * share)
    up_b_out = early_bias_out[:per_dest]
    proj_b_out = early_bias_out[per_dest : per_dest + share]
    down_b_out = early_bias_out[per_dest + share :]

    qkv_part, qkv_b_part = heads_grad(hidden_clip, first_grads, last_grads, devices)
    tokens_grad, last_send = finish(
        own_first, own_last, qkv_weight, tokens, scale_one, grad_after, qkv_part, qkv_b_part
    )
    last_got = exchange(last_send, everyone)
    qkv_w_out, qkv_b_all, late_w, late_b = last_sums(
        last_got, member_last, columns_turned, group, frames, width
    )
    qkv_b_out = lax.dynamic_slice_in_dim(qkv_b_all[0], me * 3 * share, 3 * share)
    ada_w_out = jnp.concatenate([late_w, early_w], axis=1)
    ada_b_all = jnp.concatenate([late_b[0], early_b])
    ada_share = ada_b_all.shape[0] // devices
    ada_b_out = lax.dynamic_slice_in_dim(ada_b_all, me * ada_share, ada_share)
    return (
        block_out,
        tokens_grad,
        ada_w_out,
        ada_b_out,
        qkv_w_out,
        qkv_b_out,
        proj_w_out,
        proj_b_out,
        up_w_out,
        up_b_out,
        down_w_out,
        down_b_out,
    )


def solution(mesh):
    tokens_spec = P("frm", "sp", None)
    rows_spec = P(AXES, None)
    vector_spec = P(AXES)
    return jax.shard_map(
        body,
        mesh=mesh,
        in_specs=(tokens_spec, tokens_spec, rows_spec) + (P(),) * 13,
        out_specs=(tokens_spec, tokens_spec) + (rows_spec, vector_spec) * 5,
        check_vma=False,
    )
```

```python
import functools
import math

import jax
import jax.numpy as jnp
import numpy as np
from jax import lax
from jax.experimental import pallas as pl
from jax.experimental.pallas import tpu as pltpu
from jax.sharding import PartitionSpec as P

HEADS = 16
HDIM = 64
FRAMES = 16
GRID = 16
LANES = 128
MIB = 2**20

norm_eps = 1e-06
masked_out = -1e30
score_scale = 0.125

f32 = jnp.float32
bf16 = jnp.bfloat16
NN = (((1,), (0,)), ((), ()))
NT = (((1,), (1,)), ((), ()))
TN = (((0,), (0,)), ((), ()))
AXES = ("frm", "sp")
VMEM = pltpu.VMEM


def dot(left_op, right_op, dims=NN):
    return lax.dot_general(left_op, right_op, dims, preferred_element_type=f32)


def exchange(value, groups):
    return lax.all_to_all(value, AXES, 0, 0, axis_index_groups=groups)


def to_everyone(value, devices):
    return exchange(
        jnp.broadcast_to(value[None], (devices,) + value.shape), [list(range(devices))]
    )


def rotary_lanes():
    lane = np.arange(LANES) % HDIM
    start = np.where(lane < 16, 0, np.where(lane < 40, 16, 40))
    half = np.where(lane < 16, 8, 12)
    offset = lane - start
    freq = np.exp((offset % half).astype(np.float32) * np.float32(-math.log(10000.0)) / half)
    sign = np.where(offset < half, -1.0, 1.0)
    return (
        freq.astype(np.float32),
        sign.astype(np.float32),
        (lane < 16),
        (lane >= 16) & (lane < 40),
    )


def rotate_lanes(value, cosine, sine):
    lane = lax.broadcasted_iota(jnp.int32, value.shape, 1) % HDIM
    near_first = pltpu.roll(value, LANES - 8, 1)
    near_second = pltpu.roll(value, 8, 1)
    far_first = pltpu.roll(value, LANES - 12, 1)
    far_second = pltpu.roll(value, 12, 1)
    in_first = (lane < 28) | ((lane >= 40) & (lane < 52))
    far = jnp.where(in_first, far_first, far_second)
    near = jnp.where(lane < 8, near_first, near_second)
    partner = jnp.where(lane < 16, near, far)
    return value * cosine + partner * sine


def project_kernel(tok_ref, shift_ref, scale_ref, wq_ref, wk_ref, wv_ref, bq_ref, bk_ref, bv_ref,
                   cos_ref, sin_ref, turned_ref, out_ref, hid_all):
    frames, patches, _ = tok_ref.shape

    @pl.when(pl.program_id(0) == 0)
    def _():
        for f in range(frames):
            here = slice(f * patches, (f + 1) * patches)
            x = tok_ref[f].astype(f32)
            centre = x - jnp.mean(x, axis=1, keepdims=True)
            inv = lax.rsqrt(jnp.mean(centre * centre, axis=1, keepdims=True) + norm_eps)
            hid = centre * inv * (1.0 + scale_ref[f : f + 1, :]) + shift_ref[f : f + 1, :]
            hid = hid.astype(bf16)
            hid_all[here, :] = hid
            turned_ref[:, here] = hid.T

    hid = hid_all[...]
    query = dot(hid, wq_ref[...]) + bq_ref[...]
    keys = dot(hid, wk_ref[...]) + bk_ref[...]
    vals = (dot(hid, wv_ref[...]) + bv_ref[...]).astype(bf16)
    for p in range(wq_ref.shape[1] // LANES):
        lanes = slice(p * LANES, (p + 1) * LANES)
        out_ref[p, 0] = rotate_lanes(query[:, lanes], cos_ref[...], sin_ref[...]).astype(bf16)
        out_ref[p, 1] = rotate_lanes(keys[:, lanes], cos_ref[...], sin_ref[...]).astype(bf16)
        out_ref[p, 2] = vals[:, lanes]


def in_hbm(value):
    return pltpu.with_memory_space_constraint(value, pltpu.HBM)


def whole(shape):
    return pl.BlockSpec(shape, lambda *_: (0,) * len(shape))


def project(tokens, shift_one, scale_one, qkv_weight, qkv_bias, cosine, sine, cols=256):
    frames, patches, width = tokens.shape
    rows = frames * patches
    pairs = width // LANES
    steps, some = width // cols, cols // LANES

    def column(part):
        return lambda c: (0, part * steps + c)

    return pl.pallas_call(
        project_kernel,
        out_shape=[
            pltpu.HBM((width, rows), bf16),
            pltpu.HBM((pairs, 3, rows, LANES), bf16),
        ],
        grid=(steps,),
        in_specs=[whole(tokens.shape), whole(shift_one.shape), whole(scale_one.shape)]
        + [pl.BlockSpec((width, cols), column(part)) for part in range(3)]
        + [pl.BlockSpec((1, cols), column(part)) for part in range(3)]
        + [whole((rows, LANES)), whole((rows, LANES))],
        out_specs=[
            whole((width, rows)),
            pl.BlockSpec((some, 3, rows, LANES), lambda c: (c, 0, 0, 0)),
        ],
        scratch_shapes=[VMEM((rows, width), bf16)],
        compiler_params=pltpu.CompilerParams(vmem_limit_bytes=40 * MIB),
        cost_estimate=pl.CostEstimate(
            flops=6 * rows * width * width, bytes_accessed=10 * MIB, transcendentals=0
        ),
        name="project",
    )(tokens, shift_one, scale_one, *[in_hbm(qkv_weight)] * 3, *[qkv_bias] * 3, cosine, sine)


def key_extra(first_frame, rows, patches):
    row = lax.broadcasted_iota(jnp.int32, (rows, LANES), 0)
    lane = lax.broadcasted_iota(jnp.int32, (rows, LANES), 1)
    hit = (lane == first_frame + row // patches) | ((lane >= FRAMES) & (lane < FRAMES + 3))
    return jnp.where(hit, 1.0, 0.0).astype(bf16)


def split_three(column):
    high = column.astype(bf16).astype(f32)
    rest = column - high
    mid = rest.astype(bf16).astype(f32)
    return high, mid, rest - mid


def attend_kernel(part, rows_part, patches, joined, joined_keys, qkv_ref, vis_ref, o_ref, ext_ref):
    blocks, _, rows, _ = qkv_ref.shape
    frames, frames_part = rows // patches, rows_part // patches
    tile, chunk = joined * rows_part, joined_keys * rows
    lane = lax.broadcasted_iota(jnp.int32, (tile, LANES), 1)
    mine_rows = slice(part * rows_part, (part + 1) * rows_part)
    ones = jnp.full((chunk, LANES), 1.0, bf16)

    def step(t, carry):
        query = jnp.concatenate(
            [qkv_ref[t * joined + i, 0, mine_rows, :] for i in range(joined)], axis=0
        )
        query = query * score_scale
        seen = jnp.concatenate(
            [
                jnp.broadcast_to(
                    vis_ref[pl.ds((t * joined + i) * frames + part * frames_part + f, 1), :],
                    (patches, LANES),
                )
                for i in range(joined)
                for f in range(frames_part)
            ],
            axis=0,
        )
        outs, ext_heads = [], []
        for h in range(2):
            mine = jnp.where((lane >= HDIM) == (h == 1), query, jnp.zeros_like(query))
            query_ext = jnp.concatenate([mine.astype(bf16), seen.astype(bf16)], axis=1)
            top = None
            for c in range(0, blocks, joined_keys):
                some_blocks = range(c, c + joined_keys)
                keys = jnp.concatenate(
                    [
                        jnp.concatenate(
                            [qkv_ref[b, 1], key_extra((b // 2) * frames, rows, patches)], axis=1
                        )
                        for b in some_blocks
                    ],
                    axis=0,
                )
                vals = jnp.concatenate([qkv_ref[b, 2] for b in some_blocks], axis=0)
                vals = jnp.concatenate([vals, ones], axis=1)
                scores = dot(query_ext, keys, NT)
                chunk_top = jnp.max(scores, axis=1, keepdims=True)
                new_top = chunk_top if top is None else jnp.maximum(top, chunk_top)
                some = dot(jnp.exp(scores - new_top).astype(bf16), vals)
                total = some if top is None else total * jnp.exp(top - new_top) + some
                top = new_top
            weight_sum = total[:, LANES : LANES + 1]
            outs.append(total[:, :LANES] / weight_sum)
            high, mid, low = split_three(-(top + jnp.log(weight_sum)))
            ext = jnp.where(lane == FRAMES, high, seen)
            ext = jnp.where(lane == FRAMES + 1, mid, ext)
            ext_heads.append(jnp.where(lane == FRAMES + 2, low, ext).astype(bf16))
        out = jnp.where(lane < HDIM, outs[0], outs[1]).astype(bf16)
        for i in range(joined):
            here = slice(i * rows_part, (i + 1) * rows_part)
            o_ref[t * joined + i] = out[here, :]
            for h in range(2):
                ext_ref[h, t * joined + i] = ext_heads[h][here, :]
        return carry

    lax.fori_loop(0, blocks // joined, step, 0)


def attend(heads, visible, patches, part, parts, tile=1024, chunk=1024):
    blocks, _, rows, _ = heads.shape
    rows_part = rows // parts
    keys = blocks * rows
    return pl.pallas_call(
        functools.partial(
            attend_kernel, part, rows_part, patches, tile // rows_part, chunk // rows
        ),
        out_shape=[
            pltpu.HBM((blocks, rows_part, LANES), bf16),
            pltpu.HBM((2, blocks, rows_part, LANES), bf16),
        ],
        in_specs=[pl.BlockSpec(memory_space=VMEM)] * 2,
        out_specs=[pl.BlockSpec(memory_space=VMEM)] * 2,
        compiler_params=pltpu.CompilerParams(vmem_limit_bytes=48 * MIB),
        cost_estimate=pl.CostEstimate(
            flops=8 * blocks * rows_part * keys * 2 * LANES,
            bytes_accessed=4 * MIB,
            transcendentals=0,
        ),
        name="attend",
    )(heads, visible)


def attend_back_kernel(parts, part, patches, joined, together, carried, last, *refs):
    at = 0

    def take(count):
        nonlocal at
        found = refs[at : at + count]
        at += count
        return found

    (qkv_ref, do_ref) = take(2)
    ext_refs, o_refs = take(parts), take(parts)
    ctime_ref, stime_ref, cpatch_ref, spatch_ref = take(4)
    if carried:
        carry_ref, mix_ref = take(2)
    if last:
        (grads_ref,) = take(1)
    else:
        grads_ref, carry_out, mix_ref = take(3)
    (dq_turned,) = refs[at:]
    blocks, _, rows, _ = qkv_ref.shape
    rows_part = rows // parts
    frames, frames_part = rows // patches, rows_part // patches
    lane = lax.broadcasted_iota(jnp.int32, (rows_part, LANES), 1)
    if carried:
        dq_turned[...] = carry_ref[...]
    else:
        dq_turned[...] = jnp.zeros_like(dq_turned)
        for b in range(blocks):
            for i in range(parts):
                there = slice(i * rows_part, (i + 1) * rows_part)
                mixed = do_ref[b, there, :].astype(f32) * o_refs[i][b].astype(f32)
                for h in range(2):
                    mine = jnp.where((lane >= HDIM) == (h == 1), mixed, 0.0)
                    high, mid, low = split_three(-jnp.sum(mine, axis=1, keepdims=True))
                    ext = jnp.where(lane == 1, mid, jnp.where(lane == 2, low, 0.0))
                    mix_ref[h, b, there, :] = jnp.where(lane == 0, high, ext).astype(bf16)
    key_rows = slice(part * rows_part, (part + 1) * rows_part)
    key_lane = lax.broadcasted_iota(jnp.int32, (together * rows_part, LANES), 1)
    mix_keys = jnp.where(key_lane < 3, 1.0, 0.0).astype(bf16)

    def back(value, row, half):
        cosine = ctime_ref[pl.ds(row, 1), :] + cpatch_ref[half]
        sine = stime_ref[pl.ds(row, 1), :] + spatch_ref[half]
        return rotate_lanes(value, cosine, -sine).astype(bf16)

    first = rows if last else 0

    def step(t, carry):
        key_blocks = [t * together + i for i in range(together)]
        keys = jnp.concatenate([qkv_ref[b, 1, key_rows, :] for b in key_blocks], axis=0)
        keys = keys * score_scale
        vals = jnp.concatenate([qkv_ref[b, 2, key_rows, :] for b in key_blocks], axis=0)
        turned = keys.astype(f32).T.astype(bf16)
        extra = jnp.concatenate(
            [
                key_extra((b // 2) * frames + part * frames_part, rows_part, patches)
                for b in key_blocks
            ],
            axis=0,
        )
        key_tiles, val_tiles = [], []
        for h in range(2):
            mine = (key_lane >= HDIM) == (h == 1)
            none = jnp.zeros_like(keys)
            key_tiles.append(
                jnp.concatenate([jnp.where(mine, keys, none).astype(bf16), extra], axis=1)
            )
            val_tiles.append(jnp.concatenate([jnp.where(mine, vals, none), mix_keys], axis=1))
        dk = [jnp.zeros((together * rows_part, LANES), f32)] * 2
        dv = [jnp.zeros((together * rows_part, LANES), f32)] * 2
        for c in range(0, blocks, joined):
            some = range(c, c + joined)
            span = slice(c * rows, (c + joined) * rows)
            query = jnp.concatenate([qkv_ref[b, 0] for b in some], axis=0)
            grad = jnp.concatenate([do_ref[b] for b in some], axis=0)
            for h in range(2):
                ext = jnp.concatenate([ext_refs[i][h, b] for b in some for i in range(parts)], axis=0)
                mix = jnp.concatenate([mix_ref[h, b] for b in some], axis=0)
                probs = jnp.exp(dot(key_tiles[h], jnp.concatenate([query, ext], axis=1), NT))
                dv[h] = dv[h] + dot(probs.astype(bf16), grad)
                moved = dot(val_tiles[h], jnp.concatenate([grad, mix], axis=1), NT)
                grad_scores = (probs * moved).astype(bf16)
                dk[h] = dk[h] + dot(grad_scores, query)
                head = slice(HDIM * h, HDIM * (h + 1))
                dq_turned[head, span] += dot(turned[head, :], grad_scores)
        dk = jnp.where(key_lane < HDIM, dk[0], dk[1]) * score_scale
        dv = jnp.where(key_lane < HDIM, dv[0], dv[1]).astype(bf16)
        for i, b in enumerate(key_blocks):
            for f in range(frames_part):
                rows_here = slice(i * rows_part + f * patches, i * rows_part + (f + 1) * patches)
                row = b * frames + part * frames_part + f
                keys_here = slice(first + f * patches, first + (f + 1) * patches)
                grads_ref[b, keys_here, :] = back(dk[rows_here, :], row, b % 2)
            grads_ref[b, first + rows_part : first + 2 * rows_part, :] = dv[
                i * rows_part : (i + 1) * rows_part, :
            ]
        return carry

    lax.fori_loop(0, blocks // together, step, 0)

    if last:
        for b in range(blocks):
            for f in range(frames):
                there = slice(b * rows + f * patches, b * rows + (f + 1) * patches)
                turned_back = back(dq_turned[:, there].T, b * frames + f, b % 2)
                grads_ref[b, f * patches : (f + 1) * patches, :] = turned_back
    else:
        carry_out[...] = dq_turned[...]


def attend_back(heads, grads, exts, outs, rotary, carry, part, last, patches, chunk=2048, together=2):
    parts = len(exts)
    blocks, _, rows, _ = heads.shape
    rows_part = rows // parts
    total = blocks * rows
    operands = [heads, grads, *exts, *outs, *rotary, *(carry or ())]
    kept = 2 * rows_part + (rows if last else 0)
    out_shape = [pltpu.HBM((blocks, kept, LANES), bf16)]
    if not last:
        out_shape.append(jax.ShapeDtypeStruct((LANES, total), f32))
        out_shape.append(jax.ShapeDtypeStruct((2, blocks, rows, LANES), bf16))
    return pl.pallas_call(
        functools.partial(
            attend_back_kernel, parts, part, patches, chunk // rows, together, carry is not None, last
        ),
        out_shape=out_shape,
        in_specs=[pl.BlockSpec(memory_space=VMEM)] * len(operands),
        out_specs=[pl.BlockSpec(memory_space=VMEM)] * len(out_shape),
        scratch_shapes=[VMEM((LANES, total), f32)],
        compiler_params=pltpu.CompilerParams(vmem_limit_bytes=56 * MIB),
        cost_estimate=pl.CostEstimate(
            flops=20 * total * blocks * rows_part * 2 * LANES,
            bytes_accessed=8 * MIB,
            transcendentals=0,
        ),
        name="attend_back",
    )(*operands)


def act_grad_kernel(cot_ref, gate_ref, down_ref, grad_ref, out_ref):
    frames, patches, _ = cot_ref.shape

    @pl.when(pl.program_id(0) == 0)
    def _():
        for f in range(frames):
            grad = gate_ref[f : f + 1, :] * cot_ref[f].astype(f32)
            grad_ref[f * patches : (f + 1) * patches, :] = grad.astype(bf16)

    out_ref[...] = dot(grad_ref[...], down_ref[...], NT)


def act_grad(cotangent, gate_two, down_weight, cols=512):
    frames, patches, width = cotangent.shape
    rows, inner = frames * patches, down_weight.shape[0]
    return pl.pallas_call(
        act_grad_kernel,
        out_shape=[
            jax.ShapeDtypeStruct((rows, width), bf16),
            pltpu.HBM((rows, inner), f32),
        ],
        grid=(inner // cols,),
        in_specs=[
            whole(cotangent.shape),
            whole(gate_two.shape),
            pl.BlockSpec((cols, width), lambda c: (c, 0)),
        ],
        out_specs=[whole((rows, width)), pl.BlockSpec((rows, cols), lambda c: (0, c))],
        compiler_params=pltpu.CompilerParams(vmem_limit_bytes=40 * MIB),
        cost_estimate=pl.CostEstimate(
            flops=2 * rows * width * inner, bytes_accessed=18 * MIB, transcendentals=0
        ),
        name="act_grad",
    )(cotangent, gate_two, down_weight)


def feed_kernel(hid_ref, grad_ref, actgrad_ref, up_ref, bias_ref, down_ref,
                branch_ref, back_ref, biasgrad_ref, joined_ref,
                hid_turned, up_slots, down_slots, up_sems, down_sems):
    step, steps = pl.program_id(0), pl.num_programs(0)
    width, cols = up_ref.shape
    group, clips, _, share, _ = joined_ref.shape
    some_clips, quarters = down_slots.shape[2:4]
    up_parts = width // cols
    slot = step % 2

    def copies(at):
        across = pl.ds(pl.multiple_of((at % up_parts) * cols, cols), cols)
        up_copy = pltpu.make_async_copy(
            up_slots.at[at % 2], joined_ref.at[:, :, at // up_parts, :, across], up_sems.at[at % 2]
        )
        down_copy = pltpu.make_async_copy(
            down_slots.at[at % 2],
            joined_ref.at[:, pl.ds(at * some_clips, some_clips), quarters : 2 * quarters],
            down_sems.at[at % 2],
        )
        return up_copy, down_copy

    @pl.when(step == 0)
    def _():
        hid_turned[...] = hid_ref[...].T

    @pl.when(step >= 2)
    def _():
        for copy in copies(step - 2):
            copy.wait()

    pre = dot(hid_ref[...], up_ref[...]) + bias_ref[...]
    square = pre * pre
    bend = jnp.tanh(pre * (0.7978845608 + (0.7978845608 * 0.044715) * square))
    half = 0.5 * (1.0 + bend)
    act = (pre * half).astype(bf16)
    slope = half + (0.5 * pre) * (1.0 - bend * bend) * (
        0.7978845608 + (0.7978845608 * 3.0 * 0.044715) * square
    )
    pre_grad = (slope * actgrad_ref[...]).astype(bf16)
    biasgrad_ref[...] = jnp.sum(pre_grad.astype(f32), axis=0, keepdims=True)
    branch = dot(act, down_ref[...])
    back = dot(pre_grad, up_ref[...], NT)
    up_grad = dot(hid_turned[...], pre_grad).astype(bf16)
    up_grad = up_grad.reshape(clips, group, share, cols)
    for c in range(clips):
        up_slots[slot, :, c] = up_grad[c]
    down_grad = dot(act.T, grad_ref[...]).astype(bf16)
    down_grad = down_grad.reshape(some_clips, group, quarters, share, width)
    for c in range(some_clips):
        down_slots[slot, :, c] = down_grad[c]

    @pl.when(step == 0)
    def _():
        branch_ref[...] = branch
        back_ref[...] = back

    @pl.when(step > 0)
    def _():
        branch_ref[...] += branch
        back_ref[...] += back

    for copy in copies(step):
        copy.start()

    @pl.when(step == steps - 1)
    def _():
        for at in (steps - 2, steps - 1):
            for copy in copies(at):
                copy.wait()


def feed_forward(hidden, grad, grad_act, up_weight, up_bias, down_weight, group, clips, cols=1024):
    rows, width = hidden.shape
    inner = up_weight.shape[1]
    share, quarters = width // (group * clips), inner // width
    some_clips = cols * clips // inner
    return pl.pallas_call(
        feed_kernel,
        out_shape=[
            jax.ShapeDtypeStruct((rows, width), f32),
            jax.ShapeDtypeStruct((rows, width), f32),
            jax.ShapeDtypeStruct((1, inner), f32),
            jax.ShapeDtypeStruct((group, clips, 2 * quarters + 1, share, width), bf16),
        ],
        grid=(inner // cols,),
        in_specs=[
            whole((rows, width)),
            whole((rows, width)),
            pl.BlockSpec((rows, cols), lambda c: (0, c)),
            pl.BlockSpec((width, cols), lambda c: (0, c)),
            pl.BlockSpec((1, cols), lambda c: (0, c)),
            pl.BlockSpec((cols, width), lambda c: (c, 0)),
        ],
        out_specs=[
            whole((rows, width)),
            whole((rows, width)),
            pl.BlockSpec((1, cols), lambda c: (0, c)),
            pl.BlockSpec(memory_space=pl.ANY),
        ],
        scratch_shapes=[
            VMEM((width, rows), bf16),
            VMEM((2, group, clips, share, cols), bf16),
            VMEM((2, group, some_clips, quarters, share, width), bf16),
            pltpu.SemaphoreType.DMA((2,)),
            pltpu.SemaphoreType.DMA((2,)),
        ],
        compiler_params=pltpu.CompilerParams(vmem_limit_bytes=58 * MIB),
        cost_estimate=pl.CostEstimate(
            flops=10 * rows * width * inner, bytes_accessed=44 * MIB, transcendentals=0
        ),
        name="feed_forward",
    )(hidden, grad, grad_act, up_weight, up_bias, down_weight)


def proj_grad_kernel(attn_ref, grad_ref, _, joined_ref):
    group, clips, _, share, width = joined_ref.shape
    grad = dot(attn_ref[...].T, grad_ref[...]).astype(bf16).reshape(clips, group, share, width)
    for c in range(clips):
        joined_ref[:, c, 0] = grad[c]


def proj_weight_grad(attn_low, grad_proj, joined):
    rows, width = attn_low.shape
    group, clips, entries, share, _ = joined.shape
    return pl.pallas_call(
        proj_grad_kernel,
        out_shape=jax.ShapeDtypeStruct(joined.shape, joined.dtype),
        grid=(1,),
        in_specs=[
            whole((rows, width)),
            whole((rows, width)),
            pl.BlockSpec(memory_space=pl.ANY),
        ],
        out_specs=pl.BlockSpec((group, clips, 1, share, width), lambda c: (0, 0, entries - 1, 0, 0)),
        input_output_aliases={2: 0},
        compiler_params=pltpu.CompilerParams(vmem_limit_bytes=40 * MIB),
        cost_estimate=pl.CostEstimate(
            flops=2 * rows * width * width, bytes_accessed=4 * MIB, transcendentals=0
        ),
        name="proj_weight_grad",
    )(attn_low, grad_proj, joined)


def merge_kernel(*refs):
    parts = len(refs) - 10
    att_refs = refs[:parts]
    (weight_ref, bias_ref, tok_ref, gate_one_ref, shift_ref, scale_ref,
     low_ref, proj_ref, after_ref, hid_ref) = refs[parts:]
    frames, patches, width = tok_ref.shape
    pairs, rows_part, _ = att_refs[0].shape
    for i, att_ref in enumerate(att_refs):
        low = jnp.concatenate([att_ref[p] for p in range(pairs)], axis=1)
        there = slice(i * rows_part, (i + 1) * rows_part)
        low_ref[there, :] = low
        proj = dot(low, weight_ref[...]) + bias_ref[...]
        proj_ref[there, :] = proj
        for j in range(rows_part // patches):
            f = i * (rows_part // patches) + j
            here = slice(f * patches, (f + 1) * patches)
            row = slice(f, f + 1)
            after = tok_ref[f].astype(f32) + gate_one_ref[row, :] * proj[
                j * patches : (j + 1) * patches, :
            ]
            after_ref[here, :] = after
            centre = after - jnp.mean(after, axis=1, keepdims=True)
            inv = lax.rsqrt(jnp.mean(centre * centre, axis=1, keepdims=True) + norm_eps)
            hid = centre * inv * (1.0 + scale_ref[row, :]) + shift_ref[row, :]
            hid_ref[here, :] = hid.astype(bf16)


def merge_heads(attended, proj_weight, proj_bias, tokens, mods):
    frames, patches, width = tokens.shape
    rows = frames * patches
    operands = [*attended, proj_weight, proj_bias, tokens, *mods]
    return pl.pallas_call(
        merge_kernel,
        out_shape=[
            jax.ShapeDtypeStruct((rows, width), bf16),
            jax.ShapeDtypeStruct((rows, width), f32),
            jax.ShapeDtypeStruct((rows, width), f32),
            pltpu.HBM((rows, width), bf16),
        ],
        in_specs=[pl.BlockSpec(memory_space=VMEM)] * len(operands),
        out_specs=[pl.BlockSpec(memory_space=VMEM)] * 4,
        compiler_params=pltpu.CompilerParams(vmem_limit_bytes=48 * MIB),
        cost_estimate=pl.CostEstimate(
            flops=2 * rows * width * width, bytes_accessed=16 * MIB, transcendentals=0
        ),
        name="merge_heads",
    )(*operands)


def column_sum(value):
    return jnp.sum(value, axis=0, keepdims=True)


def unmerge_kernel(back_ref, after_ref, cot_ref, gate_one_ref, scale_ref, weight_ref,
                   grad_ref, gproj_ref, parts_ref):
    frames, patches, width = cot_ref.shape
    for f in range(frames):
        here = slice(f * patches, (f + 1) * patches)
        row = slice(f, f + 1)
        after = after_ref[here, :]
        centre = after - jnp.mean(after, axis=1, keepdims=True)
        inv = lax.rsqrt(jnp.mean(centre * centre, axis=1, keepdims=True) + norm_eps)
        normed = centre * inv
        scaled = back_ref[here, :] * (1.0 + scale_ref[row, :])
        mean_grad = jnp.mean(scaled, axis=1, keepdims=True)
        mean_mix = jnp.mean(scaled * normed, axis=1, keepdims=True)
        grad = cot_ref[f].astype(f32) + inv * (scaled - mean_grad - normed * mean_mix)
        grad_ref[here, :] = grad
        gproj_ref[here, :] = (gate_one_ref[row, :] * grad).astype(bf16)
    step = 2 * patches
    for i in range(frames * patches // step):
        here = slice(i * step, (i + 1) * step)
        part = dot(gproj_ref[here, :], weight_ref[...], NT).astype(bf16)
        for p in range(parts_ref.shape[0]):
            parts_ref[p, here, :] = part[:, p * LANES : (p + 1) * LANES]


def unmerge_heads(back, after, cotangent, gate_one, scale_two, proj_weight):
    frames, patches, width = cotangent.shape
    rows = frames * patches
    operands = [back, after, cotangent, gate_one, scale_two, proj_weight]
    return pl.pallas_call(
        unmerge_kernel,
        out_shape=[
            pltpu.HBM((rows, width), f32),
            jax.ShapeDtypeStruct((rows, width), bf16),
            pltpu.HBM((width // LANES, rows, LANES), bf16),
        ],
        in_specs=[pl.BlockSpec(memory_space=VMEM)] * len(operands),
        out_specs=[pl.BlockSpec(memory_space=VMEM)] * 3,
        compiler_params=pltpu.CompilerParams(vmem_limit_bytes=48 * MIB),
        cost_estimate=pl.CostEstimate(
            flops=2 * rows * width * width, bytes_accessed=12 * MIB, transcendentals=0
        ),
        name="unmerge_heads",
    )(*operands)


def side_kernel(branch_ref, back_ref, after_ref, proj_ref, cot_ref, gate_two_ref, bias_ref,
                grad_ref, gproj_ref, gbranch_ref, out_ref, sums_ref, biases_ref):
    frames, patches, width = cot_ref.shape
    proj_sum = jnp.zeros((1, width), f32)
    down_sum = jnp.zeros((1, width), f32)
    for f in range(frames):
        here = slice(f * patches, (f + 1) * patches)
        cot = cot_ref[f].astype(f32)
        after = after_ref[here, :]
        branch = branch_ref[here, :] + bias_ref[...]
        out_ref[f] = (after + gate_two_ref[f : f + 1, :] * branch).astype(bf16)
        centre = after - jnp.mean(after, axis=1, keepdims=True)
        inv = lax.rsqrt(jnp.mean(centre * centre, axis=1, keepdims=True) + norm_eps)
        back = back_ref[here, :]
        for kind, term in enumerate(
            (grad_ref[here, :] * proj_ref[here, :], back, back * (centre * inv), cot * branch)
        ):
            sums_ref[kind * frames + f : kind * frames + f + 1, :] = column_sum(term)
        down_sum += column_sum(gbranch_ref[here, :].astype(f32))
        proj_sum += column_sum(gproj_ref[here, :].astype(f32))
    biases_ref[0:1, :] = proj_sum
    biases_ref[1:2, :] = down_sum


def side_sums(branch, back, after, proj, cotangent, gate_two, down_bias, grad_after, grad_proj,
              grad_branch):
    frames, patches, width = cotangent.shape
    operands = [branch, back, after, proj, cotangent, gate_two, down_bias, grad_after, grad_proj,
                grad_branch]
    return pl.pallas_call(
        side_kernel,
        out_shape=[
            jax.ShapeDtypeStruct((frames, patches, width), bf16),
            jax.ShapeDtypeStruct((4 * frames, width), f32),
            jax.ShapeDtypeStruct((2, width), f32),
        ],
        in_specs=[pl.BlockSpec(memory_space=VMEM)] * len(operands),
        out_specs=[pl.BlockSpec(memory_space=VMEM)] * 3,
        compiler_params=pltpu.CompilerParams(vmem_limit_bytes=48 * MIB),
        cost_estimate=pl.CostEstimate(flops=0, bytes_accessed=16 * MIB, transcendentals=0),
        name="side_sums",
    )(*operands)


def heads_grad_kernel(hid_ref, first_ref, last_ref, out_ref, bias_ref, total):
    rows = hid_ref.shape[2]
    rows_part = first_ref.shape[1] // 2
    grad = jnp.concatenate(
        [
            last_ref[0, :rows, :],
            jnp.concatenate(
                [first_ref[0, :rows_part, :], last_ref[0, rows : rows + rows_part, :]], axis=0
            ),
            jnp.concatenate([first_ref[0, rows_part:, :], last_ref[0, rows + rows_part :, :]], axis=0),
        ],
        axis=1,
    )
    some = dot(hid_ref[0], grad)
    some_bias = column_sum(grad.astype(f32))

    @pl.when(pl.program_id(0) == 0)
    def _():
        total[...] = some
        bias_ref[...] = some_bias

    @pl.when(pl.program_id(0) > 0)
    def _():
        total[...] += some
        bias_ref[...] += some_bias

    @pl.when(pl.program_id(0) == pl.num_programs(0) - 1)
    def _():
        devices, triple, _ = out_ref.shape
        share = triple // 3
        for k in range(3):
            part = total[:, k * LANES : (k + 1) * LANES].astype(bf16)
            out_ref[:, k * share : (k + 1) * share, :] = part.reshape(devices, share, LANES)


def heads_grad(hidden_clip, first, last, devices):
    blocks, width, rows = hidden_clip.shape
    shape = (devices, 3 * width // devices, LANES)
    return pl.pallas_call(
        heads_grad_kernel,
        out_shape=[
            jax.ShapeDtypeStruct(shape, bf16),
            jax.ShapeDtypeStruct((1, 3 * LANES), f32),
        ],
        grid=(blocks,),
        in_specs=[
            pl.BlockSpec((1, width, rows), lambda b: (b, 0, 0)),
            pl.BlockSpec((1,) + first.shape[1:], lambda b: (b, 0, 0)),
            pl.BlockSpec((1,) + last.shape[1:], lambda b: (b, 0, 0)),
        ],
        out_specs=[whole(shape), whole((1, 3 * LANES))],
        scratch_shapes=[VMEM((width, 3 * LANES), f32)],
        compiler_params=pltpu.CompilerParams(vmem_limit_bytes=40 * MIB),
        cost_estimate=pl.CostEstimate(
            flops=6 * blocks * rows * width * LANES, bytes_accessed=12 * MIB, transcendentals=0
        ),
        name="heads_grad",
    )(in_hbm(hidden_clip), first, last)


def finish_kernel(first_ref, last_ref, wq_ref, wk_ref, wv_ref, tok_ref, scale_ref, after_ref,
                  partbias_ref, out_ref, send_ref, total):
    frames, patches, width = tok_ref.shape
    rows = frames * patches
    rows_part = first_ref.shape[1] // 2
    step = pl.program_id(0)
    query, keys, vals = [], [], []
    for p in range(first_ref.shape[0]):
        query.append(last_ref[p, :rows, :])
        keys.append(
            jnp.concatenate(
                [first_ref[p, :rows_part, :], last_ref[p, rows : rows + rows_part, :]], axis=0
            )
        )
        vals.append(
            jnp.concatenate([first_ref[p, rows_part:, :], last_ref[p, rows + rows_part :, :]], axis=0)
        )
    some = None
    for grads, weight_ref in ((query, wq_ref), (keys, wk_ref), (vals, wv_ref)):
        term = dot(jnp.concatenate(grads, axis=1), weight_ref[...], NT)
        some = term if some is None else some + term

    @pl.when(step == 0)
    def _():
        total[...] = some

    @pl.when(step > 0)
    def _():
        total[...] += some

    @pl.when(step == pl.num_programs(0) - 1)
    def _():
        shift_sums, scale_sums = [], []
        for f in range(frames):
            here = slice(f * patches, (f + 1) * patches)
            x = tok_ref[f].astype(f32)
            centre = x - jnp.mean(x, axis=1, keepdims=True)
            inv = lax.rsqrt(jnp.mean(centre * centre, axis=1, keepdims=True) + norm_eps)
            normed = centre * inv
            back = total[here, :]
            shift_sums.append(column_sum(back))
            scale_sums.append(column_sum(back * normed))
            scaled = back * (1.0 + scale_ref[f : f + 1, :])
            mean_grad = jnp.mean(scaled, axis=1, keepdims=True)
            mean_mix = jnp.mean(scaled * normed, axis=1, keepdims=True)
            grad = after_ref[here, :] + inv * (scaled - mean_grad - normed * mean_mix)
            out_ref[f] = grad.astype(bf16)
        sums = jnp.concatenate(shift_sums + scale_sums, axis=0)
        sums = jnp.concatenate(
            [sums[:, i : i + LANES] for i in range(0, width, LANES)], axis=0
        ).astype(bf16)
        bias = [partbias_ref[:, k * LANES : (k + 1) * LANES] for k in range(3)]
        high = [value.astype(bf16).astype(f32) for value in bias]
        low = [value - upper for value, upper in zip(bias, high)]
        bias = jnp.concatenate(high + low + [jnp.zeros((10, LANES), f32)], axis=0).astype(bf16)
        count = sums.shape[0]
        for d in range(send_ref.shape[0]):
            send_ref[d, :count, :] = sums
            send_ref[d, count:, :] = bias


def finish(first, last, qkv_weight, tokens, scale_one, grad_after, part_bias, copies, cols=256):
    frames, patches, width = tokens.shape
    rows = frames * patches
    steps, some = width // cols, cols // LANES

    send_shape = (copies, 2 * frames * (width // LANES) + 16, LANES)

    def column(third):
        return lambda c: (0, third * steps + c)

    return pl.pallas_call(
        finish_kernel,
        out_shape=[
            jax.ShapeDtypeStruct((frames, patches, width), bf16),
            pltpu.HBM(send_shape, bf16),
        ],
        grid=(steps,),
        in_specs=[
            pl.BlockSpec((some,) + first.shape[1:], lambda c: (c, 0, 0)),
            pl.BlockSpec((some,) + last.shape[1:], lambda c: (c, 0, 0)),
        ]
        + [pl.BlockSpec((width, cols), column(part)) for part in range(3)]
        + [whole(tokens.shape), whole(scale_one.shape), whole((rows, width))]
        + [whole(part_bias.shape)],
        out_specs=[whole((frames, patches, width)), whole(send_shape)],
        scratch_shapes=[VMEM((rows, width), f32)],
        compiler_params=pltpu.CompilerParams(vmem_limit_bytes=48 * MIB),
        cost_estimate=pl.CostEstimate(
            flops=6 * rows * width * width, bytes_accessed=16 * MIB, transcendentals=0
        ),
        name="finish",
    )(first, last, *[qkv_weight] * 3, tokens, scale_one, grad_after, part_bias)


def last_kernel(clips, frames, got_ref, member_ref, cols_ref, early_ref, earlysum_ref,
                rows_ref, bias_ref, ada_ref, adasum_ref):
    group = got_ref.shape[0]
    share, width = rows_ref.shape[0], rows_ref.shape[1] // 3
    tiles = width // LANES
    count = 2 * frames * tiles
    starts = [3 * share + c * (count + 16) for c in range(clips)]
    some = 4 * frames
    ada_ref[:, 2 * width :] = early_ref[...]
    adasum_ref[:, 2 * width :] = earlysum_ref[...]
    for i in range(tiles // 2):
        sums = jnp.concatenate(
            [
                got_ref[:, at + i * some : at + (i + 1) * some, :].reshape(group * some, LANES)
                for at in starts
            ],
            axis=0,
        )
        for j in range(2):
            for kind in range(2):
                level = dot(member_ref[2 * j + kind], sums).astype(bf16)
                at = kind * width + (2 * i + j) * LANES
                ada_ref[:, at : at + LANES] = dot(cols_ref[...], level)
                adasum_ref[:, at : at + LANES] = column_sum(level.astype(f32))
    for p in range(group):
        bias = None
        for at in starts:
            term = got_ref[p, at + count : at + count + 16, :].astype(f32)
            bias = term if bias is None else bias + term
        for third in range(3):
            at = third * width + p * LANES
            here = slice(third * share, (third + 1) * share)
            rows_ref[:, at : at + LANES] = got_ref[p, here, :].astype(f32)
            bias_ref[:, at : at + LANES] = bias[third : third + 1, :] + bias[third + 3 : third + 4, :]


def last_sums(got, member, columns, early, early_sum, clips, frames):
    share, width = early.shape[0], early.shape[1] // 4
    return pl.pallas_call(
        functools.partial(last_kernel, clips, frames),
        out_shape=[
            jax.ShapeDtypeStruct((share, 3 * width), f32),
            jax.ShapeDtypeStruct((1, 3 * width), f32),
            jax.ShapeDtypeStruct((share, 6 * width), f32),
            jax.ShapeDtypeStruct((1, 6 * width), f32),
        ],
        in_specs=[pl.BlockSpec(memory_space=VMEM)] * 5,
        out_specs=[pl.BlockSpec(memory_space=VMEM)] * 4,
        compiler_params=pltpu.CompilerParams(vmem_limit_bytes=48 * MIB),
        cost_estimate=pl.CostEstimate(flops=0, bytes_accessed=4 * MIB, transcendentals=0),
        name="last_sums",
    )(got, member, columns, early, early_sum)


def body(
    tokens,
    out_cotangent,
    level_embed,
    ada_weight,
    ada_bias,
    qkv_weight,
    qkv_bias,
    proj_weight,
    proj_bias,
    up_weight,
    up_bias,
    down_weight,
    down_bias,
    context_count,
    frame_level,
    slot_time,
):
    frames, patches, width = tokens.shape
    rows = frames * patches
    inner = up_weight.shape[1]
    frm_count, sp_count = lax.axis_size("frm"), lax.axis_size("sp")
    devices = frm_count * sp_count
    group = FRAMES // frames * sp_count
    clips = devices // group
    frm, sp = lax.axis_index("frm"), lax.axis_index("sp")
    me = frm * sp_count + sp
    clip = me // group
    clip_groups = [list(range(first, first + group)) for first in range(0, devices, group)]
    across_clips = [list(range(first, devices, group)) for first in range(group)]
    everyone = [list(range(devices))]
    halves = 2
    share = width // devices
    per_dest = inner // devices

    levels_here = level_embed.shape[0]
    embed_all = to_everyone(level_embed, devices).reshape(devices * levels_here, width)

    clip_times = lax.dynamic_slice_in_dim(slot_time, clip * FRAMES, FRAMES)
    clip_levels = lax.dynamic_index_in_dim(frame_level, clip, 0, keepdims=False)
    context = lax.dynamic_index_in_dim(context_count, clip, 0, keepdims=False)
    seen = (clip_times[None, :] <= clip_times[:, None]) | (clip_times[None, :] < context)
    visible = jnp.pad(
        jnp.where(seen, 0.0, masked_out).astype(f32), ((0, 0), (0, LANES - FRAMES))
    )

    def by_blocks(table):
        table = table.reshape(FRAMES // frames, 1, frames, LANES)
        return jnp.broadcast_to(table, (FRAMES // frames, sp_count, frames, LANES)).reshape(
            group * frames, LANES
        )

    visible = by_blocks(visible)
    freq, sign, time_lane, row_lane = rotary_lanes()
    angle_time = clip_times.astype(f32)[:, None] * freq[None, :]
    ctime = by_blocks(jnp.where(time_lane[None, :], jnp.cos(angle_time), 0.0))
    stime = by_blocks(jnp.where(time_lane[None, :], jnp.sin(angle_time) * sign[None, :], 0.0))
    patch_ids = jnp.arange(sp_count * patches, dtype=jnp.int32).reshape(sp_count, patches)
    place = jnp.where(
        row_lane[None, None, :], (patch_ids // GRID)[..., None], (patch_ids % GRID)[..., None]
    )
    angle_patch = place.astype(f32) * freq[None, None, :]
    cpatch = jnp.where(time_lane, 0.0, jnp.cos(angle_patch))
    spatch = jnp.where(time_lane, 0.0, jnp.sin(angle_patch) * sign)
    rotary = [ctime, stime, cpatch, spatch]

    def my_table(time_part, patch_part):
        mine = lax.dynamic_slice_in_dim(time_part, me % group * frames, frames)
        half = lax.dynamic_index_in_dim(patch_part, sp, 0, keepdims=False)
        return (mine[:, None, :] + half[None]).reshape(rows, LANES)

    cosine, sine = my_table(ctime, cpatch), my_table(stime, spatch)

    my_times = lax.dynamic_slice_in_dim(slot_time, frm * frames, frames)
    my_levels = jnp.take(clip_levels, my_times)
    embed_act = jax.nn.silu(embed_all.astype(f32)).astype(bf16)
    level_ids = jnp.arange(devices * levels_here, dtype=jnp.int32)
    pick = (my_levels[:, None] == level_ids[None, :]).astype(bf16)
    my_embed = dot(pick, embed_act).astype(bf16)
    frame_mod = dot(my_embed, ada_weight) + ada_bias.astype(f32)
    frame_mod = lax.reduce_precision(frame_mod, 8, 7)
    shift_one, scale_one, gate_one, shift_two, scale_two, gate_two = [
        frame_mod[:, i * width : (i + 1) * width] for i in range(6)
    ]

    hidden_turned, head_parts = project(
        tokens, shift_one, scale_one, qkv_weight, qkv_bias.astype(f32)[None, :], cosine, sine
    )
    heads = exchange(head_parts, clip_groups)

    grad_branch, grad_act = act_grad(out_cotangent, gate_two, down_weight)
    slot_ids = (jnp.arange(devices * frames, dtype=jnp.int32) // (sp_count * frames)) * frames
    slot_ids = slot_ids + jnp.arange(devices * frames, dtype=jnp.int32) % frames
    slot_levels = frame_level[slot_ids // FRAMES, slot_time[slot_ids]]
    member_of = (level_ids[:, None] == slot_levels[None, :]).astype(bf16)
    my_columns = lax.dynamic_slice_in_dim(embed_act, me * share, share, axis=1)
    which = jnp.arange(4, dtype=jnp.int32)
    member_last = jnp.where(
        (which[:, None] == which[None, :])[:, None, None, :, None],
        member_of.reshape(1, -1, devices, 1, frames),
        jnp.zeros((), bf16),
    ).reshape(4, -1, devices * 4 * frames)
    columns_turned = my_columns.T
    heads, grad_branch, grad_act, member_of, my_columns, member_last, columns_turned = (
        lax.optimization_barrier(
            (heads, grad_branch, grad_act, member_of, my_columns, member_last, columns_turned)
        )
    )
    outs, exts, attended = [], [], []
    for part in range(halves):
        out, ext = attend(heads, visible, patches, part, halves)
        outs.append(out)
        exts.append(ext)
        attended.append(exchange(out, clip_groups))

    hidden_turned, _ = lax.optimization_barrier((hidden_turned, heads))
    hidden_clip = lax.all_gather(hidden_turned, AXES, axis_index_groups=clip_groups)

    attn_low, attn_proj, after_attn, hidden_two = merge_heads(
        attended,
        proj_weight,
        proj_bias.astype(f32)[None, :],
        tokens,
        (gate_one, shift_two, scale_two),
    )
    branch, grad_hidden_two, up_b_grad, joined = feed_forward(
        hidden_two,
        grad_branch,
        grad_act,
        up_weight,
        up_bias.astype(f32)[None, :],
        down_weight,
        group,
        clips,
    )
    grad_after, grad_proj, grad_parts = unmerge_heads(
        grad_hidden_two, after_attn, out_cotangent, gate_one, scale_two, proj_weight
    )
    grads = exchange(grad_parts, clip_groups)
    block_out, early_sums, early_biases = side_sums(
        branch,
        grad_hidden_two,
        after_attn,
        attn_proj,
        out_cotangent,
        gate_two,
        down_bias.astype(f32)[None, :],
        grad_after,
        grad_proj,
        grad_branch,
    )

    joined = proj_weight_grad(attn_low, grad_proj, joined)
    joined, hidden_clip = lax.optimization_barrier((joined, hidden_clip))
    summed = lax.psum_scatter(
        joined, AXES, scatter_dimension=0, axis_index_groups=clip_groups, tiled=True
    )[0]

    def slot_parts(slot_sums, biases):
        kinds = slot_sums.shape[0] // frames
        sums = slot_sums.reshape(kinds, frames, width).transpose(1, 0, 2).reshape(frames, -1)
        sums = jnp.broadcast_to(sums.astype(bf16)[None], (devices, frames, kinds * width))
        high = biases.astype(bf16)
        low = (biases - high.astype(f32)).astype(bf16)
        both = jnp.concatenate([high, low], axis=1).reshape(devices, frames, -1)
        lanes = -(-both.shape[2] // LANES) * LANES
        both = jnp.pad(both, ((0, 0), (0, 0), (0, lanes - both.shape[2])))
        return jnp.concatenate([sums, both], axis=2)

    def bias_share(got, count, size):
        extra = jnp.sum(got[:, :, count:].astype(f32), axis=0)
        extra = extra[:, : 2 * size // frames].reshape(-1)
        return extra[:size] + extra[size:]

    def level_out(got, count):
        slots = got[:, :, :count].reshape(devices * frames, count)
        level_grad = dot(member_of, slots).astype(bf16)
        return dot(my_columns, level_grad, TN), jnp.sum(level_grad.astype(f32), axis=0)

    early_parts = slot_parts(
        early_sums,
        jnp.concatenate(
            [
                up_b_grad.reshape(devices, per_dest),
                early_biases[0].reshape(devices, share),
                early_biases[1].reshape(devices, share),
            ],
            axis=1,
        ),
    )
    early_parts, _ = lax.optimization_barrier((early_parts, grads))
    early_got = exchange(early_parts, everyone)

    first_grads, carry, mixes = attend_back(
        heads, grads, exts, outs, rotary, None, 0, False, patches
    )
    carry, early_got = lax.optimization_barrier((carry, early_got))
    own_first = exchange(first_grads, clip_groups)
    (last_grads,) = attend_back(
        heads, grads, exts, outs, rotary, (carry, mixes), 1, True, patches
    )
    last_parts, own_first = lax.optimization_barrier((last_grads, own_first))
    own_last = exchange(last_parts, clip_groups)

    early_w, early_b = level_out(early_got, 4 * width)
    early_bias_out = bias_share(early_got, 4 * width, per_dest + 2 * share)

    qkv_part, qkv_b_part = heads_grad(hidden_clip, first_grads, last_grads, devices)
    qkv_part = qkv_part.reshape(clips, group, 3 * share, LANES)
    qkv_sum = lax.dynamic_index_in_dim(qkv_part, clip, 0, keepdims=False).astype(f32)
    for j in range(1, clips):
        some = lax.dynamic_index_in_dim(qkv_part, clip ^ j, 0, keepdims=False)
        pairs = [(source, source ^ (j * group)) for source in range(devices)]
        qkv_sum = qkv_sum + lax.ppermute(some, AXES, pairs).astype(f32)
    qkv_sum, own_last, summed = lax.optimization_barrier(
        (qkv_sum.astype(bf16), own_last, summed)
    )

    summed = lax.psum_scatter(
        summed, AXES, scatter_dimension=0, axis_index_groups=across_clips, tiled=True
    )[0].astype(f32)
    quarters = inner // width
    up_w_out = jnp.concatenate([summed[i] for i in range(quarters)], axis=1)
    down_w_out = summed[quarters : 2 * quarters].reshape(per_dest, width)
    proj_w_out = summed[2 * quarters]

    tokens_grad, last_send = finish(
        own_first, own_last, qkv_weight, tokens, scale_one, grad_after, qkv_b_part, clips
    )
    clip_got = exchange(last_send, across_clips).reshape(1, -1, LANES)
    clip_got = jnp.broadcast_to(clip_got, (group,) + clip_got.shape[1:])
    last_got = exchange(jnp.concatenate([qkv_sum, clip_got], axis=1), clip_groups)
    last_got, early_w, early_b, early_bias_out = lax.optimization_barrier(
        (last_got, early_w, early_b, early_bias_out)
    )
    up_b_out = early_bias_out[:per_dest]
    proj_b_out = early_bias_out[per_dest : per_dest + share]
    down_b_out = early_bias_out[per_dest + share :]
    qkv_w_out, qkv_b_all, ada_w_out, ada_b_all = last_sums(
        last_got, member_last, columns_turned, early_w, early_b[None, :], clips, frames
    )
    qkv_b_out = lax.dynamic_slice_in_dim(qkv_b_all[0], me * 3 * share, 3 * share)
    ada_b_all = ada_b_all[0]
    ada_share = ada_b_all.shape[0] // devices
    ada_b_out = lax.dynamic_slice_in_dim(ada_b_all, me * ada_share, ada_share)
    return (
        block_out,
        tokens_grad,
        ada_w_out,
        ada_b_out,
        qkv_w_out,
        qkv_b_out,
        proj_w_out,
        proj_b_out,
        up_w_out,
        up_b_out,
        down_w_out,
        down_b_out,
    )


def solution(mesh):
    tokens_spec = P("frm", "sp", None)
    rows_spec = P(AXES, None)
    vector_spec = P(AXES)
    return jax.shard_map(
        body,
        mesh=mesh,
        in_specs=(tokens_spec, tokens_spec, rows_spec) + (P(),) * 13,
        out_specs=(tokens_spec, tokens_spec) + (rows_spec, vector_spec) * 5,
        check_vma=False,
    )
```

```python
import functools
import math

import jax
import jax.numpy as jnp
import numpy as np
from jax import lax
from jax.experimental import pallas as pl
from jax.experimental.pallas import tpu as pltpu
from jax.sharding import PartitionSpec as P

HEADS = 16
HDIM = 64
FRAMES = 16
GRID = 16
LANES = 128
MIB = 2**20

norm_eps = 1e-06
masked_out = -1e30
score_scale = 0.125

f32 = jnp.float32
bf16 = jnp.bfloat16
NN = (((1,), (0,)), ((), ()))
NT = (((1,), (1,)), ((), ()))
TN = (((0,), (0,)), ((), ()))
AXES = ("frm", "sp")
VMEM = pltpu.VMEM


def dot(left_op, right_op, dims=NN):
    return lax.dot_general(left_op, right_op, dims, preferred_element_type=f32)


def exchange(value, groups):
    return lax.all_to_all(value, AXES, 0, 0, axis_index_groups=groups)


def to_everyone(value, devices):
    return exchange(
        jnp.broadcast_to(value[None], (devices,) + value.shape), [list(range(devices))]
    )


def rotary_lanes():
    lane = np.arange(LANES) % HDIM
    start = np.where(lane < 16, 0, np.where(lane < 40, 16, 40))
    half = np.where(lane < 16, 8, 12)
    offset = lane - start
    freq = np.exp((offset % half).astype(np.float32) * np.float32(-math.log(10000.0)) / half)
    sign = np.where(offset < half, -1.0, 1.0)
    return (
        freq.astype(np.float32),
        sign.astype(np.float32),
        (lane < 16),
        (lane >= 16) & (lane < 40),
    )


def rotate_lanes(value, cosine, sine):
    lane = lax.broadcasted_iota(jnp.int32, value.shape, 1) % HDIM
    near_first = pltpu.roll(value, LANES - 8, 1)
    near_second = pltpu.roll(value, 8, 1)
    far_first = pltpu.roll(value, LANES - 12, 1)
    far_second = pltpu.roll(value, 12, 1)
    in_first = (lane < 28) | ((lane >= 40) & (lane < 52))
    far = jnp.where(in_first, far_first, far_second)
    near = jnp.where(lane < 8, near_first, near_second)
    partner = jnp.where(lane < 16, near, far)
    return value * cosine + partner * sine


def project_kernel(tok_ref, shift_ref, scale_ref, wq_ref, wk_ref, wv_ref, bq_ref, bk_ref, bv_ref,
                   cos_ref, sin_ref, turned_ref, out_ref, hid_all):
    frames, patches, _ = tok_ref.shape

    @pl.when(pl.program_id(0) == 0)
    def _():
        for f in range(frames):
            here = slice(f * patches, (f + 1) * patches)
            x = tok_ref[f].astype(f32)
            centre = x - jnp.mean(x, axis=1, keepdims=True)
            inv = lax.rsqrt(jnp.mean(centre * centre, axis=1, keepdims=True) + norm_eps)
            hid = centre * inv * (1.0 + scale_ref[f : f + 1, :]) + shift_ref[f : f + 1, :]
            hid = hid.astype(bf16)
            hid_all[here, :] = hid
            turned_ref[:, here] = hid.T

    hid = hid_all[...]
    query = dot(hid, wq_ref[...]) + bq_ref[...]
    keys = dot(hid, wk_ref[...]) + bk_ref[...]
    vals = (dot(hid, wv_ref[...]) + bv_ref[...]).astype(bf16)
    for p in range(wq_ref.shape[1] // LANES):
        lanes = slice(p * LANES, (p + 1) * LANES)
        out_ref[p, 0] = rotate_lanes(query[:, lanes], cos_ref[...], sin_ref[...]).astype(bf16)
        out_ref[p, 1] = rotate_lanes(keys[:, lanes], cos_ref[...], sin_ref[...]).astype(bf16)
        out_ref[p, 2] = vals[:, lanes]


def in_hbm(value):
    return pltpu.with_memory_space_constraint(value, pltpu.HBM)


def whole(shape):
    return pl.BlockSpec(shape, lambda *_: (0,) * len(shape))


def project(tokens, shift_one, scale_one, qkv_weight, qkv_bias, cosine, sine, cols=256):
    frames, patches, width = tokens.shape
    rows = frames * patches
    pairs = width // LANES
    steps, some = width // cols, cols // LANES

    def column(part):
        return lambda c: (0, part * steps + c)

    return pl.pallas_call(
        project_kernel,
        out_shape=[
            pltpu.HBM((width, rows), bf16),
            pltpu.HBM((pairs, 3, rows, LANES), bf16),
        ],
        grid=(steps,),
        in_specs=[whole(tokens.shape), whole(shift_one.shape), whole(scale_one.shape)]
        + [pl.BlockSpec((width, cols), column(part)) for part in range(3)]
        + [pl.BlockSpec((1, cols), column(part)) for part in range(3)]
        + [whole((rows, LANES)), whole((rows, LANES))],
        out_specs=[
            whole((width, rows)),
            pl.BlockSpec((some, 3, rows, LANES), lambda c: (c, 0, 0, 0)),
        ],
        scratch_shapes=[VMEM((rows, width), bf16)],
        compiler_params=pltpu.CompilerParams(vmem_limit_bytes=40 * MIB),
        cost_estimate=pl.CostEstimate(
            flops=6 * rows * width * width, bytes_accessed=10 * MIB, transcendentals=0
        ),
        name="project",
    )(tokens, shift_one, scale_one, *[in_hbm(qkv_weight)] * 3, *[qkv_bias] * 3, cosine, sine)


def key_extra(first_frame, rows, patches):
    row = lax.broadcasted_iota(jnp.int32, (rows, LANES), 0)
    lane = lax.broadcasted_iota(jnp.int32, (rows, LANES), 1)
    hit = (lane == first_frame + row // patches) | ((lane >= FRAMES) & (lane < FRAMES + 3))
    return jnp.where(hit, 1.0, 0.0).astype(bf16)


def split_three(column):
    high = column.astype(bf16).astype(f32)
    rest = column - high
    mid = rest.astype(bf16).astype(f32)
    return high, mid, rest - mid


def attend_kernel(first, rows_part, patches, joined, joined_keys, qkv_ref, vis_ref, o_ref, ext_ref):
    blocks, _, rows, _ = qkv_ref.shape
    frames, frames_part = rows // patches, rows_part // patches
    tile, chunk = joined * rows_part, joined_keys * rows
    lane = lax.broadcasted_iota(jnp.int32, (tile, LANES), 1)
    mine_rows = slice(first * patches, first * patches + rows_part)
    ones = jnp.full((chunk, LANES), 1.0, bf16)

    def step(t, carry):
        query = jnp.concatenate(
            [qkv_ref[t * joined + i, 0, mine_rows, :] for i in range(joined)], axis=0
        )
        query = query * score_scale
        seen = jnp.concatenate(
            [
                jnp.broadcast_to(
                    vis_ref[pl.ds((t * joined + i) * frames + first + f, 1), :],
                    (patches, LANES),
                )
                for i in range(joined)
                for f in range(frames_part)
            ],
            axis=0,
        )
        outs, ext_heads = [], []
        for h in range(2):
            mine = jnp.where((lane >= HDIM) == (h == 1), query, jnp.zeros_like(query))
            query_ext = jnp.concatenate([mine.astype(bf16), seen.astype(bf16)], axis=1)
            top = None
            for c in range(0, blocks, joined_keys):
                some_blocks = range(c, c + joined_keys)
                keys = jnp.concatenate(
                    [
                        jnp.concatenate(
                            [qkv_ref[b, 1], key_extra((b // 2) * frames, rows, patches)], axis=1
                        )
                        for b in some_blocks
                    ],
                    axis=0,
                )
                vals = jnp.concatenate([qkv_ref[b, 2] for b in some_blocks], axis=0)
                vals = jnp.concatenate([vals, ones], axis=1)
                scores = dot(query_ext, keys, NT)
                chunk_top = jnp.max(scores, axis=1, keepdims=True)
                new_top = chunk_top if top is None else jnp.maximum(top, chunk_top)
                some = dot(jnp.exp(scores - new_top).astype(bf16), vals)
                total = some if top is None else total * jnp.exp(top - new_top) + some
                top = new_top
            weight_sum = total[:, LANES : LANES + 1]
            outs.append(total[:, :LANES] / weight_sum)
            high, mid, low = split_three(-(top + jnp.log(weight_sum)))
            ext = jnp.where(lane == FRAMES, high, seen)
            ext = jnp.where(lane == FRAMES + 1, mid, ext)
            ext_heads.append(jnp.where(lane == FRAMES + 2, low, ext).astype(bf16))
        out = jnp.where(lane < HDIM, outs[0], outs[1]).astype(bf16)
        for i in range(joined):
            here = slice(i * rows_part, (i + 1) * rows_part)
            o_ref[t * joined + i] = out[here, :]
            for h in range(2):
                ext_ref[h, t * joined + i] = ext_heads[h][here, :]
        return carry

    lax.fori_loop(0, blocks // joined, step, 0)


def attend(heads, visible, patches, first, frames_part, tile=1024, chunk=1024):
    blocks, _, rows, _ = heads.shape
    rows_part = frames_part * patches
    keys = blocks * rows
    joined = blocks
    while joined * rows_part > tile:
        joined //= 2
    return pl.pallas_call(
        functools.partial(
            attend_kernel, first, rows_part, patches, joined, chunk // rows
        ),
        out_shape=[
            pltpu.HBM((blocks, rows_part, LANES), bf16),
            pltpu.HBM((2, blocks, rows_part, LANES), bf16),
        ],
        in_specs=[pl.BlockSpec(memory_space=VMEM)] * 2,
        out_specs=[pl.BlockSpec(memory_space=VMEM)] * 2,
        compiler_params=pltpu.CompilerParams(vmem_limit_bytes=48 * MIB),
        cost_estimate=pl.CostEstimate(
            flops=8 * blocks * rows_part * keys * 2 * LANES,
            bytes_accessed=4 * MIB,
            transcendentals=0,
        ),
        name="attend",
    )(heads, visible)


def attend_back_kernel(parts, query_parts, part, patches, joined, together, carried, last, *refs):
    at = 0

    def take(count):
        nonlocal at
        found = refs[at : at + count]
        at += count
        return found

    (qkv_ref, do_ref) = take(2)
    ext_refs, o_refs = take(query_parts), take(query_parts)
    ctime_ref, stime_ref, cpatch_ref, spatch_ref = take(4)
    if carried:
        carry_ref, mix_ref = take(2)
    if last:
        (grads_ref,) = take(1)
    else:
        grads_ref, carry_out, mix_ref = take(3)
    (dq_turned,) = refs[at:]
    blocks, _, rows, _ = qkv_ref.shape
    rows_part = rows // parts
    frames, frames_part = rows // patches, rows_part // patches
    if carried:
        dq_turned[...] = carry_ref[...]
    else:
        dq_turned[...] = jnp.zeros_like(dq_turned)
        for b in range(blocks):
            at = 0
            for o_ref in o_refs:
                size = o_ref.shape[1]
                there = slice(at, at + size)
                at += size
                lane = lax.broadcasted_iota(jnp.int32, (size, LANES), 1)
                mixed = do_ref[b, there, :].astype(f32) * o_ref[b].astype(f32)
                for h in range(2):
                    mine = jnp.where((lane >= HDIM) == (h == 1), mixed, 0.0)
                    high, mid, low = split_three(-jnp.sum(mine, axis=1, keepdims=True))
                    ext = jnp.where(lane == 1, mid, jnp.where(lane == 2, low, 0.0))
                    mix_ref[h, b, there, :] = jnp.where(lane == 0, high, ext).astype(bf16)
    key_rows = slice(part * rows_part, (part + 1) * rows_part)
    key_lane = lax.broadcasted_iota(jnp.int32, (together * rows_part, LANES), 1)
    mix_keys = jnp.where(key_lane < 3, 1.0, 0.0).astype(bf16)

    def back(value, row, half):
        cosine = ctime_ref[pl.ds(row, 1), :] + cpatch_ref[half]
        sine = stime_ref[pl.ds(row, 1), :] + spatch_ref[half]
        return rotate_lanes(value, cosine, -sine).astype(bf16)

    first = rows if last else 0

    def step(t, carry):
        key_blocks = [t * together + i for i in range(together)]
        keys = jnp.concatenate([qkv_ref[b, 1, key_rows, :] for b in key_blocks], axis=0)
        keys = keys * score_scale
        vals = jnp.concatenate([qkv_ref[b, 2, key_rows, :] for b in key_blocks], axis=0)
        turned = keys.astype(f32).T.astype(bf16)
        extra = jnp.concatenate(
            [
                key_extra((b // 2) * frames + part * frames_part, rows_part, patches)
                for b in key_blocks
            ],
            axis=0,
        )
        key_tiles, val_tiles = [], []
        for h in range(2):
            mine = (key_lane >= HDIM) == (h == 1)
            none = jnp.zeros_like(keys)
            key_tiles.append(
                jnp.concatenate([jnp.where(mine, keys, none).astype(bf16), extra], axis=1)
            )
            val_tiles.append(jnp.concatenate([jnp.where(mine, vals, none), mix_keys], axis=1))
        dk = [jnp.zeros((together * rows_part, LANES), f32)] * 2
        dv = [jnp.zeros((together * rows_part, LANES), f32)] * 2
        for c in range(0, blocks, joined):
            some = range(c, c + joined)
            span = slice(c * rows, (c + joined) * rows)
            query = jnp.concatenate([qkv_ref[b, 0] for b in some], axis=0)
            grad = jnp.concatenate([do_ref[b] for b in some], axis=0)
            for h in range(2):
                ext = jnp.concatenate([ext_ref[h, b] for b in some for ext_ref in ext_refs], axis=0)
                mix = jnp.concatenate([mix_ref[h, b] for b in some], axis=0)
                probs = jnp.exp(dot(key_tiles[h], jnp.concatenate([query, ext], axis=1), NT))
                dv[h] = dv[h] + dot(probs.astype(bf16), grad)
                moved = dot(val_tiles[h], jnp.concatenate([grad, mix], axis=1), NT)
                grad_scores = (probs * moved).astype(bf16)
                dk[h] = dk[h] + dot(grad_scores, query)
                head = slice(HDIM * h, HDIM * (h + 1))
                dq_turned[head, span] += dot(turned[head, :], grad_scores)
        dk = jnp.where(key_lane < HDIM, dk[0], dk[1]) * score_scale
        dv = jnp.where(key_lane < HDIM, dv[0], dv[1]).astype(bf16)
        for i, b in enumerate(key_blocks):
            for f in range(frames_part):
                rows_here = slice(i * rows_part + f * patches, i * rows_part + (f + 1) * patches)
                row = b * frames + part * frames_part + f
                keys_here = slice(first + f * patches, first + (f + 1) * patches)
                grads_ref[b, keys_here, :] = back(dk[rows_here, :], row, b % 2)
            grads_ref[b, first + rows_part : first + 2 * rows_part, :] = dv[
                i * rows_part : (i + 1) * rows_part, :
            ]
        return carry

    lax.fori_loop(0, blocks // together, step, 0)

    if last:
        for b in range(blocks):
            for f in range(frames):
                there = slice(b * rows + f * patches, b * rows + (f + 1) * patches)
                turned_back = back(dq_turned[:, there].T, b * frames + f, b % 2)
                grads_ref[b, f * patches : (f + 1) * patches, :] = turned_back
    else:
        carry_out[...] = dq_turned[...]


def attend_back(heads, grads, exts, outs, rotary, carry, part, parts, patches, chunk=2048, together=2):
    last = part == parts - 1
    blocks, _, rows, _ = heads.shape
    rows_part = rows // parts
    total = blocks * rows
    operands = [heads, grads, *exts, *outs, *rotary, *(carry or ())]
    kept = 2 * rows_part + (rows if last else 0)
    out_shape = [pltpu.HBM((blocks, kept, LANES), bf16)]
    if not last:
        out_shape.append(jax.ShapeDtypeStruct((LANES, total), f32))
        out_shape.append(jax.ShapeDtypeStruct((2, blocks, rows, LANES), bf16))
    return pl.pallas_call(
        functools.partial(
            attend_back_kernel,
            parts,
            len(exts),
            part,
            patches,
            chunk // rows,
            together,
            carry is not None,
            last,
        ),
        out_shape=out_shape,
        in_specs=[pl.BlockSpec(memory_space=VMEM)] * len(operands),
        out_specs=[pl.BlockSpec(memory_space=VMEM)] * len(out_shape),
        scratch_shapes=[VMEM((LANES, total), f32)],
        compiler_params=pltpu.CompilerParams(vmem_limit_bytes=56 * MIB),
        cost_estimate=pl.CostEstimate(
            flops=20 * total * blocks * rows_part * 2 * LANES,
            bytes_accessed=8 * MIB,
            transcendentals=0,
        ),
        name="attend_back",
    )(*operands)


def act_grad_kernel(cot_ref, gate_ref, down_ref, grad_ref, out_ref):
    frames, patches, _ = cot_ref.shape

    @pl.when(pl.program_id(0) == 0)
    def _():
        for f in range(frames):
            grad = gate_ref[f : f + 1, :] * cot_ref[f].astype(f32)
            grad_ref[f * patches : (f + 1) * patches, :] = grad.astype(bf16)

    out_ref[...] = dot(grad_ref[...], down_ref[...], NT)


def act_grad(cotangent, gate_two, down_weight, cols=512):
    frames, patches, width = cotangent.shape
    rows, inner = frames * patches, down_weight.shape[0]
    return pl.pallas_call(
        act_grad_kernel,
        out_shape=[
            jax.ShapeDtypeStruct((rows, width), bf16),
            pltpu.HBM((rows, inner), f32),
        ],
        grid=(inner // cols,),
        in_specs=[
            whole(cotangent.shape),
            whole(gate_two.shape),
            pl.BlockSpec((cols, width), lambda c: (c, 0)),
        ],
        out_specs=[whole((rows, width)), pl.BlockSpec((rows, cols), lambda c: (0, c))],
        compiler_params=pltpu.CompilerParams(vmem_limit_bytes=40 * MIB),
        cost_estimate=pl.CostEstimate(
            flops=2 * rows * width * inner, bytes_accessed=18 * MIB, transcendentals=0
        ),
        name="act_grad",
    )(cotangent, gate_two, down_weight)


def feed_kernel(hid_ref, grad_ref, actgrad_ref, up_ref, bias_ref, down_ref,
                branch_ref, back_ref, biasgrad_ref, joined_ref,
                hid_turned, up_slots, down_slots, up_sems, down_sems):
    step, steps = pl.program_id(0), pl.num_programs(0)
    width, cols = up_ref.shape
    group, clips, _, share, _ = joined_ref.shape
    some_clips, quarters = down_slots.shape[2:4]
    up_parts = width // cols
    slot = step % 2

    def copies(at):
        across = pl.ds(pl.multiple_of((at % up_parts) * cols, cols), cols)
        up_copy = pltpu.make_async_copy(
            up_slots.at[at % 2], joined_ref.at[:, :, at // up_parts, :, across], up_sems.at[at % 2]
        )
        down_copy = pltpu.make_async_copy(
            down_slots.at[at % 2],
            joined_ref.at[:, pl.ds(at * some_clips, some_clips), quarters : 2 * quarters],
            down_sems.at[at % 2],
        )
        return up_copy, down_copy

    @pl.when(step == 0)
    def _():
        hid_turned[...] = hid_ref[...].T

    @pl.when(step >= 2)
    def _():
        for copy in copies(step - 2):
            copy.wait()

    pre = dot(hid_ref[...], up_ref[...]) + bias_ref[...]
    square = pre * pre
    bend = jnp.tanh(pre * (0.7978845608 + (0.7978845608 * 0.044715) * square))
    half = 0.5 * (1.0 + bend)
    act = (pre * half).astype(bf16)
    slope = half + (0.5 * pre) * (1.0 - bend * bend) * (
        0.7978845608 + (0.7978845608 * 3.0 * 0.044715) * square
    )
    pre_grad = (slope * actgrad_ref[...]).astype(bf16)
    biasgrad_ref[...] = jnp.sum(pre_grad.astype(f32), axis=0, keepdims=True)
    branch = dot(act, down_ref[...])
    back = dot(pre_grad, up_ref[...], NT)
    up_grad = dot(hid_turned[...], pre_grad).astype(bf16)
    up_grad = up_grad.reshape(clips, group, share, cols)
    for c in range(clips):
        up_slots[slot, :, c] = up_grad[c]
    down_grad = dot(act.T, grad_ref[...]).astype(bf16)
    down_grad = down_grad.reshape(some_clips, group, quarters, share, width)
    for c in range(some_clips):
        down_slots[slot, :, c] = down_grad[c]

    @pl.when(step == 0)
    def _():
        branch_ref[...] = branch
        back_ref[...] = back

    @pl.when(step > 0)
    def _():
        branch_ref[...] += branch
        back_ref[...] += back

    for copy in copies(step):
        copy.start()

    @pl.when(step == steps - 1)
    def _():
        for at in (steps - 2, steps - 1):
            for copy in copies(at):
                copy.wait()


def feed_forward(hidden, grad, grad_act, up_weight, up_bias, down_weight, group, clips, cols=1024):
    rows, width = hidden.shape
    inner = up_weight.shape[1]
    share, quarters = width // (group * clips), inner // width
    some_clips = cols * clips // inner
    return pl.pallas_call(
        feed_kernel,
        out_shape=[
            jax.ShapeDtypeStruct((rows, width), f32),
            jax.ShapeDtypeStruct((rows, width), f32),
            jax.ShapeDtypeStruct((1, inner), f32),
            jax.ShapeDtypeStruct((group, clips, 2 * quarters + 1, share, width), bf16),
        ],
        grid=(inner // cols,),
        in_specs=[
            whole((rows, width)),
            whole((rows, width)),
            pl.BlockSpec((rows, cols), lambda c: (0, c)),
            pl.BlockSpec((width, cols), lambda c: (0, c)),
            pl.BlockSpec((1, cols), lambda c: (0, c)),
            pl.BlockSpec((cols, width), lambda c: (c, 0)),
        ],
        out_specs=[
            whole((rows, width)),
            whole((rows, width)),
            pl.BlockSpec((1, cols), lambda c: (0, c)),
            pl.BlockSpec(memory_space=pl.ANY),
        ],
        scratch_shapes=[
            VMEM((width, rows), bf16),
            VMEM((2, group, clips, share, cols), bf16),
            VMEM((2, group, some_clips, quarters, share, width), bf16),
            pltpu.SemaphoreType.DMA((2,)),
            pltpu.SemaphoreType.DMA((2,)),
        ],
        compiler_params=pltpu.CompilerParams(vmem_limit_bytes=58 * MIB),
        cost_estimate=pl.CostEstimate(
            flops=10 * rows * width * inner, bytes_accessed=44 * MIB, transcendentals=0
        ),
        name="feed_forward",
    )(hidden, grad, grad_act, up_weight, up_bias, down_weight)


def proj_grad_kernel(attn_ref, grad_ref, _, joined_ref):
    group, clips, _, share, width = joined_ref.shape
    grad = dot(attn_ref[...].T, grad_ref[...]).astype(bf16).reshape(clips, group, share, width)
    for c in range(clips):
        joined_ref[:, c, 0] = grad[c]


def proj_weight_grad(attn_low, grad_proj, joined):
    rows, width = attn_low.shape
    group, clips, entries, share, _ = joined.shape
    return pl.pallas_call(
        proj_grad_kernel,
        out_shape=jax.ShapeDtypeStruct(joined.shape, joined.dtype),
        grid=(1,),
        in_specs=[
            whole((rows, width)),
            whole((rows, width)),
            pl.BlockSpec(memory_space=pl.ANY),
        ],
        out_specs=pl.BlockSpec((group, clips, 1, share, width), lambda c: (0, 0, entries - 1, 0, 0)),
        input_output_aliases={2: 0},
        compiler_params=pltpu.CompilerParams(vmem_limit_bytes=40 * MIB),
        cost_estimate=pl.CostEstimate(
            flops=2 * rows * width * width, bytes_accessed=4 * MIB, transcendentals=0
        ),
        name="proj_weight_grad",
    )(attn_low, grad_proj, joined)


def merge_kernel(*refs):
    parts = len(refs) - 10
    att_refs = refs[:parts]
    (weight_ref, bias_ref, tok_ref, gate_one_ref, shift_ref, scale_ref,
     low_ref, proj_ref, after_ref, hid_ref) = refs[parts:]
    frames, patches, width = tok_ref.shape
    pairs = att_refs[0].shape[0]
    at = 0
    for att_ref in att_refs:
        low = jnp.concatenate([att_ref[p] for p in range(pairs)], axis=1)
        rows_part = att_ref.shape[1]
        there = slice(at, at + rows_part)
        low_ref[there, :] = low
        proj = dot(low, weight_ref[...]) + bias_ref[...]
        proj_ref[there, :] = proj
        for j in range(rows_part // patches):
            f = at // patches + j
            here = slice(f * patches, (f + 1) * patches)
            row = slice(f, f + 1)
            after = tok_ref[f].astype(f32) + gate_one_ref[row, :] * proj[
                j * patches : (j + 1) * patches, :
            ]
            after_ref[here, :] = after
            centre = after - jnp.mean(after, axis=1, keepdims=True)
            inv = lax.rsqrt(jnp.mean(centre * centre, axis=1, keepdims=True) + norm_eps)
            hid = centre * inv * (1.0 + scale_ref[row, :]) + shift_ref[row, :]
            hid_ref[here, :] = hid.astype(bf16)
        at += rows_part


def merge_heads(attended, proj_weight, proj_bias, tokens, mods):
    frames, patches, width = tokens.shape
    rows = frames * patches
    operands = [*attended, proj_weight, proj_bias, tokens, *mods]
    return pl.pallas_call(
        merge_kernel,
        out_shape=[
            jax.ShapeDtypeStruct((rows, width), bf16),
            jax.ShapeDtypeStruct((rows, width), f32),
            jax.ShapeDtypeStruct((rows, width), f32),
            pltpu.HBM((rows, width), bf16),
        ],
        in_specs=[pl.BlockSpec(memory_space=VMEM)] * len(operands),
        out_specs=[pl.BlockSpec(memory_space=VMEM)] * 4,
        compiler_params=pltpu.CompilerParams(vmem_limit_bytes=48 * MIB),
        cost_estimate=pl.CostEstimate(
            flops=2 * rows * width * width, bytes_accessed=16 * MIB, transcendentals=0
        ),
        name="merge_heads",
    )(*operands)


def column_sum(value):
    return jnp.sum(value, axis=0, keepdims=True)


def unmerge_kernel(back_ref, after_ref, cot_ref, gate_one_ref, scale_ref, weight_ref,
                   grad_ref, gproj_ref, parts_ref):
    frames, patches, width = cot_ref.shape
    for f in range(frames):
        here = slice(f * patches, (f + 1) * patches)
        row = slice(f, f + 1)
        after = after_ref[here, :]
        centre = after - jnp.mean(after, axis=1, keepdims=True)
        inv = lax.rsqrt(jnp.mean(centre * centre, axis=1, keepdims=True) + norm_eps)
        normed = centre * inv
        scaled = back_ref[here, :] * (1.0 + scale_ref[row, :])
        mean_grad = jnp.mean(scaled, axis=1, keepdims=True)
        mean_mix = jnp.mean(scaled * normed, axis=1, keepdims=True)
        grad = cot_ref[f].astype(f32) + inv * (scaled - mean_grad - normed * mean_mix)
        grad_ref[here, :] = grad
        gproj_ref[here, :] = (gate_one_ref[row, :] * grad).astype(bf16)
    step = 2 * patches
    for i in range(frames * patches // step):
        here = slice(i * step, (i + 1) * step)
        part = dot(gproj_ref[here, :], weight_ref[...], NT).astype(bf16)
        for p in range(parts_ref.shape[0]):
            parts_ref[p, here, :] = part[:, p * LANES : (p + 1) * LANES]


def unmerge_heads(back, after, cotangent, gate_one, scale_two, proj_weight):
    frames, patches, width = cotangent.shape
    rows = frames * patches
    operands = [back, after, cotangent, gate_one, scale_two, proj_weight]
    return pl.pallas_call(
        unmerge_kernel,
        out_shape=[
            pltpu.HBM((rows, width), f32),
            jax.ShapeDtypeStruct((rows, width), bf16),
            pltpu.HBM((width // LANES, rows, LANES), bf16),
        ],
        in_specs=[pl.BlockSpec(memory_space=VMEM)] * len(operands),
        out_specs=[pl.BlockSpec(memory_space=VMEM)] * 3,
        compiler_params=pltpu.CompilerParams(vmem_limit_bytes=48 * MIB),
        cost_estimate=pl.CostEstimate(
            flops=2 * rows * width * width, bytes_accessed=12 * MIB, transcendentals=0
        ),
        name="unmerge_heads",
    )(*operands)


def side_kernel(branch_ref, back_ref, after_ref, proj_ref, cot_ref, gate_two_ref, bias_ref,
                grad_ref, gproj_ref, gbranch_ref, out_ref, sums_ref, biases_ref):
    f, frames = pl.program_id(0), pl.num_programs(0)
    cot = cot_ref[0].astype(f32)
    after = after_ref[...]
    branch = branch_ref[...] + bias_ref[...]
    out_ref[0] = (after + gate_two_ref[pl.ds(f, 1), :] * branch).astype(bf16)
    centre = after - jnp.mean(after, axis=1, keepdims=True)
    inv = lax.rsqrt(jnp.mean(centre * centre, axis=1, keepdims=True) + norm_eps)
    back = back_ref[...]
    for kind, term in enumerate(
        (grad_ref[...] * proj_ref[...], back, back * (centre * inv), cot * branch)
    ):
        sums_ref[pl.ds(kind * frames + f, 1), :] = column_sum(term)

    @pl.when(f == 0)
    def _():
        biases_ref[...] = jnp.zeros_like(biases_ref)

    biases_ref[0:1, :] += column_sum(gproj_ref[...].astype(f32))
    biases_ref[1:2, :] += column_sum(gbranch_ref[...].astype(f32))


def side_sums(branch, back, after, proj, cotangent, gate_two, down_bias, grad_after, grad_proj,
              grad_branch):
    frames, patches, width = cotangent.shape
    rows = pl.BlockSpec((patches, width), lambda f: (f, 0))
    slot = pl.BlockSpec((1, patches, width), lambda f: (f, 0, 0))
    return pl.pallas_call(
        side_kernel,
        out_shape=[
            jax.ShapeDtypeStruct((frames, patches, width), bf16),
            jax.ShapeDtypeStruct((4 * frames, width), f32),
            jax.ShapeDtypeStruct((2, width), f32),
        ],
        grid=(frames,),
        in_specs=[rows, rows, rows, rows, slot, whole(gate_two.shape), whole(down_bias.shape), rows,
                  rows, rows],
        out_specs=[slot, whole((4 * frames, width)), whole((2, width))],
        compiler_params=pltpu.CompilerParams(vmem_limit_bytes=48 * MIB),
        cost_estimate=pl.CostEstimate(flops=0, bytes_accessed=16 * MIB, transcendentals=0),
        name="side_sums",
    )(
        in_hbm(branch),
        in_hbm(back),
        in_hbm(after),
        in_hbm(proj),
        cotangent,
        gate_two,
        down_bias,
        grad_after,
        grad_proj,
        in_hbm(grad_branch),
    )


def heads_grad_kernel(hid_ref, first_ref, last_ref, out_ref, bias_ref, total):
    rows = hid_ref.shape[2]
    rows_part = first_ref.shape[1] // 2
    grad = jnp.concatenate(
        [
            last_ref[0, :rows, :],
            jnp.concatenate(
                [first_ref[0, :rows_part, :], last_ref[0, rows : rows + rows_part, :]], axis=0
            ),
            jnp.concatenate([first_ref[0, rows_part:, :], last_ref[0, rows + rows_part :, :]], axis=0),
        ],
        axis=1,
    )
    some = dot(hid_ref[0], grad)
    some_bias = column_sum(grad.astype(f32))

    @pl.when(pl.program_id(0) == 0)
    def _():
        total[...] = some
        bias_ref[...] = some_bias

    @pl.when(pl.program_id(0) > 0)
    def _():
        total[...] += some
        bias_ref[...] += some_bias

    @pl.when(pl.program_id(0) == pl.num_programs(0) - 1)
    def _():
        devices, triple, _ = out_ref.shape
        share = triple // 3
        for k in range(3):
            part = total[:, k * LANES : (k + 1) * LANES].astype(bf16)
            out_ref[:, k * share : (k + 1) * share, :] = part.reshape(devices, share, LANES)


def heads_grad(hidden_clip, first, last, devices):
    blocks, width, rows = hidden_clip.shape
    shape = (devices, 3 * width // devices, LANES)
    return pl.pallas_call(
        heads_grad_kernel,
        out_shape=[
            jax.ShapeDtypeStruct(shape, bf16),
            jax.ShapeDtypeStruct((1, 3 * LANES), f32),
        ],
        grid=(blocks,),
        in_specs=[
            pl.BlockSpec((1, width, rows), lambda b: (b, 0, 0)),
            pl.BlockSpec((1,) + first.shape[1:], lambda b: (b, 0, 0)),
            pl.BlockSpec((1,) + last.shape[1:], lambda b: (b, 0, 0)),
        ],
        out_specs=[whole(shape), whole((1, 3 * LANES))],
        scratch_shapes=[VMEM((width, 3 * LANES), f32)],
        compiler_params=pltpu.CompilerParams(vmem_limit_bytes=40 * MIB),
        cost_estimate=pl.CostEstimate(
            flops=6 * blocks * rows * width * LANES, bytes_accessed=12 * MIB, transcendentals=0
        ),
        name="heads_grad",
    )(in_hbm(hidden_clip), first, last)


def finish_kernel(first_ref, last_ref, wq_ref, wk_ref, wv_ref, tok_ref, scale_ref, after_ref,
                  partbias_ref, out_ref, send_ref, total):
    frames, patches, width = tok_ref.shape
    rows = frames * patches
    rows_part = first_ref.shape[1] // 2
    step = pl.program_id(0)
    query, keys, vals = [], [], []
    for p in range(first_ref.shape[0]):
        query.append(last_ref[p, :rows, :])
        keys.append(
            jnp.concatenate(
                [first_ref[p, :rows_part, :], last_ref[p, rows : rows + rows_part, :]], axis=0
            )
        )
        vals.append(
            jnp.concatenate([first_ref[p, rows_part:, :], last_ref[p, rows + rows_part :, :]], axis=0)
        )
    some = None
    for grads, weight_ref in ((query, wq_ref), (keys, wk_ref), (vals, wv_ref)):
        term = dot(jnp.concatenate(grads, axis=1), weight_ref[...], NT)
        some = term if some is None else some + term

    @pl.when(step == 0)
    def _():
        total[...] = some

    @pl.when(step > 0)
    def _():
        total[...] += some

    @pl.when(step == pl.num_programs(0) - 1)
    def _():
        shift_sums, scale_sums = [], []
        for f in range(frames):
            here = slice(f * patches, (f + 1) * patches)
            x = tok_ref[f].astype(f32)
            centre = x - jnp.mean(x, axis=1, keepdims=True)
            inv = lax.rsqrt(jnp.mean(centre * centre, axis=1, keepdims=True) + norm_eps)
            normed = centre * inv
            back = total[here, :]
            shift_sums.append(column_sum(back))
            scale_sums.append(column_sum(back * normed))
            scaled = back * (1.0 + scale_ref[f : f + 1, :])
            mean_grad = jnp.mean(scaled, axis=1, keepdims=True)
            mean_mix = jnp.mean(scaled * normed, axis=1, keepdims=True)
            grad = after_ref[here, :] + inv * (scaled - mean_grad - normed * mean_mix)
            out_ref[f] = grad.astype(bf16)
        sums = jnp.concatenate(shift_sums + scale_sums, axis=0)
        sums = jnp.concatenate(
            [sums[:, i : i + LANES] for i in range(0, width, LANES)], axis=0
        ).astype(bf16)
        bias = [partbias_ref[:, k * LANES : (k + 1) * LANES] for k in range(3)]
        high = [value.astype(bf16).astype(f32) for value in bias]
        low = [value - upper for value, upper in zip(bias, high)]
        bias = jnp.concatenate(high + low + [jnp.zeros((10, LANES), f32)], axis=0).astype(bf16)
        count = sums.shape[0]
        for d in range(send_ref.shape[0]):
            send_ref[d, :count, :] = sums
            send_ref[d, count:, :] = bias


def finish(first, last, qkv_weight, tokens, scale_one, grad_after, part_bias, copies, cols=256):
    frames, patches, width = tokens.shape
    rows = frames * patches
    steps, some = width // cols, cols // LANES

    send_shape = (copies, 2 * frames * (width // LANES) + 16, LANES)

    def column(third):
        return lambda c: (0, third * steps + c)

    return pl.pallas_call(
        finish_kernel,
        out_shape=[
            jax.ShapeDtypeStruct((frames, patches, width), bf16),
            pltpu.HBM(send_shape, bf16),
        ],
        grid=(steps,),
        in_specs=[
            pl.BlockSpec((some,) + first.shape[1:], lambda c: (c, 0, 0)),
            pl.BlockSpec((some,) + last.shape[1:], lambda c: (c, 0, 0)),
        ]
        + [pl.BlockSpec((width, cols), column(part)) for part in range(3)]
        + [whole(tokens.shape), whole(scale_one.shape), whole((rows, width))]
        + [whole(part_bias.shape)],
        out_specs=[whole((frames, patches, width)), whole(send_shape)],
        scratch_shapes=[VMEM((rows, width), f32)],
        compiler_params=pltpu.CompilerParams(vmem_limit_bytes=48 * MIB),
        cost_estimate=pl.CostEstimate(
            flops=6 * rows * width * width, bytes_accessed=16 * MIB, transcendentals=0
        ),
        name="finish",
    )(first, last, *[qkv_weight] * 3, tokens, scale_one, grad_after, part_bias)


def unpack_kernel(summed_ref, up_ref, down_ref, proj_ref):
    entries, share, width = summed_ref.shape
    quarters = entries // 2
    for i in range(quarters):
        up_ref[:, i * width : (i + 1) * width] = summed_ref[i].astype(f32)
        down_ref[i * share : (i + 1) * share, :] = summed_ref[quarters + i].astype(f32)
    proj_ref[...] = summed_ref[2 * quarters].astype(f32)


def unpack(summed):
    entries, share, width = summed.shape
    quarters = entries // 2
    return pl.pallas_call(
        unpack_kernel,
        out_shape=[
            jax.ShapeDtypeStruct((share, quarters * width), f32),
            jax.ShapeDtypeStruct((quarters * share, width), f32),
            jax.ShapeDtypeStruct((share, width), f32),
        ],
        in_specs=[pl.BlockSpec(memory_space=VMEM)],
        out_specs=[pl.BlockSpec(memory_space=VMEM)] * 3,
        name="unpack",
    )(summed)


def last_kernel(clips, frames, got_ref, member_ref, cols_ref, early_ref, earlysum_ref,
                rows_ref, bias_ref, ada_ref, adasum_ref):
    group = got_ref.shape[0]
    share, width = rows_ref.shape[0], rows_ref.shape[1] // 3
    tiles = width // LANES
    count = 2 * frames * tiles
    starts = [3 * share + c * (count + 16) for c in range(clips)]
    some = 4 * frames
    ada_ref[:, 2 * width :] = early_ref[...]
    adasum_ref[:, 2 * width :] = earlysum_ref[...]
    for i in range(tiles // 2):
        sums = jnp.concatenate(
            [
                got_ref[:, at + i * some : at + (i + 1) * some, :].reshape(group * some, LANES)
                for at in starts
            ],
            axis=0,
        )
        for j in range(2):
            for kind in range(2):
                level = dot(member_ref[2 * j + kind], sums).astype(bf16)
                at = kind * width + (2 * i + j) * LANES
                ada_ref[:, at : at + LANES] = dot(cols_ref[...], level)
                adasum_ref[:, at : at + LANES] = column_sum(level.astype(f32))
    for p in range(group):
        bias = None
        for at in starts:
            term = got_ref[p, at + count : at + count + 16, :].astype(f32)
            bias = term if bias is None else bias + term
        for third in range(3):
            at = third * width + p * LANES
            here = slice(third * share, (third + 1) * share)
            rows_ref[:, at : at + LANES] = got_ref[p, here, :].astype(f32)
            bias_ref[:, at : at + LANES] = bias[third : third + 1, :] + bias[third + 3 : third + 4, :]


def last_sums(got, member, columns, early, early_sum, clips, frames):
    share, width = early.shape[0], early.shape[1] // 4
    return pl.pallas_call(
        functools.partial(last_kernel, clips, frames),
        out_shape=[
            jax.ShapeDtypeStruct((share, 3 * width), f32),
            jax.ShapeDtypeStruct((1, 3 * width), f32),
            jax.ShapeDtypeStruct((share, 6 * width), f32),
            jax.ShapeDtypeStruct((1, 6 * width), f32),
        ],
        in_specs=[pl.BlockSpec(memory_space=VMEM)] * 5,
        out_specs=[pl.BlockSpec(memory_space=VMEM)] * 4,
        compiler_params=pltpu.CompilerParams(vmem_limit_bytes=48 * MIB),
        cost_estimate=pl.CostEstimate(flops=0, bytes_accessed=4 * MIB, transcendentals=0),
        name="last_sums",
    )(got, member, columns, early, early_sum)


def body(
    tokens,
    out_cotangent,
    level_embed,
    ada_weight,
    ada_bias,
    qkv_weight,
    qkv_bias,
    proj_weight,
    proj_bias,
    up_weight,
    up_bias,
    down_weight,
    down_bias,
    context_count,
    frame_level,
    slot_time,
):
    frames, patches, width = tokens.shape
    rows = frames * patches
    inner = up_weight.shape[1]
    frm_count, sp_count = lax.axis_size("frm"), lax.axis_size("sp")
    devices = frm_count * sp_count
    group = FRAMES // frames * sp_count
    clips = devices // group
    frm, sp = lax.axis_index("frm"), lax.axis_index("sp")
    me = frm * sp_count + sp
    clip = me // group
    clip_groups = [list(range(first, first + group)) for first in range(0, devices, group)]
    across_clips = [list(range(first, devices, group)) for first in range(group)]
    everyone = [list(range(devices))]
    halves = 2
    share = width // devices
    per_dest = inner // devices

    levels_here = level_embed.shape[0]
    embed_all = to_everyone(level_embed, devices).reshape(devices * levels_here, width)

    clip_times = lax.dynamic_slice_in_dim(slot_time, clip * FRAMES, FRAMES)
    clip_levels = lax.dynamic_index_in_dim(frame_level, clip, 0, keepdims=False)
    context = lax.dynamic_index_in_dim(context_count, clip, 0, keepdims=False)
    seen = (clip_times[None, :] <= clip_times[:, None]) | (clip_times[None, :] < context)
    visible = jnp.pad(
        jnp.where(seen, 0.0, masked_out).astype(f32), ((0, 0), (0, LANES - FRAMES))
    )

    def by_blocks(table):
        table = table.reshape(FRAMES // frames, 1, frames, LANES)
        return jnp.broadcast_to(table, (FRAMES // frames, sp_count, frames, LANES)).reshape(
            group * frames, LANES
        )

    visible = by_blocks(visible)
    freq, sign, time_lane, row_lane = rotary_lanes()
    angle_time = clip_times.astype(f32)[:, None] * freq[None, :]
    ctime = by_blocks(jnp.where(time_lane[None, :], jnp.cos(angle_time), 0.0))
    stime = by_blocks(jnp.where(time_lane[None, :], jnp.sin(angle_time) * sign[None, :], 0.0))
    patch_ids = jnp.arange(sp_count * patches, dtype=jnp.int32).reshape(sp_count, patches)
    place = jnp.where(
        row_lane[None, None, :], (patch_ids // GRID)[..., None], (patch_ids % GRID)[..., None]
    )
    angle_patch = place.astype(f32) * freq[None, None, :]
    cpatch = jnp.where(time_lane, 0.0, jnp.cos(angle_patch))
    spatch = jnp.where(time_lane, 0.0, jnp.sin(angle_patch) * sign)
    rotary = [ctime, stime, cpatch, spatch]

    def my_table(time_part, patch_part):
        mine = lax.dynamic_slice_in_dim(time_part, me % group * frames, frames)
        half = lax.dynamic_index_in_dim(patch_part, sp, 0, keepdims=False)
        return (mine[:, None, :] + half[None]).reshape(rows, LANES)

    cosine, sine = my_table(ctime, cpatch), my_table(stime, spatch)

    my_times = lax.dynamic_slice_in_dim(slot_time, frm * frames, frames)
    my_levels = jnp.take(clip_levels, my_times)
    embed_act = jax.nn.silu(embed_all.astype(f32)).astype(bf16)
    level_ids = jnp.arange(devices * levels_here, dtype=jnp.int32)
    pick = (my_levels[:, None] == level_ids[None, :]).astype(bf16)
    my_embed = dot(pick, embed_act).astype(bf16)

    def modulation(embeds, first, count):
        here = slice(first * width, (first + count) * width)
        rows_mod = dot(embeds, ada_weight[:, here]) + ada_bias[here].astype(f32)
        rows_mod = lax.reduce_precision(rows_mod, 8, 7)
        return [rows_mod[:, i * width : (i + 1) * width] for i in range(count)]

    shift_one, scale_one = modulation(my_embed, 0, 2)

    hidden_turned, head_parts = project(
        tokens, shift_one, scale_one, qkv_weight, qkv_bias.astype(f32)[None, :], cosine, sine
    )

    my_embed, head_parts = lax.optimization_barrier((my_embed, head_parts))
    gate_one, shift_two, scale_two, gate_two = modulation(my_embed, 2, 4)
    heads = exchange(head_parts, clip_groups)
    grad_branch, grad_act = act_grad(out_cotangent, gate_two, down_weight)
    slot_ids = (jnp.arange(devices * frames, dtype=jnp.int32) // (sp_count * frames)) * frames
    slot_ids = slot_ids + jnp.arange(devices * frames, dtype=jnp.int32) % frames
    slot_levels = frame_level[slot_ids // FRAMES, slot_time[slot_ids]]
    member_of = (level_ids[:, None] == slot_levels[None, :]).astype(bf16)
    my_columns = lax.dynamic_slice_in_dim(embed_act, me * share, share, axis=1)
    which = jnp.arange(4, dtype=jnp.int32)
    member_last = jnp.where(
        (which[:, None] == which[None, :])[:, None, None, :, None],
        member_of.reshape(1, -1, devices, 1, frames),
        jnp.zeros((), bf16),
    ).reshape(4, -1, devices * 4 * frames)
    columns_turned = my_columns.T
    heads, grad_branch, grad_act, member_of, my_columns, member_last, columns_turned = (
        lax.optimization_barrier(
            (heads, grad_branch, grad_act, member_of, my_columns, member_last, columns_turned)
        )
    )
    outs, exts, attended = [], [], []
    for first, frames_part in ((0, frames - frames // 4), (frames - frames // 4, frames // 4)):
        out, ext = attend(heads, visible, patches, first, frames_part)
        visible, out = lax.optimization_barrier((visible, out))
        outs.append(out)
        exts.append(ext)
        attended.append(exchange(out, clip_groups))

    hidden_turned, _ = lax.optimization_barrier((hidden_turned, heads))
    hidden_clip = lax.all_gather(hidden_turned, AXES, axis_index_groups=clip_groups)

    attn_low, attn_proj, after_attn, hidden_two = merge_heads(
        attended,
        proj_weight,
        proj_bias.astype(f32)[None, :],
        tokens,
        (gate_one, shift_two, scale_two),
    )
    branch, grad_hidden_two, up_b_grad, joined = feed_forward(
        hidden_two,
        grad_branch,
        grad_act,
        up_weight,
        up_bias.astype(f32)[None, :],
        down_weight,
        group,
        clips,
    )
    grad_after, grad_proj, grad_parts = unmerge_heads(
        grad_hidden_two, after_attn, out_cotangent, gate_one, scale_two, proj_weight
    )
    grads = exchange(grad_parts, clip_groups)
    block_out, early_sums, early_biases = side_sums(
        branch,
        grad_hidden_two,
        after_attn,
        attn_proj,
        out_cotangent,
        gate_two,
        down_bias.astype(f32)[None, :],
        grad_after,
        grad_proj,
        grad_branch,
    )

    joined = proj_weight_grad(attn_low, grad_proj, joined)
    joined, hidden_clip = lax.optimization_barrier((joined, hidden_clip))
    summed = lax.psum_scatter(
        joined, AXES, scatter_dimension=0, axis_index_groups=clip_groups, tiled=True
    )[0]

    def slot_parts(slot_sums, biases):
        kinds = slot_sums.shape[0] // frames
        sums = slot_sums.reshape(kinds, frames, width).transpose(1, 0, 2).reshape(frames, -1)
        sums = jnp.broadcast_to(sums.astype(bf16)[None], (devices, frames, kinds * width))
        high = biases.astype(bf16)
        low = (biases - high.astype(f32)).astype(bf16)
        both = jnp.concatenate([high, low], axis=1).reshape(devices, frames, -1)
        lanes = -(-both.shape[2] // LANES) * LANES
        both = jnp.pad(both, ((0, 0), (0, 0), (0, lanes - both.shape[2])))
        return jnp.concatenate([sums, both], axis=2)

    def bias_share(got, count, size):
        extra = jnp.sum(got[:, :, count:].astype(f32), axis=0)
        extra = extra[:, : 2 * size // frames].reshape(-1)
        return extra[:size] + extra[size:]

    def level_out(got, count):
        slots = got[:, :, :count].reshape(devices * frames, count)
        level_grad = dot(member_of, slots).astype(bf16)
        return dot(my_columns, level_grad, TN), jnp.sum(level_grad.astype(f32), axis=0)

    early_parts = slot_parts(
        early_sums,
        jnp.concatenate(
            [
                up_b_grad.reshape(devices, per_dest),
                early_biases[0].reshape(devices, share),
                early_biases[1].reshape(devices, share),
            ],
            axis=1,
        ),
    )
    early_parts, _ = lax.optimization_barrier((early_parts, grads))
    early_got = exchange(early_parts, everyone)

    first_grads, carry, mixes = attend_back(
        heads, grads, exts, outs, rotary, None, 0, halves, patches
    )
    carry, early_got = lax.optimization_barrier((carry, early_got))
    own_first = exchange(first_grads, clip_groups)
    (last_grads,) = attend_back(
        heads, grads, exts, outs, rotary, (carry, mixes), 1, halves, patches
    )
    last_parts, own_first = lax.optimization_barrier((last_grads, own_first))
    own_last = exchange(last_parts, clip_groups)

    early_w, early_b = level_out(early_got, 4 * width)
    early_bias_out = bias_share(early_got, 4 * width, per_dest + 2 * share)

    qkv_part, qkv_b_part = heads_grad(hidden_clip, first_grads, last_grads, devices)
    qkv_part = qkv_part.reshape(clips, group, 3 * share, LANES)
    qkv_sum = lax.dynamic_index_in_dim(qkv_part, clip, 0, keepdims=False).astype(f32)
    for j in range(1, clips):
        some = lax.dynamic_index_in_dim(qkv_part, clip ^ j, 0, keepdims=False)
        pairs = [(source, source ^ (j * group)) for source in range(devices)]
        qkv_sum = qkv_sum + lax.ppermute(some, AXES, pairs).astype(f32)
    qkv_sum, own_last, summed = lax.optimization_barrier(
        (qkv_sum.astype(bf16), own_last, summed)
    )

    summed = lax.psum_scatter(
        summed, AXES, scatter_dimension=0, axis_index_groups=across_clips, tiled=True
    )[0]
    up_w_out, down_w_out, proj_w_out = unpack(summed)

    tokens_grad, last_send = finish(
        own_first, own_last, qkv_weight, tokens, scale_one, grad_after, qkv_b_part, clips
    )
    clip_got = exchange(last_send, across_clips).reshape(1, -1, LANES)
    clip_got = jnp.broadcast_to(clip_got, (group,) + clip_got.shape[1:])
    last_got = exchange(jnp.concatenate([qkv_sum, clip_got], axis=1), clip_groups)
    last_got, early_w, early_b, early_bias_out = lax.optimization_barrier(
        (last_got, early_w, early_b, early_bias_out)
    )
    up_b_out = early_bias_out[:per_dest]
    proj_b_out = early_bias_out[per_dest : per_dest + share]
    down_b_out = early_bias_out[per_dest + share :]
    qkv_w_out, qkv_b_all, ada_w_out, ada_b_all = last_sums(
        last_got, member_last, columns_turned, early_w, early_b[None, :], clips, frames
    )
    qkv_b_out = lax.dynamic_slice_in_dim(qkv_b_all[0], me * 3 * share, 3 * share)
    ada_b_all = ada_b_all[0]
    ada_share = ada_b_all.shape[0] // devices
    ada_b_out = lax.dynamic_slice_in_dim(ada_b_all, me * ada_share, ada_share)
    return (
        block_out,
        tokens_grad,
        ada_w_out,
        ada_b_out,
        qkv_w_out,
        qkv_b_out,
        proj_w_out,
        proj_b_out,
        up_w_out,
        up_b_out,
        down_w_out,
        down_b_out,
    )


def solution(mesh):
    tokens_spec = P("frm", "sp", None)
    rows_spec = P(AXES, None)
    vector_spec = P(AXES)
    return jax.shard_map(
        body,
        mesh=mesh,
        in_specs=(tokens_spec, tokens_spec, rows_spec) + (P(),) * 13,
        out_specs=(tokens_spec, tokens_spec) + (rows_spec, vector_spec) * 5,
        check_vma=False,
    )
```

```python
import functools
import math

import jax
import jax.numpy as jnp
import numpy as np
from jax import lax
from jax.experimental import pallas as pl
from jax.experimental.pallas import tpu as pltpu
from jax.sharding import PartitionSpec as P

HEADS = 16
HDIM = 64
FRAMES = 16
GRID = 16
LANES = 128
MIB = 2**20

norm_eps = 1e-06
masked_out = -1e30
score_scale = 0.125

f32 = jnp.float32
bf16 = jnp.bfloat16
NN = (((1,), (0,)), ((), ()))
NT = (((1,), (1,)), ((), ()))
TN = (((0,), (0,)), ((), ()))
AXES = ("frm", "sp")
VMEM = pltpu.VMEM


def dot(left_op, right_op, dims=NN):
    return lax.dot_general(left_op, right_op, dims, preferred_element_type=f32)


def exchange(value, groups):
    return lax.all_to_all(value, AXES, 0, 0, axis_index_groups=groups)


def to_everyone(value, devices):
    return exchange(
        jnp.broadcast_to(value[None], (devices,) + value.shape), [list(range(devices))]
    )


def rotary_lanes():
    lane = np.arange(LANES) % HDIM
    start = np.where(lane < 16, 0, np.where(lane < 40, 16, 40))
    half = np.where(lane < 16, 8, 12)
    offset = lane - start
    freq = np.exp((offset % half).astype(np.float32) * np.float32(-math.log(10000.0)) / half)
    sign = np.where(offset < half, -1.0, 1.0)
    return (
        freq.astype(np.float32),
        sign.astype(np.float32),
        (lane < 16),
        (lane >= 16) & (lane < 40),
    )


def rotate_lanes(value, cosine, sine):
    lane = lax.broadcasted_iota(jnp.int32, value.shape, 1) % HDIM
    near_first = pltpu.roll(value, LANES - 8, 1)
    near_second = pltpu.roll(value, 8, 1)
    far_first = pltpu.roll(value, LANES - 12, 1)
    far_second = pltpu.roll(value, 12, 1)
    in_first = (lane < 28) | ((lane >= 40) & (lane < 52))
    far = jnp.where(in_first, far_first, far_second)
    near = jnp.where(lane < 8, near_first, near_second)
    partner = jnp.where(lane < 16, near, far)
    return value * cosine + partner * sine


def project_kernel(tok_ref, shift_ref, scale_ref, wq_ref, wk_ref, wv_ref, bq_ref, bk_ref, bv_ref,
                   cos_ref, sin_ref, turned_ref, out_ref, hid_all):
    frames, patches, _ = tok_ref.shape

    @pl.when(pl.program_id(0) == 0)
    def _():
        for f in range(frames):
            here = slice(f * patches, (f + 1) * patches)
            x = tok_ref[f].astype(f32)
            centre = x - jnp.mean(x, axis=1, keepdims=True)
            inv = lax.rsqrt(jnp.mean(centre * centre, axis=1, keepdims=True) + norm_eps)
            hid = centre * inv * (1.0 + scale_ref[f : f + 1, :]) + shift_ref[f : f + 1, :]
            hid = hid.astype(bf16)
            hid_all[here, :] = hid
            turned_ref[:, here] = hid.T

    hid = hid_all[...]
    query = dot(hid, wq_ref[...]) + bq_ref[...]
    keys = dot(hid, wk_ref[...]) + bk_ref[...]
    vals = (dot(hid, wv_ref[...]) + bv_ref[...]).astype(bf16)
    for p in range(wq_ref.shape[1] // LANES):
        lanes = slice(p * LANES, (p + 1) * LANES)
        out_ref[p, 0] = rotate_lanes(query[:, lanes], cos_ref[...], sin_ref[...]).astype(bf16)
        out_ref[p, 1] = rotate_lanes(keys[:, lanes], cos_ref[...], sin_ref[...]).astype(bf16)
        out_ref[p, 2] = vals[:, lanes]


def in_hbm(value):
    return pltpu.with_memory_space_constraint(value, pltpu.HBM)


def whole(shape):
    return pl.BlockSpec(shape, lambda *_: (0,) * len(shape))


def project(tokens, shift_one, scale_one, qkv_weight, qkv_bias, cosine, sine, cols=256):
    frames, patches, width = tokens.shape
    rows = frames * patches
    pairs = width // LANES
    steps, some = width // cols, cols // LANES

    def column(part):
        return lambda c: (0, part * steps + c)

    return pl.pallas_call(
        project_kernel,
        out_shape=[
            pltpu.HBM((width, rows), bf16),
            pltpu.HBM((pairs, 3, rows, LANES), bf16),
        ],
        grid=(steps,),
        in_specs=[whole(tokens.shape), whole(shift_one.shape), whole(scale_one.shape)]
        + [pl.BlockSpec((width, cols), column(part)) for part in range(3)]
        + [pl.BlockSpec((1, cols), column(part)) for part in range(3)]
        + [whole((rows, LANES)), whole((rows, LANES))],
        out_specs=[
            whole((width, rows)),
            pl.BlockSpec((some, 3, rows, LANES), lambda c: (c, 0, 0, 0)),
        ],
        scratch_shapes=[VMEM((rows, width), bf16)],
        compiler_params=pltpu.CompilerParams(vmem_limit_bytes=40 * MIB),
        cost_estimate=pl.CostEstimate(
            flops=6 * rows * width * width, bytes_accessed=10 * MIB, transcendentals=0
        ),
        name="project",
    )(tokens, shift_one, scale_one, *[in_hbm(qkv_weight)] * 3, *[qkv_bias] * 3, cosine, sine)


def key_extra(first_frame, rows, patches):
    row = lax.broadcasted_iota(jnp.int32, (rows, LANES), 0)
    lane = lax.broadcasted_iota(jnp.int32, (rows, LANES), 1)
    hit = (lane == first_frame + row // patches) | ((lane >= FRAMES) & (lane < FRAMES + 3))
    return jnp.where(hit, 1.0, 0.0).astype(bf16)


def split_three(column):
    high = column.astype(bf16).astype(f32)
    rest = column - high
    mid = rest.astype(bf16).astype(f32)
    return high, mid, rest - mid


def attend_kernel(first, rows_part, patches, joined, joined_keys, qkv_ref, vis_ref, o_ref, ext_ref):
    blocks, _, rows, _ = qkv_ref.shape
    frames, frames_part = rows // patches, rows_part // patches
    tile, chunk = joined * rows_part, joined_keys * rows
    lane = lax.broadcasted_iota(jnp.int32, (tile, LANES), 1)
    mine_rows = slice(first * patches, first * patches + rows_part)
    ones = jnp.full((chunk, LANES), 1.0, bf16)

    def step(t, carry):
        query = jnp.concatenate(
            [qkv_ref[t * joined + i, 0, mine_rows, :] for i in range(joined)], axis=0
        )
        query = query * score_scale
        seen = jnp.concatenate(
            [
                jnp.broadcast_to(
                    vis_ref[pl.ds((t * joined + i) * frames + first + f, 1), :],
                    (patches, LANES),
                )
                for i in range(joined)
                for f in range(frames_part)
            ],
            axis=0,
        )
        outs, ext_heads = [], []
        for h in range(2):
            mine = jnp.where((lane >= HDIM) == (h == 1), query, jnp.zeros_like(query))
            query_ext = jnp.concatenate([mine.astype(bf16), seen.astype(bf16)], axis=1)
            top = None
            for c in range(0, blocks, joined_keys):
                some_blocks = range(c, c + joined_keys)
                keys = jnp.concatenate(
                    [
                        jnp.concatenate(
                            [qkv_ref[b, 1], key_extra((b // 2) * frames, rows, patches)], axis=1
                        )
                        for b in some_blocks
                    ],
                    axis=0,
                )
                vals = jnp.concatenate([qkv_ref[b, 2] for b in some_blocks], axis=0)
                vals = jnp.concatenate([vals, ones], axis=1)
                scores = dot(query_ext, keys, NT)
                chunk_top = jnp.max(scores, axis=1, keepdims=True)
                new_top = chunk_top if top is None else jnp.maximum(top, chunk_top)
                some = dot(jnp.exp(scores - new_top).astype(bf16), vals)
                total = some if top is None else total * jnp.exp(top - new_top) + some
                top = new_top
            weight_sum = total[:, LANES : LANES + 1]
            outs.append(total[:, :LANES] / weight_sum)
            high, mid, low = split_three(-(top + jnp.log(weight_sum)))
            ext = jnp.where(lane == FRAMES, high, seen)
            ext = jnp.where(lane == FRAMES + 1, mid, ext)
            ext_heads.append(jnp.where(lane == FRAMES + 2, low, ext).astype(bf16))
        out = jnp.where(lane < HDIM, outs[0], outs[1]).astype(bf16)
        for i in range(joined):
            here = slice(i * rows_part, (i + 1) * rows_part)
            o_ref[t * joined + i] = out[here, :]
            for h in range(2):
                ext_ref[h, t * joined + i] = ext_heads[h][here, :]
        return carry

    lax.fori_loop(0, blocks // joined, step, 0)


def attend(heads, visible, patches, first, frames_part, tile=1024, chunk=1024):
    blocks, _, rows, _ = heads.shape
    rows_part = frames_part * patches
    keys = blocks * rows
    joined = blocks
    while joined * rows_part > tile:
        joined //= 2
    return pl.pallas_call(
        functools.partial(
            attend_kernel, first, rows_part, patches, joined, chunk // rows
        ),
        out_shape=[
            pltpu.HBM((blocks, rows_part, LANES), bf16),
            pltpu.HBM((2, blocks, rows_part, LANES), bf16),
        ],
        in_specs=[pl.BlockSpec(memory_space=VMEM)] * 2,
        out_specs=[pl.BlockSpec(memory_space=VMEM)] * 2,
        compiler_params=pltpu.CompilerParams(vmem_limit_bytes=48 * MIB),
        cost_estimate=pl.CostEstimate(
            flops=8 * blocks * rows_part * keys * 2 * LANES,
            bytes_accessed=4 * MIB,
            transcendentals=0,
        ),
        name="attend",
    )(heads, visible)


def attend_back_kernel(parts, query_parts, part, patches, joined, together, carried, last, *refs):
    at = 0

    def take(count):
        nonlocal at
        found = refs[at : at + count]
        at += count
        return found

    (qkv_ref, do_ref) = take(2)
    ext_refs, o_refs = take(query_parts), take(query_parts)
    ctime_ref, stime_ref, cpatch_ref, spatch_ref = take(4)
    if carried:
        carry_ref, mix_ref = take(2)
    if last:
        (grads_ref,) = take(1)
    else:
        grads_ref, carry_out, mix_ref = take(3)
    (dq_turned,) = refs[at:]
    blocks, _, rows, _ = qkv_ref.shape
    rows_part = rows // parts
    frames, frames_part = rows // patches, rows_part // patches
    if carried:
        dq_turned[...] = carry_ref[...]
    else:
        dq_turned[...] = jnp.zeros_like(dq_turned)
        for b in range(blocks):
            at = 0
            for o_ref in o_refs:
                size = o_ref.shape[1]
                there = slice(at, at + size)
                at += size
                lane = lax.broadcasted_iota(jnp.int32, (size, LANES), 1)
                mixed = do_ref[b, there, :].astype(f32) * o_ref[b].astype(f32)
                for h in range(2):
                    mine = jnp.where((lane >= HDIM) == (h == 1), mixed, 0.0)
                    high, mid, low = split_three(-jnp.sum(mine, axis=1, keepdims=True))
                    ext = jnp.where(lane == 1, mid, jnp.where(lane == 2, low, 0.0))
                    mix_ref[h, b, there, :] = jnp.where(lane == 0, high, ext).astype(bf16)
    key_rows = slice(part * rows_part, (part + 1) * rows_part)
    key_lane = lax.broadcasted_iota(jnp.int32, (together * rows_part, LANES), 1)
    mix_keys = jnp.where(key_lane < 3, 1.0, 0.0).astype(bf16)

    def back(value, row, half):
        cosine = ctime_ref[pl.ds(row, 1), :] + cpatch_ref[half]
        sine = stime_ref[pl.ds(row, 1), :] + spatch_ref[half]
        return rotate_lanes(value, cosine, -sine).astype(bf16)

    first = rows if last else 0

    def step(t, carry):
        key_blocks = [t * together + i for i in range(together)]
        keys = jnp.concatenate([qkv_ref[b, 1, key_rows, :] for b in key_blocks], axis=0)
        keys = keys * score_scale
        vals = jnp.concatenate([qkv_ref[b, 2, key_rows, :] for b in key_blocks], axis=0)
        turned = keys.astype(f32).T.astype(bf16)
        extra = jnp.concatenate(
            [
                key_extra((b // 2) * frames + part * frames_part, rows_part, patches)
                for b in key_blocks
            ],
            axis=0,
        )
        key_tiles, val_tiles = [], []
        for h in range(2):
            mine = (key_lane >= HDIM) == (h == 1)
            none = jnp.zeros_like(keys)
            key_tiles.append(
                jnp.concatenate([jnp.where(mine, keys, none).astype(bf16), extra], axis=1)
            )
            val_tiles.append(jnp.concatenate([jnp.where(mine, vals, none), mix_keys], axis=1))
        dk = [jnp.zeros((together * rows_part, LANES), f32)] * 2
        dv = [jnp.zeros((together * rows_part, LANES), f32)] * 2
        for c in range(0, blocks, joined):
            some = range(c, c + joined)
            span = slice(c * rows, (c + joined) * rows)
            query = jnp.concatenate([qkv_ref[b, 0] for b in some], axis=0)
            grad = jnp.concatenate([do_ref[b] for b in some], axis=0)
            for h in range(2):
                ext = jnp.concatenate([ext_ref[h, b] for b in some for ext_ref in ext_refs], axis=0)
                mix = jnp.concatenate([mix_ref[h, b] for b in some], axis=0)
                probs = jnp.exp(dot(key_tiles[h], jnp.concatenate([query, ext], axis=1), NT))
                dv[h] = dv[h] + dot(probs.astype(bf16), grad)
                moved = dot(val_tiles[h], jnp.concatenate([grad, mix], axis=1), NT)
                grad_scores = (probs * moved).astype(bf16)
                dk[h] = dk[h] + dot(grad_scores, query)
                head = slice(HDIM * h, HDIM * (h + 1))
                dq_turned[head, span] += dot(turned[head, :], grad_scores)
        dk = jnp.where(key_lane < HDIM, dk[0], dk[1]) * score_scale
        dv = jnp.where(key_lane < HDIM, dv[0], dv[1]).astype(bf16)
        for i, b in enumerate(key_blocks):
            for f in range(frames_part):
                rows_here = slice(i * rows_part + f * patches, i * rows_part + (f + 1) * patches)
                row = b * frames + part * frames_part + f
                keys_here = slice(first + f * patches, first + (f + 1) * patches)
                grads_ref[b, keys_here, :] = back(dk[rows_here, :], row, b % 2)
            grads_ref[b, first + rows_part : first + 2 * rows_part, :] = dv[
                i * rows_part : (i + 1) * rows_part, :
            ]
        return carry

    lax.fori_loop(0, blocks // together, step, 0)

    if last:
        for b in range(blocks):
            for f in range(frames):
                there = slice(b * rows + f * patches, b * rows + (f + 1) * patches)
                turned_back = back(dq_turned[:, there].T, b * frames + f, b % 2)
                grads_ref[b, f * patches : (f + 1) * patches, :] = turned_back
    else:
        carry_out[...] = dq_turned[...]


def attend_back(heads, grads, exts, outs, rotary, carry, part, parts, patches, chunk=2048, together=2):
    last = part == parts - 1
    blocks, _, rows, _ = heads.shape
    rows_part = rows // parts
    total = blocks * rows
    operands = [heads, grads, *exts, *outs, *rotary, *(carry or ())]
    kept = 2 * rows_part + (rows if last else 0)
    out_shape = [pltpu.HBM((blocks, kept, LANES), bf16)]
    if not last:
        out_shape.append(jax.ShapeDtypeStruct((LANES, total), f32))
        out_shape.append(jax.ShapeDtypeStruct((2, blocks, rows, LANES), bf16))
    return pl.pallas_call(
        functools.partial(
            attend_back_kernel,
            parts,
            len(exts),
            part,
            patches,
            chunk // rows,
            together,
            carry is not None,
            last,
        ),
        out_shape=out_shape,
        in_specs=[pl.BlockSpec(memory_space=VMEM)] * len(operands),
        out_specs=[pl.BlockSpec(memory_space=VMEM)] * len(out_shape),
        scratch_shapes=[VMEM((LANES, total), f32)],
        compiler_params=pltpu.CompilerParams(vmem_limit_bytes=56 * MIB),
        cost_estimate=pl.CostEstimate(
            flops=20 * total * blocks * rows_part * 2 * LANES,
            bytes_accessed=8 * MIB,
            transcendentals=0,
        ),
        name="attend_back",
    )(*operands)


def act_grad_kernel(cot_ref, gate_ref, down_ref, grad_ref, out_ref):
    frames, patches, _ = cot_ref.shape

    @pl.when(pl.program_id(0) == 0)
    def _():
        for f in range(frames):
            grad = gate_ref[f : f + 1, :] * cot_ref[f].astype(f32)
            grad_ref[f * patches : (f + 1) * patches, :] = grad.astype(bf16)

    out_ref[...] = dot(grad_ref[...], down_ref[...], NT)


def act_grad(cotangent, gate_two, down_weight, cols=512):
    frames, patches, width = cotangent.shape
    rows, inner = frames * patches, down_weight.shape[0]
    return pl.pallas_call(
        act_grad_kernel,
        out_shape=[
            jax.ShapeDtypeStruct((rows, width), bf16),
            pltpu.HBM((rows, inner), f32),
        ],
        grid=(inner // cols,),
        in_specs=[
            whole(cotangent.shape),
            whole(gate_two.shape),
            pl.BlockSpec((cols, width), lambda c: (c, 0)),
        ],
        out_specs=[whole((rows, width)), pl.BlockSpec((rows, cols), lambda c: (0, c))],
        compiler_params=pltpu.CompilerParams(vmem_limit_bytes=40 * MIB),
        cost_estimate=pl.CostEstimate(
            flops=2 * rows * width * inner, bytes_accessed=18 * MIB, transcendentals=0
        ),
        name="act_grad",
    )(cotangent, gate_two, down_weight)


def feed_kernel(hid_ref, grad_ref, actgrad_ref, up_ref, bias_ref, down_ref,
                branch_ref, back_ref, biasgrad_ref, joined_ref,
                hid_turned, up_slots, down_slots, up_sems, down_sems):
    step, steps = pl.program_id(0), pl.num_programs(0)
    width, cols = up_ref.shape
    group, clips, _, share, _ = joined_ref.shape
    some_clips, quarters = down_slots.shape[2:4]
    up_parts = width // cols
    slot = step % 2

    def copies(at):
        across = pl.ds(pl.multiple_of((at % up_parts) * cols, cols), cols)
        up_copy = pltpu.make_async_copy(
            up_slots.at[at % 2], joined_ref.at[:, :, at // up_parts, :, across], up_sems.at[at % 2]
        )
        down_copy = pltpu.make_async_copy(
            down_slots.at[at % 2],
            joined_ref.at[:, pl.ds(at * some_clips, some_clips), quarters : 2 * quarters],
            down_sems.at[at % 2],
        )
        return up_copy, down_copy

    @pl.when(step == 0)
    def _():
        hid_turned[...] = hid_ref[...].T

    @pl.when(step >= 2)
    def _():
        for copy in copies(step - 2):
            copy.wait()

    pre = dot(hid_ref[...], up_ref[...]) + bias_ref[...]
    square = pre * pre
    bend = jnp.tanh(pre * (0.7978845608 + (0.7978845608 * 0.044715) * square))
    half = 0.5 * (1.0 + bend)
    act = (pre * half).astype(bf16)
    slope = half + (0.5 * pre) * (1.0 - bend * bend) * (
        0.7978845608 + (0.7978845608 * 3.0 * 0.044715) * square
    )
    pre_grad = (slope * actgrad_ref[...]).astype(bf16)
    biasgrad_ref[...] = jnp.sum(pre_grad.astype(f32), axis=0, keepdims=True)
    branch = dot(act, down_ref[...])
    back = dot(pre_grad, up_ref[...], NT)
    up_grad = dot(hid_turned[...], pre_grad).astype(bf16)
    up_grad = up_grad.reshape(clips, group, share, cols)
    for c in range(clips):
        up_slots[slot, :, c] = up_grad[c]
    down_grad = dot(act.T, grad_ref[...]).astype(bf16)
    down_grad = down_grad.reshape(some_clips, group, quarters, share, width)
    for c in range(some_clips):
        down_slots[slot, :, c] = down_grad[c]

    @pl.when(step == 0)
    def _():
        branch_ref[...] = branch
        back_ref[...] = back

    @pl.when(step > 0)
    def _():
        branch_ref[...] += branch
        back_ref[...] += back

    for copy in copies(step):
        copy.start()

    @pl.when(step == steps - 1)
    def _():
        for at in (steps - 2, steps - 1):
            for copy in copies(at):
                copy.wait()


def feed_forward(hidden, grad, grad_act, up_weight, up_bias, down_weight, group, clips, cols=1024):
    rows, width = hidden.shape
    inner = up_weight.shape[1]
    share, quarters = width // (group * clips), inner // width
    some_clips = cols * clips // inner
    return pl.pallas_call(
        feed_kernel,
        out_shape=[
            jax.ShapeDtypeStruct((rows, width), f32),
            jax.ShapeDtypeStruct((rows, width), f32),
            jax.ShapeDtypeStruct((1, inner), f32),
            jax.ShapeDtypeStruct((group, clips, 2 * quarters + 1, share, width), bf16),
        ],
        grid=(inner // cols,),
        in_specs=[
            whole((rows, width)),
            whole((rows, width)),
            pl.BlockSpec((rows, cols), lambda c: (0, c)),
            pl.BlockSpec((width, cols), lambda c: (0, c)),
            pl.BlockSpec((1, cols), lambda c: (0, c)),
            pl.BlockSpec((cols, width), lambda c: (c, 0)),
        ],
        out_specs=[
            whole((rows, width)),
            whole((rows, width)),
            pl.BlockSpec((1, cols), lambda c: (0, c)),
            pl.BlockSpec(memory_space=pl.ANY),
        ],
        scratch_shapes=[
            VMEM((width, rows), bf16),
            VMEM((2, group, clips, share, cols), bf16),
            VMEM((2, group, some_clips, quarters, share, width), bf16),
            pltpu.SemaphoreType.DMA((2,)),
            pltpu.SemaphoreType.DMA((2,)),
        ],
        compiler_params=pltpu.CompilerParams(vmem_limit_bytes=58 * MIB),
        cost_estimate=pl.CostEstimate(
            flops=10 * rows * width * inner, bytes_accessed=44 * MIB, transcendentals=0
        ),
        name="feed_forward",
    )(hidden, grad, grad_act, up_weight, up_bias, down_weight)


def proj_grad_kernel(attn_ref, grad_ref, _, joined_ref):
    group, clips, _, share, width = joined_ref.shape
    grad = dot(attn_ref[...].T, grad_ref[...]).astype(bf16).reshape(clips, group, share, width)
    for c in range(clips):
        joined_ref[:, c, 0] = grad[c]


def proj_weight_grad(attn_low, grad_proj, joined):
    rows, width = attn_low.shape
    group, clips, entries, share, _ = joined.shape
    return pl.pallas_call(
        proj_grad_kernel,
        out_shape=jax.ShapeDtypeStruct(joined.shape, joined.dtype),
        grid=(1,),
        in_specs=[
            whole((rows, width)),
            whole((rows, width)),
            pl.BlockSpec(memory_space=pl.ANY),
        ],
        out_specs=pl.BlockSpec((group, clips, 1, share, width), lambda c: (0, 0, entries - 1, 0, 0)),
        input_output_aliases={2: 0},
        compiler_params=pltpu.CompilerParams(vmem_limit_bytes=40 * MIB),
        cost_estimate=pl.CostEstimate(
            flops=2 * rows * width * width, bytes_accessed=4 * MIB, transcendentals=0
        ),
        name="proj_weight_grad",
    )(attn_low, grad_proj, joined)


def merge_kernel(*refs):
    parts = len(refs) - 10
    att_refs = refs[:parts]
    (weight_ref, bias_ref, tok_ref, gate_one_ref, shift_ref, scale_ref,
     low_ref, proj_ref, after_ref, hid_ref) = refs[parts:]
    frames, patches, width = tok_ref.shape
    pairs = att_refs[0].shape[0]
    at = 0
    for att_ref in att_refs:
        low = jnp.concatenate([att_ref[p] for p in range(pairs)], axis=1)
        rows_part = att_ref.shape[1]
        there = slice(at, at + rows_part)
        low_ref[there, :] = low
        proj = dot(low, weight_ref[...]) + bias_ref[...]
        proj_ref[there, :] = proj
        for j in range(rows_part // patches):
            f = at // patches + j
            here = slice(f * patches, (f + 1) * patches)
            row = slice(f, f + 1)
            after = tok_ref[f].astype(f32) + gate_one_ref[row, :] * proj[
                j * patches : (j + 1) * patches, :
            ]
            after_ref[here, :] = after
            centre = after - jnp.mean(after, axis=1, keepdims=True)
            inv = lax.rsqrt(jnp.mean(centre * centre, axis=1, keepdims=True) + norm_eps)
            hid = centre * inv * (1.0 + scale_ref[row, :]) + shift_ref[row, :]
            hid_ref[here, :] = hid.astype(bf16)
        at += rows_part


def merge_heads(attended, proj_weight, proj_bias, tokens, mods):
    frames, patches, width = tokens.shape
    rows = frames * patches
    operands = [*attended, proj_weight, proj_bias, tokens, *mods]
    return pl.pallas_call(
        merge_kernel,
        out_shape=[
            jax.ShapeDtypeStruct((rows, width), bf16),
            jax.ShapeDtypeStruct((rows, width), f32),
            jax.ShapeDtypeStruct((rows, width), f32),
            pltpu.HBM((rows, width), bf16),
        ],
        in_specs=[pl.BlockSpec(memory_space=VMEM)] * len(operands),
        out_specs=[pl.BlockSpec(memory_space=VMEM)] * 4,
        compiler_params=pltpu.CompilerParams(vmem_limit_bytes=48 * MIB),
        cost_estimate=pl.CostEstimate(
            flops=2 * rows * width * width, bytes_accessed=16 * MIB, transcendentals=0
        ),
        name="merge_heads",
    )(*operands)


def column_sum(value):
    return jnp.sum(value, axis=0, keepdims=True)


def unmerge_kernel(back_ref, after_ref, cot_ref, gate_one_ref, scale_ref, weight_ref,
                   grad_ref, gproj_ref, parts_ref):
    frames, patches, width = cot_ref.shape
    for f in range(frames):
        here = slice(f * patches, (f + 1) * patches)
        row = slice(f, f + 1)
        after = after_ref[here, :]
        centre = after - jnp.mean(after, axis=1, keepdims=True)
        inv = lax.rsqrt(jnp.mean(centre * centre, axis=1, keepdims=True) + norm_eps)
        normed = centre * inv
        scaled = back_ref[here, :] * (1.0 + scale_ref[row, :])
        mean_grad = jnp.mean(scaled, axis=1, keepdims=True)
        mean_mix = jnp.mean(scaled * normed, axis=1, keepdims=True)
        grad = cot_ref[f].astype(f32) + inv * (scaled - mean_grad - normed * mean_mix)
        grad_ref[here, :] = grad
        gproj_ref[here, :] = (gate_one_ref[row, :] * grad).astype(bf16)
    step = 2 * patches
    for i in range(frames * patches // step):
        here = slice(i * step, (i + 1) * step)
        part = dot(gproj_ref[here, :], weight_ref[...], NT).astype(bf16)
        for p in range(parts_ref.shape[0]):
            parts_ref[p, here, :] = part[:, p * LANES : (p + 1) * LANES]


def unmerge_heads(back, after, cotangent, gate_one, scale_two, proj_weight):
    frames, patches, width = cotangent.shape
    rows = frames * patches
    operands = [back, after, cotangent, gate_one, scale_two, proj_weight]
    return pl.pallas_call(
        unmerge_kernel,
        out_shape=[
            pltpu.HBM((rows, width), f32),
            jax.ShapeDtypeStruct((rows, width), bf16),
            pltpu.HBM((width // LANES, rows, LANES), bf16),
        ],
        in_specs=[pl.BlockSpec(memory_space=VMEM)] * len(operands),
        out_specs=[pl.BlockSpec(memory_space=VMEM)] * 3,
        compiler_params=pltpu.CompilerParams(vmem_limit_bytes=48 * MIB),
        cost_estimate=pl.CostEstimate(
            flops=2 * rows * width * width, bytes_accessed=12 * MIB, transcendentals=0
        ),
        name="unmerge_heads",
    )(*operands)


def side_kernel(branch_ref, back_ref, after_ref, proj_ref, cot_ref, gate_two_ref, bias_ref,
                grad_ref, gproj_ref, gbranch_ref, out_ref, sums_ref, biases_ref):
    f, frames = pl.program_id(0), pl.num_programs(0)
    cot = cot_ref[0].astype(f32)
    after = after_ref[...]
    branch = branch_ref[...] + bias_ref[...]
    out_ref[0] = (after + gate_two_ref[pl.ds(f, 1), :] * branch).astype(bf16)
    centre = after - jnp.mean(after, axis=1, keepdims=True)
    inv = lax.rsqrt(jnp.mean(centre * centre, axis=1, keepdims=True) + norm_eps)
    back = back_ref[...]
    for kind, term in enumerate(
        (grad_ref[...] * proj_ref[...], back, back * (centre * inv), cot * branch)
    ):
        sums_ref[pl.ds(kind * frames + f, 1), :] = column_sum(term)

    @pl.when(f == 0)
    def _():
        biases_ref[...] = jnp.zeros_like(biases_ref)

    biases_ref[0:1, :] += column_sum(gproj_ref[...].astype(f32))
    biases_ref[1:2, :] += column_sum(gbranch_ref[...].astype(f32))


def side_sums(branch, back, after, proj, cotangent, gate_two, down_bias, grad_after, grad_proj,
              grad_branch):
    frames, patches, width = cotangent.shape
    rows = pl.BlockSpec((patches, width), lambda f: (f, 0))
    slot = pl.BlockSpec((1, patches, width), lambda f: (f, 0, 0))
    return pl.pallas_call(
        side_kernel,
        out_shape=[
            jax.ShapeDtypeStruct((frames, patches, width), bf16),
            jax.ShapeDtypeStruct((4 * frames, width), f32),
            jax.ShapeDtypeStruct((2, width), f32),
        ],
        grid=(frames,),
        in_specs=[rows, rows, rows, rows, slot, whole(gate_two.shape), whole(down_bias.shape), rows,
                  rows, rows],
        out_specs=[slot, whole((4 * frames, width)), whole((2, width))],
        compiler_params=pltpu.CompilerParams(vmem_limit_bytes=48 * MIB),
        cost_estimate=pl.CostEstimate(flops=0, bytes_accessed=16 * MIB, transcendentals=0),
        name="side_sums",
    )(
        in_hbm(branch),
        in_hbm(back),
        in_hbm(after),
        in_hbm(proj),
        cotangent,
        gate_two,
        down_bias,
        grad_after,
        grad_proj,
        in_hbm(grad_branch),
    )


def heads_grad_kernel(hid_ref, first_ref, last_ref, out_ref, bias_ref, total):
    rows = hid_ref.shape[2]
    rows_part = first_ref.shape[1] // 2
    grad = jnp.concatenate(
        [
            last_ref[0, :rows, :],
            jnp.concatenate(
                [first_ref[0, :rows_part, :], last_ref[0, rows : rows + rows_part, :]], axis=0
            ),
            jnp.concatenate([first_ref[0, rows_part:, :], last_ref[0, rows + rows_part :, :]], axis=0),
        ],
        axis=1,
    )
    some = dot(hid_ref[0], grad)
    some_bias = column_sum(grad.astype(f32))

    @pl.when(pl.program_id(0) == 0)
    def _():
        total[...] = some
        bias_ref[...] = some_bias

    @pl.when(pl.program_id(0) > 0)
    def _():
        total[...] += some
        bias_ref[...] += some_bias

    @pl.when(pl.program_id(0) == pl.num_programs(0) - 1)
    def _():
        devices, triple, _ = out_ref.shape
        share = triple // 3
        for k in range(3):
            part = total[:, k * LANES : (k + 1) * LANES].astype(bf16)
            out_ref[:, k * share : (k + 1) * share, :] = part.reshape(devices, share, LANES)


def heads_grad(hidden_clip, first, last, devices):
    blocks, width, rows = hidden_clip.shape
    shape = (devices, 3 * width // devices, LANES)
    return pl.pallas_call(
        heads_grad_kernel,
        out_shape=[
            jax.ShapeDtypeStruct(shape, bf16),
            jax.ShapeDtypeStruct((1, 3 * LANES), f32),
        ],
        grid=(blocks,),
        in_specs=[
            pl.BlockSpec((1, width, rows), lambda b: (b, 0, 0)),
            pl.BlockSpec((1,) + first.shape[1:], lambda b: (b, 0, 0)),
            pl.BlockSpec((1,) + last.shape[1:], lambda b: (b, 0, 0)),
        ],
        out_specs=[whole(shape), whole((1, 3 * LANES))],
        scratch_shapes=[VMEM((width, 3 * LANES), f32)],
        compiler_params=pltpu.CompilerParams(vmem_limit_bytes=40 * MIB),
        cost_estimate=pl.CostEstimate(
            flops=6 * blocks * rows * width * LANES, bytes_accessed=12 * MIB, transcendentals=0
        ),
        name="heads_grad",
    )(in_hbm(hidden_clip), first, last)


def finish_kernel(first_ref, last_ref, wq_ref, wk_ref, wv_ref, tok_ref, scale_ref, after_ref,
                  partbias_ref, out_ref, send_ref, total):
    frames, patches, width = tok_ref.shape
    rows = frames * patches
    rows_part = first_ref.shape[1] // 2
    step = pl.program_id(0)
    query, keys, vals = [], [], []
    for p in range(first_ref.shape[0]):
        query.append(last_ref[p, :rows, :])
        keys.append(
            jnp.concatenate(
                [first_ref[p, :rows_part, :], last_ref[p, rows : rows + rows_part, :]], axis=0
            )
        )
        vals.append(
            jnp.concatenate([first_ref[p, rows_part:, :], last_ref[p, rows + rows_part :, :]], axis=0)
        )
    some = None
    for grads, weight_ref in ((query, wq_ref), (keys, wk_ref), (vals, wv_ref)):
        term = dot(jnp.concatenate(grads, axis=1), weight_ref[...], NT)
        some = term if some is None else some + term

    @pl.when(step == 0)
    def _():
        total[...] = some

    @pl.when(step > 0)
    def _():
        total[...] += some

    @pl.when(step == pl.num_programs(0) - 1)
    def _():
        shift_sums, scale_sums = [], []
        for f in range(frames):
            here = slice(f * patches, (f + 1) * patches)
            x = tok_ref[f].astype(f32)
            centre = x - jnp.mean(x, axis=1, keepdims=True)
            inv = lax.rsqrt(jnp.mean(centre * centre, axis=1, keepdims=True) + norm_eps)
            normed = centre * inv
            back = total[here, :]
            shift_sums.append(column_sum(back))
            scale_sums.append(column_sum(back * normed))
            scaled = back * (1.0 + scale_ref[f : f + 1, :])
            mean_grad = jnp.mean(scaled, axis=1, keepdims=True)
            mean_mix = jnp.mean(scaled * normed, axis=1, keepdims=True)
            grad = after_ref[here, :] + inv * (scaled - mean_grad - normed * mean_mix)
            out_ref[f] = grad.astype(bf16)
        sums = jnp.concatenate(shift_sums + scale_sums, axis=0)
        sums = jnp.concatenate(
            [sums[:, i : i + LANES] for i in range(0, width, LANES)], axis=0
        ).astype(bf16)
        bias = [partbias_ref[:, k * LANES : (k + 1) * LANES] for k in range(3)]
        high = [value.astype(bf16).astype(f32) for value in bias]
        low = [value - upper for value, upper in zip(bias, high)]
        bias = jnp.concatenate(high + low + [jnp.zeros((10, LANES), f32)], axis=0).astype(bf16)
        count = sums.shape[0]
        for d in range(send_ref.shape[0]):
            send_ref[d, :count, :] = sums
            send_ref[d, count:, :] = bias


def finish(first, last, qkv_weight, tokens, scale_one, grad_after, part_bias, copies, cols=256):
    frames, patches, width = tokens.shape
    rows = frames * patches
    steps, some = width // cols, cols // LANES

    send_shape = (copies, 2 * frames * (width // LANES) + 16, LANES)

    def column(third):
        return lambda c: (0, third * steps + c)

    return pl.pallas_call(
        finish_kernel,
        out_shape=[
            jax.ShapeDtypeStruct((frames, patches, width), bf16),
            pltpu.HBM(send_shape, bf16),
        ],
        grid=(steps,),
        in_specs=[
            pl.BlockSpec((some,) + first.shape[1:], lambda c: (c, 0, 0)),
            pl.BlockSpec((some,) + last.shape[1:], lambda c: (c, 0, 0)),
        ]
        + [pl.BlockSpec((width, cols), column(part)) for part in range(3)]
        + [whole(tokens.shape), whole(scale_one.shape), whole((rows, width))]
        + [whole(part_bias.shape)],
        out_specs=[whole((frames, patches, width)), whole(send_shape)],
        scratch_shapes=[VMEM((rows, width), f32)],
        compiler_params=pltpu.CompilerParams(vmem_limit_bytes=48 * MIB),
        cost_estimate=pl.CostEstimate(
            flops=6 * rows * width * width, bytes_accessed=16 * MIB, transcendentals=0
        ),
        name="finish",
    )(first, last, *[qkv_weight] * 3, tokens, scale_one, grad_after, part_bias)


def unpack_kernel(summed_ref, up_ref, down_ref, proj_ref):
    entries, share, width = summed_ref.shape
    quarters = entries // 2
    for i in range(quarters):
        up_ref[:, i * width : (i + 1) * width] = summed_ref[i].astype(f32)
        down_ref[i * share : (i + 1) * share, :] = summed_ref[quarters + i].astype(f32)
    proj_ref[...] = summed_ref[2 * quarters].astype(f32)


def unpack(summed):
    entries, share, width = summed.shape
    quarters = entries // 2
    return pl.pallas_call(
        unpack_kernel,
        out_shape=[
            jax.ShapeDtypeStruct((share, quarters * width), f32),
            jax.ShapeDtypeStruct((quarters * share, width), f32),
            jax.ShapeDtypeStruct((share, width), f32),
        ],
        in_specs=[pl.BlockSpec(memory_space=VMEM)],
        out_specs=[pl.BlockSpec(memory_space=VMEM)] * 3,
        name="unpack",
    )(summed)


def last_kernel(clips, frames, got_ref, member_ref, cols_ref, early_ref, earlysum_ref,
                rows_ref, bias_ref, ada_ref, adasum_ref):
    group = got_ref.shape[0]
    share, width = rows_ref.shape[0], rows_ref.shape[1] // 3
    tiles = width // LANES
    count = 2 * frames * tiles
    starts = [3 * share + c * (count + 16) for c in range(clips)]
    some = 4 * frames
    ada_ref[:, 2 * width :] = early_ref[...]
    adasum_ref[:, 2 * width :] = earlysum_ref[...]
    for i in range(tiles // 2):
        sums = jnp.concatenate(
            [
                got_ref[:, at + i * some : at + (i + 1) * some, :].reshape(group * some, LANES)
                for at in starts
            ],
            axis=0,
        )
        for j in range(2):
            for kind in range(2):
                level = dot(member_ref[2 * j + kind], sums).astype(bf16)
                at = kind * width + (2 * i + j) * LANES
                ada_ref[:, at : at + LANES] = dot(cols_ref[...], level)
                adasum_ref[:, at : at + LANES] = column_sum(level.astype(f32))
    for p in range(group):
        bias = None
        for at in starts:
            term = got_ref[p, at + count : at + count + 16, :].astype(f32)
            bias = term if bias is None else bias + term
        for third in range(3):
            at = third * width + p * LANES
            here = slice(third * share, (third + 1) * share)
            rows_ref[:, at : at + LANES] = got_ref[p, here, :].astype(f32)
            bias_ref[:, at : at + LANES] = bias[third : third + 1, :] + bias[third + 3 : third + 4, :]


def last_sums(got, member, columns, early, early_sum, clips, frames):
    share, width = early.shape[0], early.shape[1] // 4
    return pl.pallas_call(
        functools.partial(last_kernel, clips, frames),
        out_shape=[
            jax.ShapeDtypeStruct((share, 3 * width), f32),
            jax.ShapeDtypeStruct((1, 3 * width), f32),
            jax.ShapeDtypeStruct((share, 6 * width), f32),
            jax.ShapeDtypeStruct((1, 6 * width), f32),
        ],
        in_specs=[pl.BlockSpec(memory_space=VMEM)] * 5,
        out_specs=[pl.BlockSpec(memory_space=VMEM)] * 4,
        compiler_params=pltpu.CompilerParams(vmem_limit_bytes=48 * MIB),
        cost_estimate=pl.CostEstimate(flops=0, bytes_accessed=4 * MIB, transcendentals=0),
        name="last_sums",
    )(got, member, columns, early, early_sum)


def body(
    tokens,
    out_cotangent,
    level_embed,
    ada_weight,
    ada_bias,
    qkv_weight,
    qkv_bias,
    proj_weight,
    proj_bias,
    up_weight,
    up_bias,
    down_weight,
    down_bias,
    context_count,
    frame_level,
    slot_time,
):
    frames, patches, width = tokens.shape
    rows = frames * patches
    inner = up_weight.shape[1]
    frm_count, sp_count = lax.axis_size("frm"), lax.axis_size("sp")
    devices = frm_count * sp_count
    group = FRAMES // frames * sp_count
    clips = devices // group
    frm, sp = lax.axis_index("frm"), lax.axis_index("sp")
    me = frm * sp_count + sp
    clip = me // group
    clip_groups = [list(range(first, first + group)) for first in range(0, devices, group)]
    across_clips = [list(range(first, devices, group)) for first in range(group)]
    everyone = [list(range(devices))]
    halves = 2
    share = width // devices
    per_dest = inner // devices

    levels_here = level_embed.shape[0]
    embed_all = to_everyone(level_embed, devices).reshape(devices * levels_here, width)

    clip_times = lax.dynamic_slice_in_dim(slot_time, clip * FRAMES, FRAMES)
    clip_levels = lax.dynamic_index_in_dim(frame_level, clip, 0, keepdims=False)
    context = lax.dynamic_index_in_dim(context_count, clip, 0, keepdims=False)
    seen = (clip_times[None, :] <= clip_times[:, None]) | (clip_times[None, :] < context)
    visible = jnp.pad(
        jnp.where(seen, 0.0, masked_out).astype(f32), ((0, 0), (0, LANES - FRAMES))
    )

    def by_blocks(table):
        table = table.reshape(FRAMES // frames, 1, frames, LANES)
        return jnp.broadcast_to(table, (FRAMES // frames, sp_count, frames, LANES)).reshape(
            group * frames, LANES
        )

    visible = by_blocks(visible)
    freq, sign, time_lane, row_lane = rotary_lanes()
    angle_time = clip_times.astype(f32)[:, None] * freq[None, :]
    ctime = by_blocks(jnp.where(time_lane[None, :], jnp.cos(angle_time), 0.0))
    stime = by_blocks(jnp.where(time_lane[None, :], jnp.sin(angle_time) * sign[None, :], 0.0))
    patch_ids = jnp.arange(sp_count * patches, dtype=jnp.int32).reshape(sp_count, patches)
    place = jnp.where(
        row_lane[None, None, :], (patch_ids // GRID)[..., None], (patch_ids % GRID)[..., None]
    )
    angle_patch = place.astype(f32) * freq[None, None, :]
    cpatch = jnp.where(time_lane, 0.0, jnp.cos(angle_patch))
    spatch = jnp.where(time_lane, 0.0, jnp.sin(angle_patch) * sign)
    rotary = [ctime, stime, cpatch, spatch]

    def my_table(time_part, patch_part):
        mine = lax.dynamic_slice_in_dim(time_part, me % group * frames, frames)
        half = lax.dynamic_index_in_dim(patch_part, sp, 0, keepdims=False)
        return (mine[:, None, :] + half[None]).reshape(rows, LANES)

    cosine, sine = my_table(ctime, cpatch), my_table(stime, spatch)

    my_times = lax.dynamic_slice_in_dim(slot_time, frm * frames, frames)
    my_levels = jnp.take(clip_levels, my_times)
    embed_act = jax.nn.silu(embed_all.astype(f32)).astype(bf16)
    level_ids = jnp.arange(devices * levels_here, dtype=jnp.int32)
    pick = (my_levels[:, None] == level_ids[None, :]).astype(bf16)
    my_embed = dot(pick, embed_act).astype(bf16)

    def modulation(embeds, first, count):
        here = slice(first * width, (first + count) * width)
        rows_mod = dot(embeds, ada_weight[:, here]) + ada_bias[here].astype(f32)
        rows_mod = lax.reduce_precision(rows_mod, 8, 7)
        return [rows_mod[:, i * width : (i + 1) * width] for i in range(count)]

    shift_one, scale_one = modulation(my_embed, 0, 2)

    hidden_turned, head_parts = project(
        tokens, shift_one, scale_one, qkv_weight, qkv_bias.astype(f32)[None, :], cosine, sine
    )

    my_embed, head_parts = lax.optimization_barrier((my_embed, head_parts))
    gate_one, shift_two, scale_two, gate_two = modulation(my_embed, 2, 4)
    heads = exchange(head_parts, clip_groups)
    grad_branch, grad_act = act_grad(out_cotangent, gate_two, down_weight)
    slot_ids = (jnp.arange(devices * frames, dtype=jnp.int32) // (sp_count * frames)) * frames
    slot_ids = slot_ids + jnp.arange(devices * frames, dtype=jnp.int32) % frames
    slot_levels = frame_level[slot_ids // FRAMES, slot_time[slot_ids]]
    member_of = (level_ids[:, None] == slot_levels[None, :]).astype(bf16)
    my_columns = lax.dynamic_slice_in_dim(embed_act, me * share, share, axis=1)
    which = jnp.arange(4, dtype=jnp.int32)
    member_last = jnp.where(
        (which[:, None] == which[None, :])[:, None, None, :, None],
        member_of.reshape(1, -1, devices, 1, frames),
        jnp.zeros((), bf16),
    ).reshape(4, -1, devices * 4 * frames)
    columns_turned = my_columns.T
    heads, grad_branch, grad_act, member_of, my_columns, member_last, columns_turned = (
        lax.optimization_barrier(
            (heads, grad_branch, grad_act, member_of, my_columns, member_last, columns_turned)
        )
    )
    outs, exts, attended = [], [], []
    for first, frames_part in ((0, frames - frames // 4), (frames - frames // 4, frames // 4)):
        out, ext = attend(heads, visible, patches, first, frames_part)
        visible, out = lax.optimization_barrier((visible, out))
        sent = out
        if attended:
            sent, attended[0] = lax.optimization_barrier((sent, attended[0]))
        outs.append(out)
        exts.append(ext)
        attended.append(exchange(sent, clip_groups))

    hidden_turned, _ = lax.optimization_barrier((hidden_turned, heads))
    hidden_clip = lax.all_gather(hidden_turned, AXES, axis_index_groups=clip_groups)

    attn_low, attn_proj, after_attn, hidden_two = merge_heads(
        attended,
        proj_weight,
        proj_bias.astype(f32)[None, :],
        tokens,
        (gate_one, shift_two, scale_two),
    )
    branch, grad_hidden_two, up_b_grad, joined = feed_forward(
        hidden_two,
        grad_branch,
        grad_act,
        up_weight,
        up_bias.astype(f32)[None, :],
        down_weight,
        group,
        clips,
    )
    grad_after, grad_proj, grad_parts = unmerge_heads(
        grad_hidden_two, after_attn, out_cotangent, gate_one, scale_two, proj_weight
    )
    grads = exchange(grad_parts, clip_groups)
    block_out, early_sums, early_biases = side_sums(
        branch,
        grad_hidden_two,
        after_attn,
        attn_proj,
        out_cotangent,
        gate_two,
        down_bias.astype(f32)[None, :],
        grad_after,
        grad_proj,
        grad_branch,
    )

    joined = proj_weight_grad(attn_low, grad_proj, joined)
    joined, hidden_clip = lax.optimization_barrier((joined, hidden_clip))
    summed = lax.psum_scatter(
        joined, AXES, scatter_dimension=0, axis_index_groups=clip_groups, tiled=True
    )[0]

    def slot_parts(slot_sums, biases):
        kinds = slot_sums.shape[0] // frames
        sums = slot_sums.reshape(kinds, frames, width).transpose(1, 0, 2).reshape(frames, -1)
        sums = jnp.broadcast_to(sums.astype(bf16)[None], (devices, frames, kinds * width))
        high = biases.astype(bf16)
        low = (biases - high.astype(f32)).astype(bf16)
        both = jnp.concatenate([high, low], axis=1).reshape(devices, frames, -1)
        lanes = -(-both.shape[2] // LANES) * LANES
        both = jnp.pad(both, ((0, 0), (0, 0), (0, lanes - both.shape[2])))
        return jnp.concatenate([sums, both], axis=2)

    def bias_share(got, count, size):
        extra = jnp.sum(got[:, :, count:].astype(f32), axis=0)
        extra = extra[:, : 2 * size // frames].reshape(-1)
        return extra[:size] + extra[size:]

    def level_out(got, count):
        slots = got[:, :, :count].reshape(devices * frames, count)
        level_grad = dot(member_of, slots).astype(bf16)
        return dot(my_columns, level_grad, TN), jnp.sum(level_grad.astype(f32), axis=0)

    early_parts = slot_parts(
        early_sums,
        jnp.concatenate(
            [
                up_b_grad.reshape(devices, per_dest),
                early_biases[0].reshape(devices, share),
                early_biases[1].reshape(devices, share),
            ],
            axis=1,
        ),
    )
    early_parts, _ = lax.optimization_barrier((early_parts, grads))
    early_got = exchange(early_parts, everyone)

    first_grads, carry, mixes = attend_back(
        heads, grads, exts, outs, rotary, None, 0, halves, patches
    )
    carry, early_got = lax.optimization_barrier((carry, early_got))
    own_first = exchange(first_grads, clip_groups)
    (last_grads,) = attend_back(
        heads, grads, exts, outs, rotary, (carry, mixes), 1, halves, patches
    )
    last_parts, own_first = lax.optimization_barrier((last_grads, own_first))
    own_last = exchange(last_parts, clip_groups)

    early_w, early_b = level_out(early_got, 4 * width)
    early_bias_out = bias_share(early_got, 4 * width, per_dest + 2 * share)

    qkv_part, qkv_b_part = heads_grad(hidden_clip, first_grads, last_grads, devices)
    qkv_part = qkv_part.reshape(clips, group, 3 * share, LANES)
    qkv_sum = lax.dynamic_index_in_dim(qkv_part, clip, 0, keepdims=False).astype(f32)
    for j in range(1, clips):
        some = lax.dynamic_index_in_dim(qkv_part, clip ^ j, 0, keepdims=False)
        pairs = [(source, source ^ (j * group)) for source in range(devices)]
        qkv_sum = qkv_sum + lax.ppermute(some, AXES, pairs).astype(f32)
    qkv_sum, own_last, summed = lax.optimization_barrier(
        (qkv_sum.astype(bf16), own_last, summed)
    )

    summed = lax.psum_scatter(
        summed, AXES, scatter_dimension=0, axis_index_groups=across_clips, tiled=True
    )[0]
    up_w_out, down_w_out, proj_w_out = unpack(summed)

    tokens_grad, last_send = finish(
        own_first, own_last, qkv_weight, tokens, scale_one, grad_after, qkv_b_part, clips
    )
    clip_got = exchange(last_send, across_clips).reshape(1, -1, LANES)
    clip_got = jnp.broadcast_to(clip_got, (group,) + clip_got.shape[1:])
    last_got = exchange(jnp.concatenate([qkv_sum, clip_got], axis=1), clip_groups)
    last_got, early_w, early_b, early_bias_out = lax.optimization_barrier(
        (last_got, early_w, early_b, early_bias_out)
    )
    up_b_out = early_bias_out[:per_dest]
    proj_b_out = early_bias_out[per_dest : per_dest + share]
    down_b_out = early_bias_out[per_dest + share :]
    qkv_w_out, qkv_b_all, ada_w_out, ada_b_all = last_sums(
        last_got, member_last, columns_turned, early_w, early_b[None, :], clips, frames
    )
    qkv_b_out = lax.dynamic_slice_in_dim(qkv_b_all[0], me * 3 * share, 3 * share)
    ada_b_all = ada_b_all[0]
    ada_share = ada_b_all.shape[0] // devices
    ada_b_out = lax.dynamic_slice_in_dim(ada_b_all, me * ada_share, ada_share)
    return (
        block_out,
        tokens_grad,
        ada_w_out,
        ada_b_out,
        qkv_w_out,
        qkv_b_out,
        proj_w_out,
        proj_b_out,
        up_w_out,
        up_b_out,
        down_w_out,
        down_b_out,
    )


def solution(mesh):
    tokens_spec = P("frm", "sp", None)
    rows_spec = P(AXES, None)
    vector_spec = P(AXES)
    return jax.shard_map(
        body,
        mesh=mesh,
        in_specs=(tokens_spec, tokens_spec, rows_spec) + (P(),) * 13,
        out_specs=(tokens_spec, tokens_spec) + (rows_spec, vector_spec) * 5,
        check_vma=False,
    )
```

```python
import functools
import math

import jax
import jax.numpy as jnp
import numpy as np
from jax import lax
from jax.experimental import pallas as pl
from jax.experimental.pallas import tpu as pltpu
from jax.sharding import PartitionSpec as P

HEADS = 16
HDIM = 64
FRAMES = 16
GRID = 16
LANES = 128
MIB = 2**20

norm_eps = 1e-06
masked_out = -1e30
score_scale = 0.125

f32 = jnp.float32
bf16 = jnp.bfloat16
NN = (((1,), (0,)), ((), ()))
NT = (((1,), (1,)), ((), ()))
TN = (((0,), (0,)), ((), ()))
AXES = ("frm", "sp")
VMEM = pltpu.VMEM


def dot(left_op, right_op, dims=NN):
    return lax.dot_general(left_op, right_op, dims, preferred_element_type=f32)


def exchange(value, groups):
    return lax.all_to_all(value, AXES, 0, 0, axis_index_groups=groups)


def to_everyone(value, devices):
    return exchange(
        jnp.broadcast_to(value[None], (devices,) + value.shape), [list(range(devices))]
    )


def rotary_lanes():
    lane = np.arange(LANES) % HDIM
    start = np.where(lane < 16, 0, np.where(lane < 40, 16, 40))
    half = np.where(lane < 16, 8, 12)
    offset = lane - start
    freq = np.exp((offset % half).astype(np.float32) * np.float32(-math.log(10000.0)) / half)
    sign = np.where(offset < half, -1.0, 1.0)
    return (
        freq.astype(np.float32),
        sign.astype(np.float32),
        (lane < 16),
        (lane >= 16) & (lane < 40),
    )


def rotate_lanes(value, cosine, sine):
    lane = lax.broadcasted_iota(jnp.int32, value.shape, 1) % HDIM
    near_first = pltpu.roll(value, LANES - 8, 1)
    near_second = pltpu.roll(value, 8, 1)
    far_first = pltpu.roll(value, LANES - 12, 1)
    far_second = pltpu.roll(value, 12, 1)
    in_first = (lane < 28) | ((lane >= 40) & (lane < 52))
    far = jnp.where(in_first, far_first, far_second)
    near = jnp.where(lane < 8, near_first, near_second)
    partner = jnp.where(lane < 16, near, far)
    return value * cosine + partner * sine


def project_kernel(tok_ref, shift_ref, scale_ref, wq_ref, wk_ref, wv_ref, bq_ref, bk_ref, bv_ref,
                   cos_ref, sin_ref, turned_ref, out_ref, hid_all):
    frames, patches, _ = tok_ref.shape

    @pl.when(pl.program_id(0) == 0)
    def _():
        for f in range(frames):
            here = slice(f * patches, (f + 1) * patches)
            x = tok_ref[f].astype(f32)
            centre = x - jnp.mean(x, axis=1, keepdims=True)
            inv = lax.rsqrt(jnp.mean(centre * centre, axis=1, keepdims=True) + norm_eps)
            hid = centre * inv * (1.0 + scale_ref[f : f + 1, :]) + shift_ref[f : f + 1, :]
            hid = hid.astype(bf16)
            hid_all[here, :] = hid
            turned_ref[:, here] = hid.T

    hid = hid_all[...]
    query = dot(hid, wq_ref[...]) + bq_ref[...]
    keys = dot(hid, wk_ref[...]) + bk_ref[...]
    vals = (dot(hid, wv_ref[...]) + bv_ref[...]).astype(bf16)
    for p in range(wq_ref.shape[1] // LANES):
        lanes = slice(p * LANES, (p + 1) * LANES)
        out_ref[p, 0] = rotate_lanes(query[:, lanes], cos_ref[...], sin_ref[...]).astype(bf16)
        out_ref[p, 1] = rotate_lanes(keys[:, lanes], cos_ref[...], sin_ref[...]).astype(bf16)
        out_ref[p, 2] = vals[:, lanes]


def in_hbm(value):
    return pltpu.with_memory_space_constraint(value, pltpu.HBM)


def whole(shape):
    return pl.BlockSpec(shape, lambda *_: (0,) * len(shape))


def project(tokens, shift_one, scale_one, qkv_weight, qkv_bias, cosine, sine, cols=256):
    frames, patches, width = tokens.shape
    rows = frames * patches
    pairs = width // LANES
    steps, some = width // cols, cols // LANES

    def column(part):
        return lambda c: (0, part * steps + c)

    return pl.pallas_call(
        project_kernel,
        out_shape=[
            pltpu.HBM((width, rows), bf16),
            pltpu.HBM((pairs, 3, rows, LANES), bf16),
        ],
        grid=(steps,),
        in_specs=[whole(tokens.shape), whole(shift_one.shape), whole(scale_one.shape)]
        + [pl.BlockSpec((width, cols), column(part)) for part in range(3)]
        + [pl.BlockSpec((1, cols), column(part)) for part in range(3)]
        + [whole((rows, LANES)), whole((rows, LANES))],
        out_specs=[
            whole((width, rows)),
            pl.BlockSpec((some, 3, rows, LANES), lambda c: (c, 0, 0, 0)),
        ],
        scratch_shapes=[VMEM((rows, width), bf16)],
        compiler_params=pltpu.CompilerParams(vmem_limit_bytes=40 * MIB),
        cost_estimate=pl.CostEstimate(
            flops=6 * rows * width * width, bytes_accessed=10 * MIB, transcendentals=0
        ),
        name="project",
    )(tokens, shift_one, scale_one, *[in_hbm(qkv_weight)] * 3, *[qkv_bias] * 3, cosine, sine)


def key_extra(first_frame, rows, patches):
    row = lax.broadcasted_iota(jnp.int32, (rows, LANES), 0)
    lane = lax.broadcasted_iota(jnp.int32, (rows, LANES), 1)
    hit = (lane == first_frame + row // patches) | ((lane >= FRAMES) & (lane < FRAMES + 3))
    return jnp.where(hit, 1.0, 0.0).astype(bf16)


def split_three(column):
    high = column.astype(bf16).astype(f32)
    rest = column - high
    mid = rest.astype(bf16).astype(f32)
    return high, mid, rest - mid


def attend_kernel(first, rows_part, patches, joined, joined_keys, qkv_ref, vis_ref, o_ref, ext_ref):
    blocks, _, rows, _ = qkv_ref.shape
    frames, frames_part = rows // patches, rows_part // patches
    tile, chunk = joined * rows_part, joined_keys * rows
    lane = lax.broadcasted_iota(jnp.int32, (tile, LANES), 1)
    mine_rows = slice(first * patches, first * patches + rows_part)
    ones = jnp.full((chunk, LANES), 1.0, bf16)

    def step(t, carry):
        query = jnp.concatenate(
            [qkv_ref[t * joined + i, 0, mine_rows, :] for i in range(joined)], axis=0
        )
        query = query * score_scale
        seen = jnp.concatenate(
            [
                jnp.broadcast_to(
                    vis_ref[pl.ds((t * joined + i) * frames + first + f, 1), :],
                    (patches, LANES),
                )
                for i in range(joined)
                for f in range(frames_part)
            ],
            axis=0,
        )
        outs, ext_heads = [], []
        for h in range(2):
            mine = jnp.where((lane >= HDIM) == (h == 1), query, jnp.zeros_like(query))
            query_ext = jnp.concatenate([mine.astype(bf16), seen.astype(bf16)], axis=1)
            top = None
            for c in range(0, blocks, joined_keys):
                some_blocks = range(c, c + joined_keys)
                keys = jnp.concatenate(
                    [
                        jnp.concatenate(
                            [qkv_ref[b, 1], key_extra((b // 2) * frames, rows, patches)], axis=1
                        )
                        for b in some_blocks
                    ],
                    axis=0,
                )
                vals = jnp.concatenate([qkv_ref[b, 2] for b in some_blocks], axis=0)
                vals = jnp.concatenate([vals, ones], axis=1)
                scores = dot(query_ext, keys, NT)
                chunk_top = jnp.max(scores, axis=1, keepdims=True)
                new_top = chunk_top if top is None else jnp.maximum(top, chunk_top)
                some = dot(jnp.exp(scores - new_top).astype(bf16), vals)
                total = some if top is None else total * jnp.exp(top - new_top) + some
                top = new_top
            weight_sum = total[:, LANES : LANES + 1]
            outs.append(total[:, :LANES] / weight_sum)
            high, mid, low = split_three(-(top + jnp.log(weight_sum)))
            ext = jnp.where(lane == FRAMES, high, seen)
            ext = jnp.where(lane == FRAMES + 1, mid, ext)
            ext_heads.append(jnp.where(lane == FRAMES + 2, low, ext).astype(bf16))
        out = jnp.where(lane < HDIM, outs[0], outs[1]).astype(bf16)
        for i in range(joined):
            here = slice(i * rows_part, (i + 1) * rows_part)
            o_ref[t * joined + i] = out[here, :]
            for h in range(2):
                ext_ref[h, t * joined + i] = ext_heads[h][here, :]
        return carry

    lax.fori_loop(0, blocks // joined, step, 0)


def attend(heads, visible, patches, first, frames_part, tile=1024, chunk=1024):
    blocks, _, rows, _ = heads.shape
    rows_part = frames_part * patches
    keys = blocks * rows
    joined = blocks
    while joined * rows_part > tile:
        joined //= 2
    return pl.pallas_call(
        functools.partial(
            attend_kernel, first, rows_part, patches, joined, chunk // rows
        ),
        out_shape=[
            pltpu.HBM((blocks, rows_part, LANES), bf16),
            pltpu.HBM((2, blocks, rows_part, LANES), bf16),
        ],
        in_specs=[pl.BlockSpec(memory_space=VMEM)] * 2,
        out_specs=[pl.BlockSpec(memory_space=VMEM)] * 2,
        compiler_params=pltpu.CompilerParams(vmem_limit_bytes=48 * MIB),
        cost_estimate=pl.CostEstimate(
            flops=8 * blocks * rows_part * keys * 2 * LANES,
            bytes_accessed=4 * MIB,
            transcendentals=0,
        ),
        name="attend",
    )(heads, visible)


def attend_back_kernel(parts, query_parts, part, patches, joined, together, carried, last, *refs):
    at = 0

    def take(count):
        nonlocal at
        found = refs[at : at + count]
        at += count
        return found

    (qkv_ref, do_ref) = take(2)
    ext_refs, o_refs = take(query_parts), take(query_parts)
    ctime_ref, stime_ref, cpatch_ref, spatch_ref = take(4)
    if carried:
        carry_ref, mix_ref = take(2)
    if last:
        (grads_ref,) = take(1)
    else:
        grads_ref, carry_out, mix_ref = take(3)
    (dq_turned,) = refs[at:]
    blocks, _, rows, _ = qkv_ref.shape
    rows_part = rows // parts
    frames, frames_part = rows // patches, rows_part // patches
    if carried:
        dq_turned[...] = carry_ref[...]
    else:
        dq_turned[...] = jnp.zeros_like(dq_turned)
        for b in range(blocks):
            at = 0
            for o_ref in o_refs:
                size = o_ref.shape[1]
                there = slice(at, at + size)
                at += size
                lane = lax.broadcasted_iota(jnp.int32, (size, LANES), 1)
                mixed = do_ref[b, there, :].astype(f32) * o_ref[b].astype(f32)
                for h in range(2):
                    mine = jnp.where((lane >= HDIM) == (h == 1), mixed, 0.0)
                    high, mid, low = split_three(-jnp.sum(mine, axis=1, keepdims=True))
                    ext = jnp.where(lane == 1, mid, jnp.where(lane == 2, low, 0.0))
                    mix_ref[h, b, there, :] = jnp.where(lane == 0, high, ext).astype(bf16)
    key_rows = slice(part * rows_part, (part + 1) * rows_part)
    key_lane = lax.broadcasted_iota(jnp.int32, (together * rows_part, LANES), 1)
    mix_keys = jnp.where(key_lane < 3, 1.0, 0.0).astype(bf16)

    def back(value, row, half):
        cosine = ctime_ref[pl.ds(row, 1), :] + cpatch_ref[half]
        sine = stime_ref[pl.ds(row, 1), :] + spatch_ref[half]
        return rotate_lanes(value, cosine, -sine).astype(bf16)

    first = rows if last else 0

    def step(t, carry):
        key_blocks = [t * together + i for i in range(together)]
        keys = jnp.concatenate([qkv_ref[b, 1, key_rows, :] for b in key_blocks], axis=0)
        keys = keys * score_scale
        vals = jnp.concatenate([qkv_ref[b, 2, key_rows, :] for b in key_blocks], axis=0)
        turned = keys.astype(f32).T.astype(bf16)
        extra = jnp.concatenate(
            [
                key_extra((b // 2) * frames + part * frames_part, rows_part, patches)
                for b in key_blocks
            ],
            axis=0,
        )
        key_tiles, val_tiles = [], []
        for h in range(2):
            mine = (key_lane >= HDIM) == (h == 1)
            none = jnp.zeros_like(keys)
            key_tiles.append(
                jnp.concatenate([jnp.where(mine, keys, none).astype(bf16), extra], axis=1)
            )
            val_tiles.append(jnp.concatenate([jnp.where(mine, vals, none), mix_keys], axis=1))
        dk = [jnp.zeros((together * rows_part, LANES), f32)] * 2
        dv = [jnp.zeros((together * rows_part, LANES), f32)] * 2
        for c in range(0, blocks, joined):
            some = range(c, c + joined)
            span = slice(c * rows, (c + joined) * rows)
            query = jnp.concatenate([qkv_ref[b, 0] for b in some], axis=0)
            grad = jnp.concatenate([do_ref[b] for b in some], axis=0)
            for h in range(2):
                ext = jnp.concatenate([ext_ref[h, b] for b in some for ext_ref in ext_refs], axis=0)
                mix = jnp.concatenate([mix_ref[h, b] for b in some], axis=0)
                probs = jnp.exp(dot(key_tiles[h], jnp.concatenate([query, ext], axis=1), NT))
                dv[h] = dv[h] + dot(probs.astype(bf16), grad)
                moved = dot(val_tiles[h], jnp.concatenate([grad, mix], axis=1), NT)
                grad_scores = (probs * moved).astype(bf16)
                dk[h] = dk[h] + dot(grad_scores, query)
                head = slice(HDIM * h, HDIM * (h + 1))
                dq_turned[head, span] += dot(turned[head, :], grad_scores)
        dk = jnp.where(key_lane < HDIM, dk[0], dk[1]) * score_scale
        dv = jnp.where(key_lane < HDIM, dv[0], dv[1]).astype(bf16)
        for i, b in enumerate(key_blocks):
            for f in range(frames_part):
                rows_here = slice(i * rows_part + f * patches, i * rows_part + (f + 1) * patches)
                row = b * frames + part * frames_part + f
                keys_here = slice(first + f * patches, first + (f + 1) * patches)
                grads_ref[b, keys_here, :] = back(dk[rows_here, :], row, b % 2)
            grads_ref[b, first + rows_part : first + 2 * rows_part, :] = dv[
                i * rows_part : (i + 1) * rows_part, :
            ]
        return carry

    lax.fori_loop(0, blocks // together, step, 0)

    if last:
        for b in range(blocks):
            for f in range(frames):
                there = slice(b * rows + f * patches, b * rows + (f + 1) * patches)
                turned_back = back(dq_turned[:, there].T, b * frames + f, b % 2)
                grads_ref[b, f * patches : (f + 1) * patches, :] = turned_back
    else:
        carry_out[...] = dq_turned[...]


def attend_back(heads, grads, exts, outs, rotary, carry, part, parts, patches, chunk=2048, together=2):
    last = part == parts - 1
    blocks, _, rows, _ = heads.shape
    rows_part = rows // parts
    total = blocks * rows
    operands = [heads, grads, *exts, *outs, *rotary, *(carry or ())]
    kept = 2 * rows_part + (rows if last else 0)
    out_shape = [pltpu.HBM((blocks, kept, LANES), bf16)]
    if not last:
        out_shape.append(jax.ShapeDtypeStruct((LANES, total), f32))
        out_shape.append(jax.ShapeDtypeStruct((2, blocks, rows, LANES), bf16))
    return pl.pallas_call(
        functools.partial(
            attend_back_kernel,
            parts,
            len(exts),
            part,
            patches,
            chunk // rows,
            together,
            carry is not None,
            last,
        ),
        out_shape=out_shape,
        in_specs=[pl.BlockSpec(memory_space=VMEM)] * len(operands),
        out_specs=[pl.BlockSpec(memory_space=VMEM)] * len(out_shape),
        scratch_shapes=[VMEM((LANES, total), f32)],
        compiler_params=pltpu.CompilerParams(vmem_limit_bytes=56 * MIB),
        cost_estimate=pl.CostEstimate(
            flops=20 * total * blocks * rows_part * 2 * LANES,
            bytes_accessed=8 * MIB,
            transcendentals=0,
        ),
        name="attend_back",
    )(*operands)


def act_grad_kernel(cot_ref, gate_ref, down_ref, grad_ref, out_ref):
    frames, patches, _ = cot_ref.shape

    @pl.when(pl.program_id(0) == 0)
    def _():
        for f in range(frames):
            grad = gate_ref[f : f + 1, :] * cot_ref[f].astype(f32)
            grad_ref[f * patches : (f + 1) * patches, :] = grad.astype(bf16)

    out_ref[...] = dot(grad_ref[...], down_ref[...], NT)


def act_grad(cotangent, gate_two, down_weight, cols=512):
    frames, patches, width = cotangent.shape
    rows, inner = frames * patches, down_weight.shape[0]
    return pl.pallas_call(
        act_grad_kernel,
        out_shape=[
            jax.ShapeDtypeStruct((rows, width), bf16),
            pltpu.HBM((rows, inner), f32),
        ],
        grid=(inner // cols,),
        in_specs=[
            whole(cotangent.shape),
            whole(gate_two.shape),
            pl.BlockSpec((cols, width), lambda c: (c, 0)),
        ],
        out_specs=[whole((rows, width)), pl.BlockSpec((rows, cols), lambda c: (0, c))],
        compiler_params=pltpu.CompilerParams(vmem_limit_bytes=40 * MIB),
        cost_estimate=pl.CostEstimate(
            flops=2 * rows * width * inner, bytes_accessed=18 * MIB, transcendentals=0
        ),
        name="act_grad",
    )(cotangent, gate_two, down_weight)


def feed_kernel(hid_ref, grad_ref, actgrad_ref, up_ref, bias_ref, down_ref,
                branch_ref, back_ref, biasgrad_ref, joined_ref,
                hid_turned, up_slots, down_slots, up_sems, down_sems):
    step, steps = pl.program_id(0), pl.num_programs(0)
    width, cols = up_ref.shape
    group, clips, _, share, _ = joined_ref.shape
    some_clips, quarters = down_slots.shape[2:4]
    up_parts = width // cols
    slot = step % 2

    def copies(at):
        across = pl.ds(pl.multiple_of((at % up_parts) * cols, cols), cols)
        up_copy = pltpu.make_async_copy(
            up_slots.at[at % 2], joined_ref.at[:, :, at // up_parts, :, across], up_sems.at[at % 2]
        )
        down_copy = pltpu.make_async_copy(
            down_slots.at[at % 2],
            joined_ref.at[:, pl.ds(at * some_clips, some_clips), quarters : 2 * quarters],
            down_sems.at[at % 2],
        )
        return up_copy, down_copy

    @pl.when(step == 0)
    def _():
        hid_turned[...] = hid_ref[...].T

    @pl.when(step >= 2)
    def _():
        for copy in copies(step - 2):
            copy.wait()

    pre = dot(hid_ref[...], up_ref[...]) + bias_ref[...]
    square = pre * pre
    bend = jnp.tanh(pre * (0.7978845608 + (0.7978845608 * 0.044715) * square))
    half = 0.5 * (1.0 + bend)
    act = (pre * half).astype(bf16)
    slope = half + (0.5 * pre) * (1.0 - bend * bend) * (
        0.7978845608 + (0.7978845608 * 3.0 * 0.044715) * square
    )
    pre_grad = (slope * actgrad_ref[...]).astype(bf16)
    biasgrad_ref[...] = jnp.sum(pre_grad.astype(f32), axis=0, keepdims=True)
    branch = dot(act, down_ref[...])
    back = dot(pre_grad, up_ref[...], NT)
    up_grad = dot(hid_turned[...], pre_grad).astype(bf16)
    up_grad = up_grad.reshape(clips, group, share, cols)
    for c in range(clips):
        up_slots[slot, :, c] = up_grad[c]
    down_grad = dot(act.T, grad_ref[...]).astype(bf16)
    down_grad = down_grad.reshape(some_clips, group, quarters, share, width)
    for c in range(some_clips):
        down_slots[slot, :, c] = down_grad[c]

    @pl.when(step == 0)
    def _():
        branch_ref[...] = branch
        back_ref[...] = back

    @pl.when(step > 0)
    def _():
        branch_ref[...] += branch
        back_ref[...] += back

    for copy in copies(step):
        copy.start()

    @pl.when(step == steps - 1)
    def _():
        for at in (steps - 2, steps - 1):
            for copy in copies(at):
                copy.wait()


def feed_forward(hidden, grad, grad_act, up_weight, up_bias, down_weight, group, clips, cols=1024):
    rows, width = hidden.shape
    inner = up_weight.shape[1]
    share, quarters = width // (group * clips), inner // width
    some_clips = cols * clips // inner
    return pl.pallas_call(
        feed_kernel,
        out_shape=[
            jax.ShapeDtypeStruct((rows, width), f32),
            jax.ShapeDtypeStruct((rows, width), f32),
            jax.ShapeDtypeStruct((1, inner), f32),
            jax.ShapeDtypeStruct((group, clips, 2 * quarters + 1, share, width), bf16),
        ],
        grid=(inner // cols,),
        in_specs=[
            whole((rows, width)),
            whole((rows, width)),
            pl.BlockSpec((rows, cols), lambda c: (0, c)),
            pl.BlockSpec((width, cols), lambda c: (0, c)),
            pl.BlockSpec((1, cols), lambda c: (0, c)),
            pl.BlockSpec((cols, width), lambda c: (c, 0)),
        ],
        out_specs=[
            whole((rows, width)),
            whole((rows, width)),
            pl.BlockSpec((1, cols), lambda c: (0, c)),
            pl.BlockSpec(memory_space=pl.ANY),
        ],
        scratch_shapes=[
            VMEM((width, rows), bf16),
            VMEM((2, group, clips, share, cols), bf16),
            VMEM((2, group, some_clips, quarters, share, width), bf16),
            pltpu.SemaphoreType.DMA((2,)),
            pltpu.SemaphoreType.DMA((2,)),
        ],
        compiler_params=pltpu.CompilerParams(vmem_limit_bytes=58 * MIB),
        cost_estimate=pl.CostEstimate(
            flops=10 * rows * width * inner, bytes_accessed=44 * MIB, transcendentals=0
        ),
        name="feed_forward",
    )(hidden, grad, grad_act, up_weight, up_bias, down_weight)


def proj_grad_kernel(attn_ref, grad_ref, _, joined_ref):
    group, clips, _, share, width = joined_ref.shape
    grad = dot(attn_ref[...].T, grad_ref[...]).astype(bf16).reshape(clips, group, share, width)
    for c in range(clips):
        joined_ref[:, c, 0] = grad[c]


def proj_weight_grad(attn_low, grad_proj, joined):
    rows, width = attn_low.shape
    group, clips, entries, share, _ = joined.shape
    return pl.pallas_call(
        proj_grad_kernel,
        out_shape=jax.ShapeDtypeStruct(joined.shape, joined.dtype),
        grid=(1,),
        in_specs=[
            whole((rows, width)),
            whole((rows, width)),
            pl.BlockSpec(memory_space=pl.ANY),
        ],
        out_specs=pl.BlockSpec((group, clips, 1, share, width), lambda c: (0, 0, entries - 1, 0, 0)),
        input_output_aliases={2: 0},
        compiler_params=pltpu.CompilerParams(vmem_limit_bytes=40 * MIB),
        cost_estimate=pl.CostEstimate(
            flops=2 * rows * width * width, bytes_accessed=4 * MIB, transcendentals=0
        ),
        name="proj_weight_grad",
    )(attn_low, grad_proj, joined)


def merge_kernel(*refs):
    parts = len(refs) - 10
    att_refs = refs[:parts]
    (weight_ref, bias_ref, tok_ref, gate_one_ref, shift_ref, scale_ref,
     low_ref, proj_ref, after_ref, hid_ref) = refs[parts:]
    frames, patches, width = tok_ref.shape
    pairs = att_refs[0].shape[0]
    at = 0
    for att_ref in att_refs:
        low = jnp.concatenate([att_ref[p] for p in range(pairs)], axis=1)
        rows_part = att_ref.shape[1]
        there = slice(at, at + rows_part)
        low_ref[there, :] = low
        proj = dot(low, weight_ref[...]) + bias_ref[...]
        proj_ref[there, :] = proj
        for j in range(rows_part // patches):
            f = at // patches + j
            here = slice(f * patches, (f + 1) * patches)
            row = slice(f, f + 1)
            after = tok_ref[f].astype(f32) + gate_one_ref[row, :] * proj[
                j * patches : (j + 1) * patches, :
            ]
            after_ref[here, :] = after
            centre = after - jnp.mean(after, axis=1, keepdims=True)
            inv = lax.rsqrt(jnp.mean(centre * centre, axis=1, keepdims=True) + norm_eps)
            hid = centre * inv * (1.0 + scale_ref[row, :]) + shift_ref[row, :]
            hid_ref[here, :] = hid.astype(bf16)
        at += rows_part


def merge_heads(attended, proj_weight, proj_bias, tokens, mods):
    frames, patches, width = tokens.shape
    rows = frames * patches
    operands = [*attended, proj_weight, proj_bias, tokens, *mods]
    return pl.pallas_call(
        merge_kernel,
        out_shape=[
            jax.ShapeDtypeStruct((rows, width), bf16),
            jax.ShapeDtypeStruct((rows, width), f32),
            jax.ShapeDtypeStruct((rows, width), f32),
            pltpu.HBM((rows, width), bf16),
        ],
        in_specs=[pl.BlockSpec(memory_space=VMEM)] * len(operands),
        out_specs=[pl.BlockSpec(memory_space=VMEM)] * 4,
        compiler_params=pltpu.CompilerParams(vmem_limit_bytes=48 * MIB),
        cost_estimate=pl.CostEstimate(
            flops=2 * rows * width * width, bytes_accessed=16 * MIB, transcendentals=0
        ),
        name="merge_heads",
    )(*operands)


def column_sum(value):
    return jnp.sum(value, axis=0, keepdims=True)


def unmerge_kernel(back_ref, after_ref, cot_ref, gate_one_ref, scale_ref, weight_ref,
                   grad_ref, gproj_ref, parts_ref):
    frames, patches, width = cot_ref.shape
    for f in range(frames):
        here = slice(f * patches, (f + 1) * patches)
        row = slice(f, f + 1)
        after = after_ref[here, :]
        centre = after - jnp.mean(after, axis=1, keepdims=True)
        inv = lax.rsqrt(jnp.mean(centre * centre, axis=1, keepdims=True) + norm_eps)
        normed = centre * inv
        scaled = back_ref[here, :] * (1.0 + scale_ref[row, :])
        mean_grad = jnp.mean(scaled, axis=1, keepdims=True)
        mean_mix = jnp.mean(scaled * normed, axis=1, keepdims=True)
        grad = cot_ref[f].astype(f32) + inv * (scaled - mean_grad - normed * mean_mix)
        grad_ref[here, :] = grad
        gproj_ref[here, :] = (gate_one_ref[row, :] * grad).astype(bf16)
    step = 2 * patches
    for i in range(frames * patches // step):
        here = slice(i * step, (i + 1) * step)
        part = dot(gproj_ref[here, :], weight_ref[...], NT).astype(bf16)
        for p in range(parts_ref.shape[0]):
            parts_ref[p, here, :] = part[:, p * LANES : (p + 1) * LANES]


def unmerge_heads(back, after, cotangent, gate_one, scale_two, proj_weight):
    frames, patches, width = cotangent.shape
    rows = frames * patches
    operands = [back, after, cotangent, gate_one, scale_two, proj_weight]
    return pl.pallas_call(
        unmerge_kernel,
        out_shape=[
            pltpu.HBM((rows, width), f32),
            jax.ShapeDtypeStruct((rows, width), bf16),
            pltpu.HBM((width // LANES, rows, LANES), bf16),
        ],
        in_specs=[pl.BlockSpec(memory_space=VMEM)] * len(operands),
        out_specs=[pl.BlockSpec(memory_space=VMEM)] * 3,
        compiler_params=pltpu.CompilerParams(vmem_limit_bytes=48 * MIB),
        cost_estimate=pl.CostEstimate(
            flops=2 * rows * width * width, bytes_accessed=12 * MIB, transcendentals=0
        ),
        name="unmerge_heads",
    )(*operands)


def side_kernel(branch_ref, back_ref, after_ref, proj_ref, cot_ref, gate_two_ref, bias_ref,
                grad_ref, gproj_ref, gbranch_ref, out_ref, sums_ref, biases_ref):
    f, frames = pl.program_id(0), pl.num_programs(0)
    cot = cot_ref[0].astype(f32)
    after = after_ref[...]
    branch = branch_ref[...] + bias_ref[...]
    out_ref[0] = (after + gate_two_ref[pl.ds(f, 1), :] * branch).astype(bf16)
    centre = after - jnp.mean(after, axis=1, keepdims=True)
    inv = lax.rsqrt(jnp.mean(centre * centre, axis=1, keepdims=True) + norm_eps)
    back = back_ref[...]
    for kind, term in enumerate(
        (grad_ref[...] * proj_ref[...], back, back * (centre * inv), cot * branch)
    ):
        sums_ref[pl.ds(kind * frames + f, 1), :] = column_sum(term)

    @pl.when(f == 0)
    def _():
        biases_ref[...] = jnp.zeros_like(biases_ref)

    biases_ref[0:1, :] += column_sum(gproj_ref[...].astype(f32))
    biases_ref[1:2, :] += column_sum(gbranch_ref[...].astype(f32))


def side_sums(branch, back, after, proj, cotangent, gate_two, down_bias, grad_after, grad_proj,
              grad_branch):
    frames, patches, width = cotangent.shape
    rows = pl.BlockSpec((patches, width), lambda f: (f, 0))
    slot = pl.BlockSpec((1, patches, width), lambda f: (f, 0, 0))
    return pl.pallas_call(
        side_kernel,
        out_shape=[
            jax.ShapeDtypeStruct((frames, patches, width), bf16),
            jax.ShapeDtypeStruct((4 * frames, width), f32),
            jax.ShapeDtypeStruct((2, width), f32),
        ],
        grid=(frames,),
        in_specs=[rows, rows, rows, rows, slot, whole(gate_two.shape), whole(down_bias.shape), rows,
                  rows, rows],
        out_specs=[slot, whole((4 * frames, width)), whole((2, width))],
        compiler_params=pltpu.CompilerParams(vmem_limit_bytes=48 * MIB),
        cost_estimate=pl.CostEstimate(flops=0, bytes_accessed=16 * MIB, transcendentals=0),
        name="side_sums",
    )(
        in_hbm(branch),
        in_hbm(back),
        in_hbm(after),
        in_hbm(proj),
        cotangent,
        gate_two,
        down_bias,
        grad_after,
        grad_proj,
        in_hbm(grad_branch),
    )


def heads_grad_kernel(hid_ref, first_ref, last_ref, out_ref, bias_ref, total):
    rows = hid_ref.shape[2]
    rows_part = first_ref.shape[1] // 2
    grad = jnp.concatenate(
        [
            last_ref[0, :rows, :],
            jnp.concatenate(
                [first_ref[0, :rows_part, :], last_ref[0, rows : rows + rows_part, :]], axis=0
            ),
            jnp.concatenate([first_ref[0, rows_part:, :], last_ref[0, rows + rows_part :, :]], axis=0),
        ],
        axis=1,
    )
    some = dot(hid_ref[0], grad)
    some_bias = column_sum(grad.astype(f32))

    @pl.when(pl.program_id(0) == 0)
    def _():
        total[...] = some
        bias_ref[...] = some_bias

    @pl.when(pl.program_id(0) > 0)
    def _():
        total[...] += some
        bias_ref[...] += some_bias

    @pl.when(pl.program_id(0) == pl.num_programs(0) - 1)
    def _():
        devices, triple, _ = out_ref.shape
        share = triple // 3
        for k in range(3):
            part = total[:, k * LANES : (k + 1) * LANES].astype(bf16)
            out_ref[:, k * share : (k + 1) * share, :] = part.reshape(devices, share, LANES)


def heads_grad(hidden_clip, first, last, devices):
    blocks, width, rows = hidden_clip.shape
    shape = (devices, 3 * width // devices, LANES)
    return pl.pallas_call(
        heads_grad_kernel,
        out_shape=[
            jax.ShapeDtypeStruct(shape, bf16),
            jax.ShapeDtypeStruct((1, 3 * LANES), f32),
        ],
        grid=(blocks,),
        in_specs=[
            pl.BlockSpec((1, width, rows), lambda b: (b, 0, 0)),
            pl.BlockSpec((1,) + first.shape[1:], lambda b: (b, 0, 0)),
            pl.BlockSpec((1,) + last.shape[1:], lambda b: (b, 0, 0)),
        ],
        out_specs=[whole(shape), whole((1, 3 * LANES))],
        scratch_shapes=[VMEM((width, 3 * LANES), f32)],
        compiler_params=pltpu.CompilerParams(vmem_limit_bytes=40 * MIB),
        cost_estimate=pl.CostEstimate(
            flops=6 * blocks * rows * width * LANES, bytes_accessed=12 * MIB, transcendentals=0
        ),
        name="heads_grad",
    )(in_hbm(hidden_clip), in_hbm(first), in_hbm(last))


def finish_kernel(first_ref, last_ref, wq_ref, wk_ref, wv_ref, tok_ref, scale_ref, after_ref,
                  partbias_ref, out_ref, send_ref, total):
    frames, patches, width = tok_ref.shape
    rows = frames * patches
    rows_part = first_ref.shape[1] // 2
    step = pl.program_id(0)
    query, keys, vals = [], [], []
    for p in range(first_ref.shape[0]):
        query.append(last_ref[p, :rows, :])
        keys.append(
            jnp.concatenate(
                [first_ref[p, :rows_part, :], last_ref[p, rows : rows + rows_part, :]], axis=0
            )
        )
        vals.append(
            jnp.concatenate([first_ref[p, rows_part:, :], last_ref[p, rows + rows_part :, :]], axis=0)
        )
    some = None
    for grads, weight_ref in ((query, wq_ref), (keys, wk_ref), (vals, wv_ref)):
        term = dot(jnp.concatenate(grads, axis=1), weight_ref[...], NT)
        some = term if some is None else some + term

    @pl.when(step == 0)
    def _():
        total[...] = some

    @pl.when(step > 0)
    def _():
        total[...] += some

    @pl.when(step == pl.num_programs(0) - 1)
    def _():
        shift_sums, scale_sums = [], []
        for f in range(frames):
            here = slice(f * patches, (f + 1) * patches)
            x = tok_ref[f].astype(f32)
            centre = x - jnp.mean(x, axis=1, keepdims=True)
            inv = lax.rsqrt(jnp.mean(centre * centre, axis=1, keepdims=True) + norm_eps)
            normed = centre * inv
            back = total[here, :]
            shift_sums.append(column_sum(back))
            scale_sums.append(column_sum(back * normed))
            scaled = back * (1.0 + scale_ref[f : f + 1, :])
            mean_grad = jnp.mean(scaled, axis=1, keepdims=True)
            mean_mix = jnp.mean(scaled * normed, axis=1, keepdims=True)
            grad = after_ref[here, :] + inv * (scaled - mean_grad - normed * mean_mix)
            out_ref[f] = grad.astype(bf16)
        sums = jnp.concatenate(shift_sums + scale_sums, axis=0)
        sums = jnp.concatenate(
            [sums[:, i : i + LANES] for i in range(0, width, LANES)], axis=0
        ).astype(bf16)
        bias = [partbias_ref[:, k * LANES : (k + 1) * LANES] for k in range(3)]
        high = [value.astype(bf16).astype(f32) for value in bias]
        low = [value - upper for value, upper in zip(bias, high)]
        bias = jnp.concatenate(high + low + [jnp.zeros((10, LANES), f32)], axis=0).astype(bf16)
        count = sums.shape[0]
        for d in range(send_ref.shape[0]):
            send_ref[d, :count, :] = sums
            send_ref[d, count:, :] = bias


def finish(first, last, qkv_weight, tokens, scale_one, grad_after, part_bias, copies, cols=256):
    frames, patches, width = tokens.shape
    rows = frames * patches
    steps, some = width // cols, cols // LANES

    send_shape = (copies, 2 * frames * (width // LANES) + 16, LANES)

    def column(third):
        return lambda c: (0, third * steps + c)

    return pl.pallas_call(
        finish_kernel,
        out_shape=[
            jax.ShapeDtypeStruct((frames, patches, width), bf16),
            pltpu.HBM(send_shape, bf16),
        ],
        grid=(steps,),
        in_specs=[
            pl.BlockSpec((some,) + first.shape[1:], lambda c: (c, 0, 0)),
            pl.BlockSpec((some,) + last.shape[1:], lambda c: (c, 0, 0)),
        ]
        + [pl.BlockSpec((width, cols), column(part)) for part in range(3)]
        + [whole(tokens.shape), whole(scale_one.shape), whole((rows, width))]
        + [whole(part_bias.shape)],
        out_specs=[whole((frames, patches, width)), whole(send_shape)],
        scratch_shapes=[VMEM((rows, width), f32)],
        compiler_params=pltpu.CompilerParams(vmem_limit_bytes=48 * MIB),
        cost_estimate=pl.CostEstimate(
            flops=6 * rows * width * width, bytes_accessed=16 * MIB, transcendentals=0
        ),
        name="finish",
    )(first, last, *[qkv_weight] * 3, tokens, scale_one, grad_after, part_bias)


def unpack_kernel(summed_ref, up_ref, down_ref, proj_ref):
    entries, share, width = summed_ref.shape
    quarters = entries // 2
    for i in range(quarters):
        up_ref[:, i * width : (i + 1) * width] = summed_ref[i].astype(f32)
        down_ref[i * share : (i + 1) * share, :] = summed_ref[quarters + i].astype(f32)
    proj_ref[...] = summed_ref[2 * quarters].astype(f32)


def unpack(summed):
    entries, share, width = summed.shape
    quarters = entries // 2
    return pl.pallas_call(
        unpack_kernel,
        out_shape=[
            jax.ShapeDtypeStruct((share, quarters * width), f32),
            jax.ShapeDtypeStruct((quarters * share, width), f32),
            jax.ShapeDtypeStruct((share, width), f32),
        ],
        in_specs=[pl.BlockSpec(memory_space=VMEM)],
        out_specs=[pl.BlockSpec(memory_space=VMEM)] * 3,
        name="unpack",
    )(summed)


def last_kernel(clips, frames, got_ref, member_ref, cols_ref, early_ref, earlysum_ref,
                rows_ref, bias_ref, ada_ref, adasum_ref):
    group = got_ref.shape[0]
    share, width = rows_ref.shape[0], rows_ref.shape[1] // 3
    tiles = width // LANES
    count = 2 * frames * tiles
    starts = [3 * share + c * (count + 16) for c in range(clips)]
    some = 4 * frames
    ada_ref[:, 2 * width :] = early_ref[...]
    adasum_ref[:, 2 * width :] = earlysum_ref[...]
    for i in range(tiles // 2):
        sums = jnp.concatenate(
            [
                got_ref[:, at + i * some : at + (i + 1) * some, :].reshape(group * some, LANES)
                for at in starts
            ],
            axis=0,
        )
        for j in range(2):
            for kind in range(2):
                level = dot(member_ref[2 * j + kind], sums).astype(bf16)
                at = kind * width + (2 * i + j) * LANES
                ada_ref[:, at : at + LANES] = dot(cols_ref[...], level)
                adasum_ref[:, at : at + LANES] = column_sum(level.astype(f32))
    for p in range(group):
        bias = None
        for at in starts:
            term = got_ref[p, at + count : at + count + 16, :].astype(f32)
            bias = term if bias is None else bias + term
        for third in range(3):
            at = third * width + p * LANES
            here = slice(third * share, (third + 1) * share)
            rows_ref[:, at : at + LANES] = got_ref[p, here, :].astype(f32)
            bias_ref[:, at : at + LANES] = bias[third : third + 1, :] + bias[third + 3 : third + 4, :]


def last_sums(got, member, columns, early, early_sum, clips, frames):
    share, width = early.shape[0], early.shape[1] // 4
    return pl.pallas_call(
        functools.partial(last_kernel, clips, frames),
        out_shape=[
            jax.ShapeDtypeStruct((share, 3 * width), f32),
            jax.ShapeDtypeStruct((1, 3 * width), f32),
            jax.ShapeDtypeStruct((share, 6 * width), f32),
            jax.ShapeDtypeStruct((1, 6 * width), f32),
        ],
        in_specs=[pl.BlockSpec(memory_space=VMEM)] * 5,
        out_specs=[pl.BlockSpec(memory_space=VMEM)] * 4,
        compiler_params=pltpu.CompilerParams(vmem_limit_bytes=48 * MIB),
        cost_estimate=pl.CostEstimate(flops=0, bytes_accessed=4 * MIB, transcendentals=0),
        name="last_sums",
    )(got, member, columns, early, early_sum)


def body(
    tokens,
    out_cotangent,
    level_embed,
    ada_weight,
    ada_bias,
    qkv_weight,
    qkv_bias,
    proj_weight,
    proj_bias,
    up_weight,
    up_bias,
    down_weight,
    down_bias,
    context_count,
    frame_level,
    slot_time,
):
    frames, patches, width = tokens.shape
    rows = frames * patches
    inner = up_weight.shape[1]
    frm_count, sp_count = lax.axis_size("frm"), lax.axis_size("sp")
    devices = frm_count * sp_count
    group = FRAMES // frames * sp_count
    clips = devices // group
    frm, sp = lax.axis_index("frm"), lax.axis_index("sp")
    me = frm * sp_count + sp
    clip = me // group
    clip_groups = [list(range(first, first + group)) for first in range(0, devices, group)]
    across_clips = [list(range(first, devices, group)) for first in range(group)]
    everyone = [list(range(devices))]
    halves = 2
    share = width // devices
    per_dest = inner // devices

    levels_here = level_embed.shape[0]
    embed_all = to_everyone(level_embed, devices).reshape(devices * levels_here, width)

    clip_times = lax.dynamic_slice_in_dim(slot_time, clip * FRAMES, FRAMES)
    clip_levels = lax.dynamic_index_in_dim(frame_level, clip, 0, keepdims=False)
    context = lax.dynamic_index_in_dim(context_count, clip, 0, keepdims=False)
    seen = (clip_times[None, :] <= clip_times[:, None]) | (clip_times[None, :] < context)
    visible = jnp.pad(
        jnp.where(seen, 0.0, masked_out).astype(f32), ((0, 0), (0, LANES - FRAMES))
    )

    def by_blocks(table):
        table = table.reshape(FRAMES // frames, 1, frames, LANES)
        return jnp.broadcast_to(table, (FRAMES // frames, sp_count, frames, LANES)).reshape(
            group * frames, LANES
        )

    visible = by_blocks(visible)
    freq, sign, time_lane, row_lane = rotary_lanes()
    angle_time = clip_times.astype(f32)[:, None] * freq[None, :]
    ctime = by_blocks(jnp.where(time_lane[None, :], jnp.cos(angle_time), 0.0))
    stime = by_blocks(jnp.where(time_lane[None, :], jnp.sin(angle_time) * sign[None, :], 0.0))
    patch_ids = jnp.arange(sp_count * patches, dtype=jnp.int32).reshape(sp_count, patches)
    place = jnp.where(
        row_lane[None, None, :], (patch_ids // GRID)[..., None], (patch_ids % GRID)[..., None]
    )
    angle_patch = place.astype(f32) * freq[None, None, :]
    cpatch = jnp.where(time_lane, 0.0, jnp.cos(angle_patch))
    spatch = jnp.where(time_lane, 0.0, jnp.sin(angle_patch) * sign)
    rotary = [ctime, stime, cpatch, spatch]

    def my_table(time_part, patch_part):
        mine = lax.dynamic_slice_in_dim(time_part, me % group * frames, frames)
        half = lax.dynamic_index_in_dim(patch_part, sp, 0, keepdims=False)
        return (mine[:, None, :] + half[None]).reshape(rows, LANES)

    cosine, sine = my_table(ctime, cpatch), my_table(stime, spatch)

    my_times = lax.dynamic_slice_in_dim(slot_time, frm * frames, frames)
    my_levels = jnp.take(clip_levels, my_times)
    embed_act = jax.nn.silu(embed_all.astype(f32)).astype(bf16)
    level_ids = jnp.arange(devices * levels_here, dtype=jnp.int32)
    pick = (my_levels[:, None] == level_ids[None, :]).astype(bf16)
    my_embed = dot(pick, embed_act).astype(bf16)

    def modulation(embeds, first, count):
        here = slice(first * width, (first + count) * width)
        rows_mod = dot(embeds, ada_weight[:, here]) + ada_bias[here].astype(f32)
        rows_mod = lax.reduce_precision(rows_mod, 8, 7)
        return [rows_mod[:, i * width : (i + 1) * width] for i in range(count)]

    shift_one, scale_one = modulation(my_embed, 0, 2)

    hidden_turned, head_parts = project(
        tokens, shift_one, scale_one, qkv_weight, qkv_bias.astype(f32)[None, :], cosine, sine
    )

    my_embed, head_parts = lax.optimization_barrier((my_embed, head_parts))
    gate_one, shift_two, scale_two, gate_two = modulation(my_embed, 2, 4)
    heads = exchange(head_parts, clip_groups)
    grad_branch, grad_act = act_grad(out_cotangent, gate_two, down_weight)
    slot_ids = (jnp.arange(devices * frames, dtype=jnp.int32) // (sp_count * frames)) * frames
    slot_ids = slot_ids + jnp.arange(devices * frames, dtype=jnp.int32) % frames
    slot_levels = frame_level[slot_ids // FRAMES, slot_time[slot_ids]]
    member_of = (level_ids[:, None] == slot_levels[None, :]).astype(bf16)
    my_columns = lax.dynamic_slice_in_dim(embed_act, me * share, share, axis=1)
    which = jnp.arange(4, dtype=jnp.int32)
    member_last = jnp.where(
        (which[:, None] == which[None, :])[:, None, None, :, None],
        member_of.reshape(1, -1, devices, 1, frames),
        jnp.zeros((), bf16),
    ).reshape(4, -1, devices * 4 * frames)
    columns_turned = my_columns.T
    heads, grad_branch, grad_act, member_of, my_columns, member_last, columns_turned = (
        lax.optimization_barrier(
            (heads, grad_branch, grad_act, member_of, my_columns, member_last, columns_turned)
        )
    )
    outs, exts, attended = [], [], []
    for first, frames_part in ((0, frames - frames // 4), (frames - frames // 4, frames // 4)):
        out, ext = attend(heads, visible, patches, first, frames_part)
        visible, out = lax.optimization_barrier((visible, out))
        sent = out
        if attended:
            sent, attended[0] = lax.optimization_barrier((sent, attended[0]))
        outs.append(out)
        exts.append(ext)
        attended.append(exchange(sent, clip_groups))

    hidden_turned, _ = lax.optimization_barrier((hidden_turned, heads))
    hidden_clip = lax.all_gather(hidden_turned, AXES, axis_index_groups=clip_groups)

    attn_low, attn_proj, after_attn, hidden_two = merge_heads(
        attended,
        proj_weight,
        proj_bias.astype(f32)[None, :],
        tokens,
        (gate_one, shift_two, scale_two),
    )
    branch, grad_hidden_two, up_b_grad, joined = feed_forward(
        hidden_two,
        grad_branch,
        grad_act,
        up_weight,
        up_bias.astype(f32)[None, :],
        down_weight,
        group,
        clips,
    )
    grad_after, grad_proj, grad_parts = unmerge_heads(
        grad_hidden_two, after_attn, out_cotangent, gate_one, scale_two, proj_weight
    )
    grads = exchange(grad_parts, clip_groups)
    block_out, early_sums, early_biases = side_sums(
        branch,
        grad_hidden_two,
        after_attn,
        attn_proj,
        out_cotangent,
        gate_two,
        down_bias.astype(f32)[None, :],
        grad_after,
        grad_proj,
        grad_branch,
    )

    joined = proj_weight_grad(attn_low, grad_proj, joined)
    joined, hidden_clip = lax.optimization_barrier((joined, hidden_clip))
    summed = lax.psum_scatter(
        joined, AXES, scatter_dimension=0, axis_index_groups=clip_groups, tiled=True
    )[0]

    def slot_parts(slot_sums, biases):
        kinds = slot_sums.shape[0] // frames
        sums = slot_sums.reshape(kinds, frames, width).transpose(1, 0, 2).reshape(frames, -1)
        sums = jnp.broadcast_to(sums.astype(bf16)[None], (devices, frames, kinds * width))
        high = biases.astype(bf16)
        low = (biases - high.astype(f32)).astype(bf16)
        both = jnp.concatenate([high, low], axis=1).reshape(devices, frames, -1)
        lanes = -(-both.shape[2] // LANES) * LANES
        both = jnp.pad(both, ((0, 0), (0, 0), (0, lanes - both.shape[2])))
        return jnp.concatenate([sums, both], axis=2)

    def bias_share(got, count, size):
        extra = jnp.sum(got[:, :, count:].astype(f32), axis=0)
        extra = extra[:, : 2 * size // frames].reshape(-1)
        return extra[:size] + extra[size:]

    def level_out(got, count):
        slots = got[:, :, :count].reshape(devices * frames, count)
        level_grad = dot(member_of, slots).astype(bf16)
        return dot(my_columns, level_grad, TN), jnp.sum(level_grad.astype(f32), axis=0)

    early_parts = slot_parts(
        early_sums,
        jnp.concatenate(
            [
                up_b_grad.reshape(devices, per_dest),
                early_biases[0].reshape(devices, share),
                early_biases[1].reshape(devices, share),
            ],
            axis=1,
        ),
    )
    early_parts, _ = lax.optimization_barrier((early_parts, grads))
    early_got = exchange(early_parts, everyone)

    first_grads, carry, mixes = attend_back(
        heads, grads, exts, outs, rotary, None, 0, halves, patches
    )
    carry, early_got = lax.optimization_barrier((carry, early_got))
    own_first = exchange(first_grads, clip_groups)
    (last_grads,) = attend_back(
        heads, grads, exts, outs, rotary, (carry, mixes), 1, halves, patches
    )
    last_parts, own_first = lax.optimization_barrier((last_grads, own_first))
    own_last = exchange(last_parts, clip_groups)

    early_w, early_b = level_out(early_got, 4 * width)
    early_bias_out = bias_share(early_got, 4 * width, per_dest + 2 * share)

    qkv_part, qkv_b_part = heads_grad(hidden_clip, first_grads, last_grads, devices)
    qkv_part = qkv_part.reshape(clips, group, 3 * share, LANES)
    qkv_sum = lax.dynamic_index_in_dim(qkv_part, clip, 0, keepdims=False).astype(f32)
    for j in range(1, clips):
        some = lax.dynamic_index_in_dim(qkv_part, clip ^ j, 0, keepdims=False)
        pairs = [(source, source ^ (j * group)) for source in range(devices)]
        qkv_sum = qkv_sum + lax.ppermute(some, AXES, pairs).astype(f32)
    qkv_sum, own_last, summed = lax.optimization_barrier(
        (qkv_sum.astype(bf16), own_last, summed)
    )

    summed = lax.psum_scatter(
        summed, AXES, scatter_dimension=0, axis_index_groups=across_clips, tiled=True
    )[0]
    up_w_out, down_w_out, proj_w_out = unpack(summed)

    tokens_grad, last_send = finish(
        own_first, own_last, qkv_weight, tokens, scale_one, grad_after, qkv_b_part, clips
    )
    clip_got = exchange(last_send, across_clips).reshape(1, -1, LANES)
    clip_got = jnp.broadcast_to(clip_got, (group,) + clip_got.shape[1:])
    last_got = exchange(jnp.concatenate([qkv_sum, clip_got], axis=1), clip_groups)
    last_got, early_w, early_b, early_bias_out = lax.optimization_barrier(
        (last_got, early_w, early_b, early_bias_out)
    )
    up_b_out = early_bias_out[:per_dest]
    proj_b_out = early_bias_out[per_dest : per_dest + share]
    down_b_out = early_bias_out[per_dest + share :]
    qkv_w_out, qkv_b_all, ada_w_out, ada_b_all = last_sums(
        last_got, member_last, columns_turned, early_w, early_b[None, :], clips, frames
    )
    qkv_b_out = lax.dynamic_slice_in_dim(qkv_b_all[0], me * 3 * share, 3 * share)
    ada_b_all = ada_b_all[0]
    ada_share = ada_b_all.shape[0] // devices
    ada_b_out = lax.dynamic_slice_in_dim(ada_b_all, me * ada_share, ada_share)
    return (
        block_out,
        tokens_grad,
        ada_w_out,
        ada_b_out,
        qkv_w_out,
        qkv_b_out,
        proj_w_out,
        proj_b_out,
        up_w_out,
        up_b_out,
        down_w_out,
        down_b_out,
    )


def solution(mesh):
    tokens_spec = P("frm", "sp", None)
    rows_spec = P(AXES, None)
    vector_spec = P(AXES)
    return jax.shard_map(
        body,
        mesh=mesh,
        in_specs=(tokens_spec, tokens_spec, rows_spec) + (P(),) * 13,
        out_specs=(tokens_spec, tokens_spec) + (rows_spec, vector_spec) * 5,
        check_vma=False,
    )
```
